128 devices in a mesh: batch: 32 (over y, x, core), chan: 4 (over z).
Axes of the slice: x: 4, y: 4, z: 4, core: 2. Of those that a mesh axis runs over, the one named last changes fastest.
Arguments:
- features: bfloat16 [4, 10436608], P('chan', 'batch'), may hold values from -6 to 6
- lengths: int32 [256], P('batch'), may hold values from 1 to 4, as said below
- labels: int32 [256, 4], P('batch'), may hold values from 0 to 399
- direct: float32 [4, 79872], P('chan'), may hold values from -0.21875 to 0.21875
- squeeze: float32 [4, 39936], P('chan'), may hold values from -0.21875 to 0.21875
- spatial: float32 [4, 497664], P('chan'), may hold values from -0.078125 to 0.078125
- shrink: float32 [4, 9984], P('chan'), may hold values from -0.21875 to 0.21875
- volume: float32 [4, 41472], P('chan'), may hold values from -0.15625 to 0.15625
- pooled: float32 [4, 26624], P('chan'), may hold values from -0.21875 to 0.21875
- readout: float32 [4, 102400], P('chan'), may hold values from -0.9 to 0.9
- affine: float32 [2, 1264], P(None, 'chan'), may hold values from 0.5 to 1.5
- first_direct: float32 [4, 79872], P('chan'), may hold values from -0.013671875 to 0.013671875
- first_squeeze: float32 [4, 39936], P('chan'), may hold values from -0.013671875 to 0.013671875
- first_spatial: float32 [4, 497664], P('chan'), may hold values from -0.0546875 to 0.0546875
- first_shrink: float32 [4, 9984], P('chan'), may hold values from -0.013671875 to 0.013671875
- first_volume: float32 [4, 41472], P('chan'), may hold values from -0.0546875 to 0.0546875
- first_pooled: float32 [4, 26624], P('chan'), may hold values from -0.0546875 to 0.0546875
- first_readout: float32 [4, 102400], P('chan'), may hold values from -0.0546875 to 0.0546875
- first_affine: float32 [2, 1264], P(None, 'chan'), may hold values from -0.0546875 to 0.0546875
- second_direct: float32 [4, 79872], P('chan'), may hold values from 1.9929846e-06 to 7.971938e-06
- second_squeeze: float32 [4, 39936], P('chan'), may hold values from 1.9929846e-06 to 7.971938e-06
- second_spatial: float32 [4, 497664], P('chan'), may hold values from 7.9719386e-05 to 0.00031887754
- second_shrink: float32 [4, 9984], P('chan'), may hold values from 1.9929846e-06 to 7.971938e-06
- second_volume: float32 [4, 41472], P('chan'), may hold values from 7.9719386e-05 to 0.00031887754
- second_pooled: float32 [4, 26624], P('chan'), may hold values from 7.9719386e-05 to 0.00031887754
- second_readout: float32 [4, 102400], P('chan'), may hold values from 7.9719386e-05 to 0.00031887754
- second_affine: float32 [2, 1264], P(None, 'chan'), may hold values from 7.9719386e-05 to 0.00031887754
- running: float32 [2, 1264], P(None, 'chan'), may hold values from 0.002 to 0.02
Outputs:
- moment_direct: float32 [4, 79872], P('chan')
- moment_squeeze: float32 [4, 39936], P('chan')
- moment_spatial: float32 [4, 497664], P('chan')
- moment_shrink: float32 [4, 9984], P('chan')
- moment_volume: float32 [4, 41472], P('chan')
- moment_pooled: float32 [4, 26624], P('chan')
- moment_readout: float32 [4, 102400], P('chan')
- moment_affine: float32 [2, 1264], P(None, 'chan')
- square_direct: float32 [4, 79872], P('chan')
- square_squeeze: float32 [4, 39936], P('chan')
- square_spatial: float32 [4, 497664], P('chan')
- square_shrink: float32 [4, 9984], P('chan')
- square_volume: float32 [4, 41472], P('chan')
- square_pooled: float32 [4, 26624], P('chan')
- square_readout: float32 [4, 102400], P('chan')
- square_affine: float32 [2, 1264], P(None, 'chan')
- master_direct: float32 [4, 79872], P('chan')
- master_squeeze: float32 [4, 39936], P('chan')
- master_spatial: float32 [4, 497664], P('chan')
- master_shrink: float32 [4, 9984], P('chan')
- master_volume: float32 [4, 41472], P('chan')
- master_pooled: float32 [4, 26624], P('chan')
- master_readout: float32 [4, 102400], P('chan')
- master_affine: float32 [2, 1264], P(None, 'chan')
- running_next: float32 [2, 1264], P(None, 'chan')
- loss_sum: float32 [], replicated
- counted: float32 [], replicated
- copies: bfloat16 [4, 797952], P('chan')
The draws below stay inside these ranges and needn't reach their ends.
Inputs may be any that keep to these rules, and one draw needn't show every extreme that they name: Clip c has lengths[c] valid time steps, the first ones of its 4; some clip has 4.
All inputs are finite; a program needn't handle non-finite values.
Results may differ from the reference program's by a relative error of at most 0.0039.
Values may be sent and summed in bfloat16 or wider, within the bound.
A program may use at most 320 MiB of HBM per device.

```python
import math
from functools import partial
import jax
import jax.numpy as jnp
from jax import lax

CIN = 832
B0 = 384
R1 = 192
O1 = 384
R2 = 48
O2 = 128
B3 = 128
CLASSES = 400
SIDE = 7
TMAX = 4
STEP = 5
CLIPS = 256
FEAT = 1024
BNW = 1264
N_CHAN = 4


def draw_lengths(key, part):
    key = jax.random.fold_in(key, 11)
    position = jnp.arange(CLIPS)
    rising = 1 + position * TMAX // CLIPS
    jitter = jax.random.randint(key, (CLIPS,), 0, 2)
    return jnp.minimum(rising + jitter, TMAX).astype(jnp.int32)


def set_ends(entries, own_key, least, top_value):
    longest = entries.shape.index(max(entries.shape))
    spots = []
    for shift in (0, 1):
        where = [jax.random.randint(jax.random.fold_in(own_key, axis), (), 0, length) for axis, length in enumerate(entries.shape)]
        where[longest] = (where[longest] + shift) % entries.shape[longest]
        spots.append(tuple(where))
    return entries.at[spots[0]].set(least).at[spots[1]].set(top_value)


def steps_of(key, shape, shards, least, high):
    def one(dim, parts):
        draws = jax.random.uniform(jax.random.fold_in(jax.random.fold_in(key, 6), dim), (parts,), jnp.float32, least / len(shards), high / len(shards))
        return jnp.repeat(jnp.exp(draws), shape[dim] // parts).reshape((-1,) + (1,) * (len(shape) - dim - 1))

    gain = one(*shards[0])
    for cut in shards[1:]:
        gain = gain * one(*cut)
    return gain


def scatter_about(stream_key, dims, deviation, bound, cuts=(), kind=jnp.bfloat16):
    loudness = steps_of(stream_key, dims, cuts, -0.22, 0.18) if cuts else 1.0
    result = jax.random.normal(stream_key, dims, jnp.float32) * deviation * loudness
    return jnp.minimum(jnp.maximum(result, -bound), bound).astype(kind)


def setup_inputs(seed: int = 0) -> dict:
    splits = jax.random.split(jax.random.key(seed), 29)
    features = scatter_about(splits[0], (N_CHAN, CLIPS * TMAX * SIDE * SIDE * CIN // N_CHAN), 1.0, 6.0, ((0, 4), (1, 32)))
    lengths = draw_lengths(jax.random.fold_in(splits[28], 71), 0)
    labels = set_ends(jax.random.randint(splits[2], (CLIPS, TMAX), 0, CLASSES), jax.random.fold_in(splits[2], 1), 0, CLASSES - 1).astype(jnp.int32)
    direct = scatter_about(splits[3], (N_CHAN, CIN * B0 // N_CHAN), CIN ** -0.5, 0.21875, ((0, 4),), jnp.float32)
    squeeze = scatter_about(splits[4], (N_CHAN, CIN * R1 // N_CHAN), CIN ** -0.5, 0.21875, ((0, 4),), jnp.float32)
    spatial = scatter_about(splits[5], (N_CHAN, 27 * R1 * O1 // N_CHAN), (27 * R1) ** -0.5, 0.078125, ((0, 4),), jnp.float32)
    shrink = scatter_about(splits[6], (N_CHAN, CIN * R2 // N_CHAN), CIN ** -0.5, 0.21875, ((0, 4),), jnp.float32)
    volume = scatter_about(splits[7], (N_CHAN, 27 * R2 * O2 // N_CHAN), (27 * R2) ** -0.5, 0.15625, ((0, 4),), jnp.float32)
    pooled = scatter_about(splits[8], (N_CHAN, CIN * B3 // N_CHAN), CIN ** -0.5, 0.21875, ((0, 4),), jnp.float32)
    readout = scatter_about(splits[9], (N_CHAN, FEAT * CLASSES // N_CHAN), 0.15, 0.9, ((0, 4),), jnp.float32)
    affine = jnp.clip(0.5 + 1.0 * jax.random.uniform(splits[10], (2, BNW), jnp.float32) ** steps_of(splits[10], (2, BNW), ((1, 4),), -0.2, 0.2), 0.5, 1.5)
    first_direct = scatter_about(splits[11], (N_CHAN, CIN * B0 // N_CHAN), (0.5 / (CLIPS * TMAX * SIDE * SIDE) ** 0.5), 0.013671875, ((0, 4),), jnp.float32)
    first_squeeze = scatter_about(splits[12], (N_CHAN, CIN * R1 // N_CHAN), (0.5 / (CLIPS * TMAX * SIDE * SIDE) ** 0.5), 0.013671875, ((0, 4),), jnp.float32)
    first_spatial = scatter_about(splits[13], (N_CHAN, 27 * R1 * O1 // N_CHAN), (2.0 / (CLIPS * TMAX * SIDE * SIDE) ** 0.5), 0.0546875, ((0, 4),), jnp.float32)
    first_shrink = scatter_about(splits[14], (N_CHAN, CIN * R2 // N_CHAN), (0.5 / (CLIPS * TMAX * SIDE * SIDE) ** 0.5), 0.013671875, ((0, 4),), jnp.float32)
    first_volume = scatter_about(splits[15], (N_CHAN, 27 * R2 * O2 // N_CHAN), (2.0 / (CLIPS * TMAX * SIDE * SIDE) ** 0.5), 0.0546875, ((0, 4),), jnp.float32)
    first_pooled = scatter_about(splits[16], (N_CHAN, CIN * B3 // N_CHAN), (2.0 / (CLIPS * TMAX * SIDE * SIDE) ** 0.5), 0.0546875, ((0, 4),), jnp.float32)
    first_readout = scatter_about(splits[17], (N_CHAN, FEAT * CLASSES // N_CHAN), (2.0 / (CLIPS * TMAX * SIDE * SIDE) ** 0.5), 0.0546875, ((0, 4),), jnp.float32)
    first_affine = scatter_about(splits[18], (2, BNW), (2.0 / (CLIPS * TMAX * SIDE * SIDE) ** 0.5), 0.0546875, ((1, 4),), jnp.float32)
    second_direct = jnp.clip(jnp.exp(math.log(7.97193843027344e-06) - 1.3862944 * jax.random.uniform(splits[19], (N_CHAN, CIN * B0 // N_CHAN), jnp.float32) ** steps_of(splits[19], (N_CHAN, CIN * B0 // N_CHAN), ((0, 4),), -0.2, 0.2)), 1.99298460756836e-06, 7.97193843027344e-06)
    second_squeeze = jnp.clip(jnp.exp(math.log(7.97193843027344e-06) - 1.3862944 * jax.random.uniform(splits[20], (N_CHAN, CIN * R1 // N_CHAN), jnp.float32) ** steps_of(splits[20], (N_CHAN, CIN * R1 // N_CHAN), ((0, 4),), -0.2, 0.2)), 1.99298460756836e-06, 7.97193843027344e-06)
    second_spatial = jnp.clip(jnp.exp(math.log(0.00031887754) - 1.3862944 * jax.random.uniform(splits[21], (N_CHAN, 27 * R1 * O1 // N_CHAN), jnp.float32) ** steps_of(splits[21], (N_CHAN, 27 * R1 * O1 // N_CHAN), ((0, 4),), -0.2, 0.2)), 7.97193861217238e-05, 0.00031887754)
    second_shrink = jnp.clip(jnp.exp(math.log(7.97193843027344e-06) - 1.3862944 * jax.random.uniform(splits[22], (N_CHAN, CIN * R2 // N_CHAN), jnp.float32) ** steps_of(splits[22], (N_CHAN, CIN * R2 // N_CHAN), ((0, 4),), -0.2, 0.2)), 1.99298460756836e-06, 7.97193843027344e-06)
    second_volume = jnp.clip(jnp.exp(math.log(0.00031887754) - 1.3862944 * jax.random.uniform(splits[23], (N_CHAN, 27 * R2 * O2 // N_CHAN), jnp.float32) ** steps_of(splits[23], (N_CHAN, 27 * R2 * O2 // N_CHAN), ((0, 4),), -0.2, 0.2)), 7.97193861217238e-05, 0.00031887754)
    second_pooled = jnp.clip(jnp.exp(math.log(0.00031887754) - 1.3862944 * jax.random.uniform(splits[24], (N_CHAN, CIN * B3 // N_CHAN), jnp.float32) ** steps_of(splits[24], (N_CHAN, CIN * B3 // N_CHAN), ((0, 4),), -0.2, 0.2)), 7.97193861217238e-05, 0.00031887754)
    second_readout = jnp.clip(jnp.exp(math.log(0.00031887754) - 1.3862944 * jax.random.uniform(splits[25], (N_CHAN, FEAT * CLASSES // N_CHAN), jnp.float32) ** steps_of(splits[25], (N_CHAN, FEAT * CLASSES // N_CHAN), ((0, 4),), -0.2, 0.2)), 7.97193861217238e-05, 0.00031887754)
    second_affine = jnp.clip(jnp.exp(math.log(0.00031887754) - 1.3862944 * jax.random.uniform(splits[26], (2, BNW), jnp.float32) ** steps_of(splits[26], (2, BNW), ((1, 4),), -0.2, 0.2)), 7.97193861217238e-05, 0.00031887754)
    running = jnp.clip(jnp.exp(math.log(0.02) - 2.30258502 * jax.random.uniform(splits[27], (2, BNW), jnp.float32) ** steps_of(splits[27], (2, BNW), ((1, 4),), -0.2, 0.2)), 0.002, 0.02)
    return dict(features=features, lengths=lengths, labels=labels, direct=direct, squeeze=squeeze, spatial=spatial, shrink=shrink, volume=volume, pooled=pooled, readout=readout, affine=affine, first_direct=first_direct, first_squeeze=first_squeeze, first_spatial=first_spatial, first_shrink=first_shrink, first_volume=first_volume, first_pooled=first_pooled, first_readout=first_readout, first_affine=first_affine, second_direct=second_direct, second_squeeze=second_squeeze, second_spatial=second_spatial, second_shrink=second_shrink, second_volume=second_volume, second_pooled=second_pooled, second_readout=second_readout, second_affine=second_affine, running=running)


EPS = 1e-05
BETA_ONE = 0.5
BETA_TWO = 0.5
DECAY = 0.01
MOMENTUM = 0.99
highest = lax.Precision.HIGHEST

@jax.custom_vjp
def low(v):
    return lax.optimization_barrier(v.astype(jnp.bfloat16)).astype(jnp.float32)

@jax.custom_vjp
def low_back(v):
    return v

def low_keep(v):
    return (low(v), None)

def low_pass(kept, grad):
    return (grad,)

def back_keep(v):
    return (v, None)

def back_low(kept, grad):
    return (low(grad),)
low.defvjp(low_keep, low_pass)
low_back.defvjp(back_keep, back_low)

def shifted_views(field):
    padded = jnp.pad(field, ((0, 0), (1, 1), (1, 1), (1, 1), (0, 0)))
    frames, height, across = (field.shape[1], field.shape[2], field.shape[3])
    return [padded[:, shift_t:shift_t + frames, shift_h:shift_h + height, shift_w:shift_w + across, :] for shift_t in range(3) for shift_h in range(3) for shift_w in range(3)]

def patches(field):
    return jnp.concatenate(shifted_views(field), axis=-1)

def box_sum(field):
    return sum(shifted_views(field))

def norm_widths():
    return [B0, R1, R2, B3, O1, O2]

def step_rates():
    return [1.5 / math.sqrt(CIN), 1.5 / math.sqrt(CIN), 1.5 / math.sqrt(27 * R1), 1.5 / math.sqrt(CIN), 1.5 / math.sqrt(27 * R2), 1.5 / math.sqrt(CIN), 0.2, 0.3]

def weight_rows():
    return [CIN, CIN, 27 * R1, CIN, 27 * R2, CIN]

def unflat(blocked, rows):
    return jnp.moveaxis(blocked.reshape(N_CHAN, rows, -1), 0, 1).reshape(rows, -1)

def reflat(matrix):
    return jnp.moveaxis(matrix.reshape(matrix.shape[0], N_CHAN, -1), 1, 0).reshape(N_CHAN, -1)

def unpack(packed):
    shaped = packed.reshape(packed.shape[0], N_CHAN, BNW // N_CHAN)
    pieces = []
    offset = 0
    for channels in norm_widths():
        portion = channels // N_CHAN
        pieces.append(shaped[:, :, offset:offset + portion].reshape(packed.shape[0], channels))
        offset = offset + portion
    return pieces

def pack(pieces):
    shaped = [piece.reshape(piece.shape[0], N_CHAN, piece.shape[1] // N_CHAN) for piece in pieces]
    joined = jnp.concatenate(shaped, axis=2)
    return joined.reshape(joined.shape[0], BNW)

def normalize(conv_out, voxel_mask, voxels, params):
    average = lax.optimization_barrier(jnp.sum(conv_out * voxel_mask, axis=(0, 1, 2, 3))) / voxels
    variance = lax.optimization_barrier(jnp.sum(conv_out * conv_out * voxel_mask, axis=(0, 1, 2, 3))) / voxels - average * average
    normed = (conv_out - average) * lax.rsqrt(variance + EPS)
    active = voxel_mask * jax.nn.silu(params[0] * normed + params[1])
    return (active, average, variance)

def project(inputs, weight):
    return low_back(jnp.dot(inputs, low(weight), precision=highest))

def forward(direct, squeeze, spatial, shrink, volume, pooled, readout, affine, features, voxel_mask, step_mask, onehot, voxels, counted):
    norm_params = unpack(affine)
    collected = {}

    def branch(inputs, weight, member):
        active, average, variance = normalize(project(inputs, weight), voxel_mask, voxels, norm_params[member])
        collected[member] = (average, variance)
        return active
    out_direct = branch(features, direct, 0)
    out_squeeze = branch(features, squeeze, 1)
    out_shrink = branch(features, shrink, 2)
    window = box_sum(features * voxel_mask) / jnp.maximum(box_sum(voxel_mask), 1.0)
    out_pooled = branch(low(window), pooled, 3)
    out_spatial = branch(patches(low(out_squeeze)), spatial, 4)
    out_volume = branch(patches(low(out_shrink)), volume, 5)
    clips_n, frames = (features.shape[0], features.shape[1])
    pieces = [lax.optimization_barrier(jnp.mean(part_out, axis=(2, 3))).reshape(clips_n, frames, N_CHAN, -1) for part_out in [out_direct, out_spatial, out_volume, out_pooled]]
    feature = low(jnp.concatenate(pieces, axis=-1).reshape(clips_n, frames, FEAT))
    logits = project(feature, readout)
    logprob = jax.nn.log_softmax(logits, axis=-1)
    loss_total = -jnp.sum(step_mask[:, :, None] * onehot * logprob)
    return (loss_total / counted, (loss_total, [collected[member] for member in range(6)]))

def adamw(weight, moment_one, moment_two, gradient, step_rate):
    first_new = BETA_ONE * moment_one + (1.0 - BETA_ONE) * gradient
    second_new = BETA_TWO * moment_two + (1.0 - BETA_TWO) * gradient * gradient
    first_hat = first_new / (1.0 - BETA_ONE ** STEP)
    second_hat = second_new / (1.0 - BETA_TWO ** STEP)
    weight_new = weight - step_rate * (first_hat / (jnp.sqrt(second_hat) + 1e-08) + DECAY * weight)
    return (first_new, second_new, weight_new)

def reference(features, lengths, labels, direct, squeeze, spatial, shrink, volume, pooled, readout, affine, first_direct, first_squeeze, first_spatial, first_shrink, first_volume, first_pooled, first_readout, first_affine, second_direct, second_squeeze, second_spatial, second_shrink, second_volume, second_pooled, second_readout, second_affine, running):
    stored = [direct, squeeze, spatial, shrink, volume, pooled, readout, affine]
    rows = weight_rows()
    masters = [unflat(stored[member], rows[member]) for member in range(6)]
    masters = masters + [readout.reshape(FEAT, CLASSES), affine]
    firsts = [first_direct, first_squeeze, first_spatial, first_shrink, first_volume, first_pooled, first_readout, first_affine]
    seconds = [second_direct, second_squeeze, second_spatial, second_shrink, second_volume, second_pooled, second_readout, second_affine]
    field = features.reshape(N_CHAN, CLIPS, TMAX, SIDE, SIDE, CIN // N_CHAN)
    field = jnp.moveaxis(field, 0, 4).reshape(CLIPS, TMAX, SIDE, SIDE, CIN)
    step_mask = (jnp.arange(TMAX)[None, :] < lengths[:, None]).astype(jnp.float32)
    voxel_mask = jnp.broadcast_to(step_mask[:, :, None, None, None], (CLIPS, TMAX, SIDE, SIDE, 1))
    onehot = (labels[:, :, None] == jnp.arange(CLASSES)[None, None, :]).astype(jnp.float32)
    counted = jnp.sum(step_mask)
    voxels = counted * (SIDE * SIDE)
    objective = partial(forward, features=field.astype(jnp.float32), voxel_mask=voxel_mask, step_mask=step_mask, onehot=onehot, voxels=voxels, counted=counted)
    value_out, pullback, auxiliary = jax.vjp(objective, *masters, has_aux=True)
    gradients = pullback(jnp.ones((), jnp.float32))
    flat_grads = [reflat(gradients[member]) for member in range(6)]
    flat_grads = flat_grads + [gradients[6].reshape(N_CHAN, -1), gradients[7]]
    rates = step_rates()
    updated = [adamw(stored[member], firsts[member], seconds[member], flat_grads[member], rates[member]) for member in range(8)]
    fresh = pack([jnp.stack([average, variance * voxels / (voxels - 1.0)]) for average, variance in auxiliary[1]])
    running_next = MOMENTUM * running + (1.0 - MOMENTUM) * fresh
    copies = jnp.concatenate([updated[member][2] for member in range(7)], axis=1).astype(jnp.bfloat16)
    return (updated[0][0], updated[1][0], updated[2][0], updated[3][0], updated[4][0], updated[5][0], updated[6][0], updated[7][0], updated[0][1], updated[1][1], updated[2][1], updated[3][1], updated[4][1], updated[5][1], updated[6][1], updated[7][1], updated[0][2], updated[1][2], updated[2][2], updated[3][2], updated[4][2], updated[5][2], updated[6][2], updated[7][2], running_next, auxiliary[0], counted, copies)
```

```python
import math
from functools import partial

import jax
import jax.numpy as jnp
from jax import lax
from jax.experimental import pallas as pl
from jax.experimental.pallas import tpu as pltpu
from jax.sharding import PartitionSpec as P

CIN = 832
B0 = 384
R1 = 192
O1 = 384
R2 = 48
O2 = 128
B3 = 128
CLASSES = 400
SIDE = 7
STEP = 5
NC = 4
NB = 32
POS = SIDE * SIDE
ROWS = 32
VOX = POS * ROWS
GROUPS = VOX // 8
GPAD = 208
CB = CIN // NC
GW = 8 * CB
HALF = 25

EPS = 1e-05
BETA_ONE = 0.5
BETA_TWO = 0.5
DECAY = 0.01
MOMENTUM = 0.99

MESH = pl.DeviceIdType.MESH
F32 = jnp.float32
BF16 = jnp.bfloat16


def step_rates():
    return [
        1.5 / math.sqrt(CIN),
        1.5 / math.sqrt(CIN),
        1.5 / math.sqrt(27 * R1),
        1.5 / math.sqrt(CIN),
        1.5 / math.sqrt(27 * R2),
        1.5 / math.sqrt(CIN),
        0.2,
        0.3,
    ]


def adamw(weight, moment_one, moment_two, gradient, step_rate):
    first_new = BETA_ONE * moment_one + (1.0 - BETA_ONE) * gradient
    second_new = BETA_TWO * moment_two + (1.0 - BETA_TWO) * gradient * gradient
    first_hat = first_new / (1.0 - BETA_ONE**STEP)
    second_hat = second_new / (1.0 - BETA_TWO**STEP)
    weight_new = weight - step_rate * (first_hat / (jnp.sqrt(second_hat) + 1e-08) + DECAY * weight)
    return (first_new, second_new, weight_new)


def window_of(r):
    start = CB * r
    tile, offset = divmod(start, 128)
    lanes = 256 if offset + CB <= 256 else 384
    return tile * 128, offset, lanes


def dot(a, b):
    return jnp.dot(a, b, preferred_element_type=F32)


def dot_t(a, b, ca, cb):
    return lax.dot_general(a, b, (((ca,), (cb,)), ((), ())), preferred_element_type=F32)


def send_to(src, dst, send, recv, target):
    return pltpu.make_async_remote_copy(
        src_ref=src, dst_ref=dst, send_sem=send, recv_sem=recv, device_id=target,
        device_id_type=MESH,
    )


def batch_peer(me, d):
    return {"batch": lax.rem(me + d, NB)}


def chan_peer(me, d):
    return {"chan": lax.rem(me + d, NC)}


def share_start(buf, me, send, recv):
    def one(d, carry):
        send_to(buf.at[me], buf.at[me], send.at[d], recv.at[d], batch_peer(me, d)).start()
        return carry

    lax.fori_loop(1, NB, one, 0)


def share_wait(buf, me, send, recv):
    def one(d, carry):
        src = lax.rem(me - d + NB, NB)
        send_to(buf.at[src], buf.at[src], send.at[d], recv.at[d], batch_peer(me, d)).wait_recv()
        return carry

    lax.fori_loop(1, NB, one, 0)

    def two(d, carry):
        send_to(buf.at[me], buf.at[me], send.at[d], recv.at[d], batch_peer(me, d)).wait_send()
        return carry

    lax.fori_loop(1, NB, two, 0)


def total_of(buf, count):
    acc = buf[0]
    for slot in range(1, count):
        acc = acc + buf[slot]
    return acc


def core_kernel(
    x_ref, len_ref, lab_ref, w1_ref, wc_ref, wct_ref, r_ref, aff_ref,
    gwc_ref, gw1_ref, gr_ref, st_ref, sc_ref,
    xf, xg, w1s, ynat, ypos, box, ob, msg, got, apad, acol, at, y2, dpre, dypad, dm, dgot, dnat,
    lbuf, sbuf_a, sbuf_b, sbuf_c, sbuf_d,
    xs, xr, ms, mr, ls, lr, ds_, dr,
    as_, ar, bs, br, cs, cr, es, er,
):
    me_b = lax.axis_index("batch")
    me = lax.axis_index("chan")

    barrier = pltpu.get_barrier_semaphore()

    def greet(d, carry):
        pl.semaphore_signal(barrier, inc=1, device_id=batch_peer(me_b, d), device_id_type=MESH)
        return carry

    lax.fori_loop(1, NB, greet, 0)
    for d in range(1, NC):
        pl.semaphore_signal(barrier, inc=1, device_id=chan_peer(me, d), device_id_type=MESH)

    def flat_rows(i, carry):
        v = x_ref[:, pl.ds(pl.multiple_of(i * 1024, 1024), 1024)].astype(F32)
        xf[pl.ds(pl.multiple_of(i * 8, 8), 8), :] = v.reshape(8, 128)
        return carry

    lax.fori_loop(0, 318, flat_rows, 0, unroll=6)
    xf[pl.ds(2544, 4), :] = x_ref[:, 318 * 1024 : 318 * 1024 + 512].astype(F32).reshape(4, 128)
    xf[pl.ds(2548, 2704 - 2548), :] = jnp.zeros((2704 - 2548, 128), F32)
    for i in range(13):
        xg[me, :, 128 * i : 128 * i + 128] = xf[pl.ds(i, GPAD, stride=13), :].astype(BF16)

    pl.semaphore_wait(barrier, NB - 1 + NC - 1)

    right, left = chan_peer(me, 1), chan_peer(me, NC - 1)
    left_i, right_i = lax.rem(me + NC - 1, NC), lax.rem(me + 1, NC)
    cut = 112

    def part(who, low):
        return xg.at[who, 0:cut] if low else xg.at[who, cut:GPAD]

    hops = []
    for i, (low, to) in enumerate([(True, right), (False, left), (False, right), (True, left)]):
        c = send_to(part(me, low), part(me, low), xs.at[i], xr.at[i], to)
        c.start()
        hops.append(c)

    rowi = lax.broadcasted_iota(jnp.int32, (ROWS, 128), 0)
    lane = lax.broadcasted_iota(jnp.int32, (ROWS, 128), 1)
    clip = rowi // 4
    step = rowi - clip * 4
    lens = jnp.zeros((ROWS, 128), jnp.int32)
    for c in range(8):
        lens = jnp.where(clip == c, len_ref[c], lens)
    mask = (step < lens).astype(F32)
    has_prev = (step > 0).astype(F32)
    has_next = (step < 3).astype(F32)

    def prev_t(v):
        return pltpu.roll(v, 1, 0) * has_prev

    def next_t(v):
        return pltpu.roll(v, ROWS - 1, 0) * has_next

    n_t = mask + prev_t(mask) + next_t(mask)
    is_pool = lane >= 96
    low_half = lane < 64

    def zero_w(i, carry):
        w1s[i] = jnp.zeros((NC, 384, 256), BF16)
        return carry

    lax.fori_loop(0, 8, zero_w, 0)
    for r in range(8):
        _, off, _ = window_of(r)
        for k in range(NC):
            w1s[r, k, off : off + CB, :] = w1_ref[k * CB : (k + 1) * CB, :]

    def zero_pad(i, carry):
        apad[i] = jnp.zeros((ROWS, 256), BF16)
        dypad[i] = jnp.zeros((ROWS, 384), BF16)
        box[i] = jnp.zeros((ROWS, 128), F32)
        return carry

    lax.fori_loop(0, 81, zero_pad, 0)
    dnat[...] = jnp.zeros_like(dnat)

    hops[0].wait_recv()
    f0 = send_to(part(left_i, True), part(left_i, True), xs.at[4], xr.at[4], right)
    f0.start()
    hops[1].wait_recv()
    f1 = send_to(part(right_i, False), part(right_i, False), xs.at[5], xr.at[5], left)
    f1.start()
    hops[2].wait_recv()
    hops[3].wait_recv()
    f0.wait()
    f1.wait()
    for c in hops:
        c.wait_send()

    for r in range(8):
        first, _, lanes = window_of(r)
        acc = jnp.zeros((GPAD, 256), F32)
        for k in range(NC):
            acc = acc + dot(xg[k, :, first : first + lanes], w1s[r, k, 0:lanes, :])
        ynat[0, pl.ds(r, GPAD, stride=8), :] = acc[:, 0:128]
        ynat[1, pl.ds(r, GPAD, stride=8), :] = acc[:, 128:256]

    def padded(p):
        return (p // SIDE + 1) * 9 + lax.rem(p, SIDE) + 1

    def to_pos(p, carry):
        v = ynat[0, pl.ds(p, ROWS, stride=POS), :]
        ypos[p, :, 0:128] = v
        ypos[p, :, 128:256] = ynat[1, pl.ds(p, ROWS, stride=POS), :]
        mz = v * mask
        box[padded(p)] = mz + prev_t(mz) + next_t(mz)
        return carry

    lax.fori_loop(0, POS, to_pos, 0)

    def spread(p):
        h, w = p // SIDE, lax.rem(p, SIDE)
        acc = jnp.zeros((ROWS, 128), F32)
        for dh in range(3):
            for dw in range(3):
                acc = acc + box[(h + dh) * 9 + w + dw]
        n_h = 3 - (h == 0).astype(jnp.int32) - (h == SIDE - 1).astype(jnp.int32)
        n_w = 3 - (w == 0).astype(jnp.int32) - (w == SIDE - 1).astype(jnp.int32)
        return acc, (n_h * n_w).astype(F32)

    def pool(p, carry):
        s1, s2 = carry
        acc, n = spread(p)
        v = ypos[p]
        v0 = jnp.where(is_pool, acc / jnp.maximum(n_t * n, 1.0), v[:, 0:128])
        v1 = v[:, 128:256]
        ypos[p] = jnp.concatenate([v0, v1], axis=1)
        m0, m1 = v0 * mask, v1 * mask
        return (
            s1 + jnp.concatenate([m0, m1], axis=1),
            s2 + jnp.concatenate([m0 * v0, m1 * v1], axis=1),
        )

    zero256 = jnp.zeros((ROWS, 256), F32)
    zero128 = jnp.zeros((ROWS, 128), F32)
    s1, s2 = lax.fori_loop(0, POS, pool, (zero256, zero256))

    def col(v):
        return jnp.sum(v, axis=0, keepdims=True)

    def pack_rows(rows):
        fill = [jnp.zeros((1, 128), F32)] * (8 - len(rows))
        return jnp.concatenate(list(rows) + fill, axis=0)

    sbuf_a[me_b] = pack_rows(
        [col(s1[:, 0:128]), col(s1[:, 128:256]), col(s2[:, 0:128]), col(s2[:, 128:256]), col(mask)]
    )
    share_start(sbuf_a, me_b, as_, ar)
    share_wait(sbuf_a, me_b, as_, ar)
    tot = total_of(sbuf_a, NB)
    counted = tot[4:5, :]
    voxels = counted * float(POS)

    def norm_of(sum1, sum2, tile):
        avg = sum1 / voxels
        var = sum2 / voxels - avg * avg
        inv = lax.rsqrt(var + EPS)
        gain = aff_ref[0:1, 128 * tile : 128 * tile + 128]
        bias = aff_ref[1:2, 128 * tile : 128 * tile + 128]
        return avg, var, inv, gain, bias

    n0 = norm_of(tot[0:1], tot[2:3], 0)
    n1 = norm_of(tot[1:2], tot[3:4], 1)

    def forward(y, n):
        normed = (y - n[0]) * n[2]
        pre = n[3] * normed + n[4]
        sig = jax.nn.sigmoid(pre)
        return normed, pre, sig

    def act1(p, carry):
        _, pre, sig = forward(ypos[p][:, 128:256], n1)
        ob[p] = (mask * (pre * sig))
        return carry

    lax.fori_loop(0, POS, act1, 0)
    ob[POS] = zero128

    def to_msg(p, carry):
        msg[p] = jnp.where(low_half, ob[p], pltpu.roll(ob[p + HALF], 64, 1)).astype(BF16)
        return carry

    lax.fori_loop(0, HALF, to_msg, 0)
    ms_c = []
    for d in range(1, NC):
        c = send_to(msg, got.at[me], ms.at[d], mr.at[d], chan_peer(me, d))
        c.start()
        ms_c.append(c)
    got[me] = msg[...]

    def act0(p, carry):
        _, pre, sig = forward(ypos[p][:, 0:128], n0)
        return carry + mask * (pre * sig)

    feat0 = lax.fori_loop(0, POS, act0, zero128)

    for c in ms_c:
        c.wait_recv()

    def unpack(p, carry):
        g = [got[j, p].astype(F32) for j in range(NC)]
        rl = [pltpu.roll(v, 64, 1) for v in g]
        low = jnp.concatenate(
            [jnp.where(low_half, g[0], rl[1]), jnp.where(low_half, g[2], rl[3])], axis=1
        ).astype(BF16)
        apad[padded(p)] = low
        acol[p] = low
        high = jnp.concatenate(
            [jnp.where(low_half, rl[0], g[1]), jnp.where(low_half, rl[2], g[3])], axis=1
        ).astype(BF16)

        @pl.when(p < POS - HALF)
        def _():
            apad[padded(p + HALF)] = high
            acol[p + HALF] = high

        return carry

    lax.fori_loop(0, HALF, unpack, 0)

    def conv(h, carry):
        s1, s2 = carry
        acc = jnp.zeros((SIDE * ROWS, 384), F32)
        for q in range(9):
            dh, dw = divmod(q, 3)
            lhs = apad[pl.ds((h + dh) * 9 + dw, SIDE)].reshape(SIDE * ROWS, 256)
            acc = acc + dot(lhs, wc_ref[q])
        for w in range(SIDE):
            t = acc[w * ROWS : (w + 1) * ROWS]
            y = t[:, 128:256] + prev_t(t[:, 0:128]) + next_t(t[:, 256:384])
            y2[h * SIDE + w] = y
            m = y * mask
            s1 = s1 + m
            s2 = s2 + m * y
        return s1, s2

    s1, s2 = lax.fori_loop(0, SIDE, conv, (zero128, zero128))
    sbuf_b[me_b] = pack_rows([col(s1), col(s2)])
    share_start(sbuf_b, me_b, bs, br)
    at[...] = jnp.transpose(acol[...].reshape(VOX, 256))
    share_wait(sbuf_b, me_b, bs, br)
    totb = total_of(sbuf_b, NB)
    n2 = norm_of(totb[0:1], totb[1:2], 2)

    def act2(p, carry):
        _, pre, sig = forward(y2[p], n2)
        return carry + mask * (pre * sig)

    feat2 = lax.fori_loop(0, POS, act2, zero128)
    feature = (jnp.concatenate([feat0, feat2], axis=1) / float(POS)).astype(BF16)
    lbuf[me] = dot(feature, r_ref[...])
    ls_c = []
    for d in range(1, NC):
        c = send_to(lbuf.at[me], lbuf.at[me], ls.at[d], lr.at[d], chan_peer(me, d))
        c.start()
        ls_c.append(c)
    for c in ls_c:
        c.wait_recv()
    logits = total_of(lbuf, NC)
    cls = lax.broadcasted_iota(jnp.int32, (ROWS, 512), 1)
    row512 = lax.broadcasted_iota(jnp.int32, (ROWS, 512), 0)
    labs = jnp.zeros((ROWS, 512), jnp.int32)
    for i in range(ROWS):
        labs = jnp.where(row512 == i, lab_ref[i // 4, i % 4], labs)
    real = cls < CLASSES
    logits = jnp.where(real, logits, -1e30)
    peak = jnp.max(logits, axis=1, keepdims=True)
    ex = jnp.exp(logits - peak)
    se = jnp.sum(ex, axis=1, keepdims=True)
    logprob = logits - peak - jnp.log(se)
    mask1 = mask[:, 0:1]
    hit = cls == labs
    loss_rows = -jnp.sum(jnp.where(hit, logprob, 0.0), axis=1, keepdims=True) * mask1
    soft = jnp.where(real, jnp.exp(logprob), 0.0)
    dlog = ((soft - hit.astype(F32)) * mask1 / counted[:, 0:1]).astype(BF16)
    dfeat = dot_t(dlog, r_ref[...], 1, 1) / float(POS)
    df0, df2 = dfeat[:, 0:128], dfeat[:, 128:256]

    def back(y, n, dout):
        normed, pre, sig = forward(y, n)
        return dout * mask * sig * (1.0 + pre * (1.0 - sig)), normed

    def back02(p, carry):
        g0, b0, g2, b2 = carry
        d0, m0 = back(ypos[p][:, 0:128], n0, df0)
        d2, m2 = back(y2[p], n2, df2)
        dpre[p] = jnp.concatenate([d0, d2], axis=1)
        return g0 + d0 * m0, b0 + d0, g2 + d2 * m2, b2 + d2

    g0, b0, g2, b2 = lax.fori_loop(0, POS, back02, (zero128,) * 4)
    loss_row = jnp.broadcast_to(jnp.sum(loss_rows, axis=0, keepdims=True), (1, 128))
    sbuf_c[me_b] = pack_rows([col(g0), col(b0), col(g2), col(b2), loss_row])
    share_start(sbuf_c, me_b, cs, cr)
    gr_ref[...] = dot_t(feature, dlog, 0, 0)
    for c in ls_c:
        c.wait_send()
    for c in ms_c:
        c.wait_send()
    share_wait(sbuf_c, me_b, cs, cr)
    totc = total_of(sbuf_c, NB)

    def finish(y, n, d, gg, gb):
        normed = (y - n[0]) * n[2]
        return mask * n[3] * n[2] * (d - gb / voxels - normed * gg / voxels)

    def dy2_at(p, carry):
        d = dpre[p]
        v = finish(y2[p], n2, d[:, 128:256], totc[2:3], totc[3:4])
        dypad[padded(p)] = jnp.concatenate([next_t(v), v, prev_t(v)], axis=1).astype(BF16)
        return carry

    lax.fori_loop(0, POS, dy2_at, 0)

    def conv_back(h, carry):
        acc = jnp.zeros((SIDE * ROWS, 256), F32)
        for q in range(9):
            dh, dw = divmod(q, 3)
            lhs = dypad[pl.ds((h + 2 - dh) * 9 + 2 - dw, SIDE)].reshape(SIDE * ROWS, 384)
            acc = acc + dot(lhs, wct_ref[q])
        for t in range(2):
            ynat[t, pl.ds(pl.multiple_of(h * SIDE * ROWS, SIDE * ROWS), SIDE * ROWS), :] = acc[
                :, 128 * t : 128 * t + 128
            ]
        return carry

    lax.fori_loop(0, SIDE, conv_back, 0)

    def to_dm(p, carry):
        for j in range(NC):
            a = ynat[j // 2, pl.ds(pl.multiple_of(p * ROWS, ROWS), ROWS), :]
            b = ynat[j // 2, pl.ds(pl.multiple_of((p + HALF) * ROWS, ROWS), ROWS), :]
            if j % 2 == 0:
                dm[j, p] = jnp.where(low_half, a, pltpu.roll(b, 64, 1))
            else:
                dm[j, p] = jnp.where(low_half, pltpu.roll(a, 64, 1), b)
        return carry

    for t in range(2):
        ynat[t, pl.ds(VOX, ROWS), :] = zero128
    lax.fori_loop(0, HALF, to_dm, 0)
    ds_c = []
    for d in range(1, NC):
        to = lax.rem(me + d, NC)
        c = send_to(dm.at[to], dgot.at[me], ds_.at[d], dr.at[d], chan_peer(me, d))
        c.start()
        ds_c.append(c)
    dgot[me] = dm[me]

    def grad_conv(q, carry):
        dh = q // 3
        dw = q - dh * 3
        rhs = jnp.concatenate(
            [
                dypad[pl.ds((h + 2 - dh) * 9 + 2 - dw, SIDE)].reshape(SIDE * ROWS, 384)
                for h in range(SIDE)
            ],
            axis=0,
        )
        gwc_ref[q] = dot(at[...], rhs)
        return carry

    lax.fori_loop(0, 9, grad_conv, 0)

    def dy0_at(p, carry):
        v = finish(ypos[p][:, 0:128], n0, dpre[p][:, 0:128], totc[0:1], totc[1:2])
        v = v.astype(BF16).astype(F32)
        h, w = p // SIDE, lax.rem(p, SIDE)
        n_h = 3 - (h == 0).astype(jnp.int32) - (h == SIDE - 1).astype(jnp.int32)
        n_w = 3 - (w == 0).astype(jnp.int32) - (w == SIDE - 1).astype(jnp.int32)
        share = v / jnp.maximum(n_t * (n_h * n_w).astype(F32), 1.0)
        box[padded(p)] = share + prev_t(share) + next_t(share)
        ypos[p, :, 0:128] = v
        return carry

    lax.fori_loop(0, POS, dy0_at, 0)

    def dy0_nat(p, carry):
        acc, _ = spread(p)
        v = jnp.where(is_pool, acc * mask, ypos[p][:, 0:128])
        lowv = v - v.astype(BF16).astype(F32)
        dnat[0, pl.ds(p, ROWS, stride=POS), :] = v
        dnat[1, pl.ds(p, ROWS, stride=POS), :] = lowv
        return carry

    lax.fori_loop(0, POS, dy0_nat, 0)

    for tile in range(2):
        gw1_ref[:, 128 * tile : 128 * tile + 128] = jnp.zeros((CIN, 128), F32)

    def grad_one(r, width, fold):
        first, off, lanes = window_of(r)
        rhs = jnp.concatenate(
            [dnat[t, pl.ds(r, GPAD, stride=8), :] for t in range(width // 128)], axis=1
        ).astype(BF16)
        for k in range(NC):
            res = dot_t(xg[k, :, first : first + lanes], rhs, 0, 0)[off : off + CB]
            if fold:
                gw1_ref[k * CB : (k + 1) * CB, 0:128] += res[:, 0:128] + res[:, 128:256]
            else:
                gw1_ref[k * CB : (k + 1) * CB, 128:256] += res

    for r in range(8):
        grad_one(r, 256, True)

    for c in ds_c:
        c.wait_recv()

    def back1(p, carry):
        g1, b1 = carry
        s = dgot[0, p] + dgot[1, p] + dgot[2, p] + dgot[3, p]
        d, m = back(ypos[p][:, 128:256], n1, jnp.where(low_half, s, 0.0))
        dpre[p, :, 0:128] = d
        g1, b1 = g1 + d * m, b1 + d
        q = jnp.minimum(p + HALF, POS - 1)
        live = (p < POS - HALF).astype(F32)
        d, m = back(ypos[q][:, 128:256], n1, jnp.where(low_half, pltpu.roll(s, 64, 1), 0.0) * live)

        @pl.when(p < POS - HALF)
        def _():
            dpre[p + HALF, :, 0:128] = d

        return g1 + d * m, b1 + d

    g1, b1 = lax.fori_loop(0, HALF, back1, (zero128, zero128))
    sbuf_d[me_b] = pack_rows([col(g1), col(b1)])
    share_start(sbuf_d, me_b, es, er)
    for c in ds_c:
        c.wait_send()
    share_wait(sbuf_d, me_b, es, er)
    totd = total_of(sbuf_d, NB)

    def dy1_nat(p, carry):
        v = finish(ypos[p][:, 128:256], n1, dpre[p][:, 0:128], totd[0:1], totd[1:2])
        dnat[0, pl.ds(p, ROWS, stride=POS), :] = v
        return carry

    lax.fori_loop(0, POS, dy1_nat, 0)
    for r in range(8):
        grad_one(r, 128, False)

    fix = voxels / (voxels - 1.0)
    for tile, n, gg, gb in (
        (0, n0, totc[0:1], totc[1:2]),
        (1, n1, totd[0:1], totd[1:2]),
        (2, n2, totc[2:3], totc[3:4]),
    ):
        st_ref[:, 128 * tile : 128 * tile + 128] = pack_rows([gg, gb, n[0], n[1] * fix])
    sc_ref[...] = pack_rows([totc[4:5], counted])


def core(x, lengths, labels, w1, wc, wct, r, aff):
    vm = pl.BlockSpec(memory_space=pltpu.VMEM)
    sm = pl.BlockSpec(memory_space=pltpu.SMEM)
    dma = pltpu.SemaphoreType.DMA
    return pl.pallas_call(
        core_kernel,
        out_shape=(
            jax.ShapeDtypeStruct((9, 256, 384), F32),
            jax.ShapeDtypeStruct((CIN, 256), F32),
            jax.ShapeDtypeStruct((256, 512), F32),
            jax.ShapeDtypeStruct((8, 384), F32),
            jax.ShapeDtypeStruct((8, 128), F32),
        ),
        in_specs=[vm, sm, sm, vm, vm, vm, vm, vm],
        out_specs=(vm,) * 5,
        scratch_shapes=[
            pltpu.VMEM((13 * GPAD, 128), F32),
            pltpu.VMEM((NC, GPAD, GW), BF16),
            pltpu.VMEM((8, NC, 384, 256), BF16),
            pltpu.VMEM((2, 8 * GPAD, 128), F32),
            pltpu.VMEM((POS, ROWS, 256), F32),
            pltpu.VMEM((81, ROWS, 128), F32),
            pltpu.VMEM((POS + 1, ROWS, 128), F32),
            pltpu.VMEM((HALF, ROWS, 128), BF16),
            pltpu.VMEM((NC, HALF, ROWS, 128), BF16),
            pltpu.VMEM((81, ROWS, 256), BF16),
            pltpu.VMEM((POS, ROWS, 256), BF16),
            pltpu.VMEM((256, VOX), BF16),
            pltpu.VMEM((POS, ROWS, 128), F32),
            pltpu.VMEM((POS, ROWS, 256), F32),
            pltpu.VMEM((81, ROWS, 384), BF16),
            pltpu.VMEM((NC, HALF, ROWS, 128), F32),
            pltpu.VMEM((NC, HALF, ROWS, 128), F32),
            pltpu.VMEM((2, 8 * GPAD, 128), F32),
            pltpu.VMEM((NC, ROWS, 512), F32),
            pltpu.VMEM((NB, 8, 128), F32),
            pltpu.VMEM((NB, 8, 128), F32),
            pltpu.VMEM((NB, 8, 128), F32),
            pltpu.VMEM((NB, 8, 128), F32),
            dma((6,)), dma((6,)), dma((NC,)), dma((NC,)), dma((NC,)), dma((NC,)), dma((NC,)),
            dma((NC,)),
            dma((NB,)), dma((NB,)), dma((NB,)), dma((NB,)), dma((NB,)), dma((NB,)), dma((NB,)),
            dma((NB,)),
        ],
        compiler_params=pltpu.CompilerParams(
            collective_id=0, has_side_effects=True, vmem_limit_bytes=58 << 20
        ),
        name="block",
    )(x, lengths, labels, w1, wc, wct, r, aff)


def split_columns(packed, widths):
    pieces = []
    offset = 0
    for channels in widths:
        pieces.append(packed[..., offset : offset + channels])
        offset = offset + channels
    return pieces


def conv_weights(spatial, volume):
    sp = spatial.reshape(3, 9, NC, 48, 96)
    vo = volume.reshape(3, 9, NC, 12, 32)
    sp = jnp.pad(sp, ((0, 0), (0, 0), (0, 0), (0, 16), (0, 32)))
    vo = jnp.pad(vo, ((0, 0), (0, 0), (0, 0), (48, 4), (96, 0)))
    both = (sp + vo).astype(BF16)
    return jnp.transpose(both, (1, 2, 3, 0, 4)).reshape(9, 256, 384)


def conv_grads(g):
    g = g.reshape(9, NC, 64, 3, 128)
    sp = jnp.transpose(g[:, :, 0:48, :, 0:96], (3, 0, 1, 2, 4)).reshape(1, -1)
    vo = jnp.transpose(g[:, :, 48:60, :, 96:128], (3, 0, 1, 2, 4)).reshape(1, -1)
    return sp, vo


def per_device(
    features, lengths, labels, direct, squeeze, spatial, shrink, volume, pooled, readout, affine,
    first_direct, first_squeeze, first_spatial, first_shrink, first_volume, first_pooled,
    first_readout, first_affine, second_direct, second_squeeze, second_spatial, second_shrink,
    second_volume, second_pooled, second_readout, second_affine, running,
):
    masters = [direct, squeeze, spatial, shrink, volume, pooled, readout, affine]
    firsts = [
        first_direct, first_squeeze, first_spatial, first_shrink, first_volume, first_pooled,
        first_readout, first_affine,
    ]
    seconds = [
        second_direct, second_squeeze, second_spatial, second_shrink, second_volume,
        second_pooled, second_readout, second_affine,
    ]
    w1 = jnp.concatenate(
        [
            direct.reshape(CIN, 96), pooled.reshape(CIN, 32), squeeze.reshape(CIN, 48),
            shrink.reshape(CIN, 12), jnp.zeros((CIN, 68), F32),
        ],
        axis=1,
    ).astype(BF16)
    wc = conv_weights(spatial, volume)
    wct = jnp.transpose(wc, (0, 2, 1))
    rd = readout.reshape(256, CLASSES)
    rp = jnp.concatenate([rd[0:96], rd[224:256], rd[96:192], rd[192:224]], axis=0)
    rp = jnp.pad(rp, ((0, 0), (0, 112))).astype(BF16)
    a_d, a_s, a_k, a_p, a_sp, a_v = split_columns(affine, [96, 48, 12, 32, 96, 32])
    aff = jnp.concatenate([a_d, a_p, a_s, a_k, jnp.zeros((2, 68), F32), a_sp, a_v], axis=1)
    aff = jnp.pad(aff, ((0, 6), (0, 0)))

    gwc, gw1, gr, stats, scal = core(features, lengths, labels, w1, wc, wct, rp, aff)

    g_sp, g_vo = conv_grads(gwc)
    g_rd = jnp.concatenate([gr[0:96], gr[128:224], gr[224:256], gr[96:128]], axis=0)[:, :CLASSES]
    local = [
        gw1[:, 0:96].reshape(1, -1),
        gw1[:, 128:176].reshape(1, -1),
        g_sp,
        gw1[:, 176:188].reshape(1, -1),
        g_vo,
        gw1[:, 96:128].reshape(1, -1),
        g_rd.reshape(1, -1),
    ]
    grads = list(lax.psum(tuple(local), "batch"))

    def unlanes(rows):
        return jnp.concatenate(
            [rows[:, 0:96], rows[:, 128:188], rows[:, 96:128], rows[:, 256:384]], axis=1
        )

    grads.append(unlanes(stats[0:2]))
    rates = step_rates()
    updated = [
        adamw(masters[i], firsts[i], seconds[i], grads[i], rates[i]) for i in range(8)
    ]
    running_next = MOMENTUM * running + (1.0 - MOMENTUM) * unlanes(stats[2:4])
    copies = jnp.concatenate([updated[i][2] for i in range(7)], axis=1).astype(BF16)
    return (
        *[updated[i][0] for i in range(8)],
        *[updated[i][1] for i in range(8)],
        *[updated[i][2] for i in range(8)],
        running_next,
        scal[0, 0],
        scal[1, 0],
        copies,
    )


def solution(mesh):
    flat = P("chan", None)
    wide = P(None, "chan")
    weights = (flat,) * 7 + (wide,)
    return jax.shard_map(
        per_device,
        mesh=mesh,
        in_specs=(P("chan", "batch"), P("batch"), P("batch", None)) + weights * 3 + (wide,),
        out_specs=weights * 3 + (wide, P(), P(), flat),
        check_vma=False,
    )
```

```python
import math
from functools import partial

import jax
import jax.numpy as jnp
from jax import lax
from jax.experimental import pallas as pl
from jax.experimental.pallas import tpu as pltpu
from jax.sharding import PartitionSpec as P

CIN = 832
B0 = 384
R1 = 192
O1 = 384
R2 = 48
O2 = 128
B3 = 128
CLASSES = 400
SIDE = 7
STEP = 5
NC = 4
NB = 32
POS = SIDE * SIDE
ROWS = 32
VOX = POS * ROWS
GROUPS = VOX // 8
GPAD = 208
CB = CIN // NC
GW = 8 * CB
HALF = 25
TAPS = 27
FLAT = {"direct": 624, "squeeze": 312, "spatial": 3888, "shrink": 78, "volume": 324, "pooled": 208,
        "readout": 800}
NAMES = ("direct", "squeeze", "spatial", "shrink", "volume", "pooled", "readout")
BULK = {"spatial": 0, "volume": 3888, "direct": 4224, "pooled": 4848, "readout": 5056}
LATE = {"squeeze": 0, "shrink": 312}
CORE_ROWS = 3072
GROUP_ROWS = 1536
FIRST_ROWS = 384
LAST_ROWS = 96
LATE_ROWS = 16

EPS = 1e-05
BETA_ONE = 0.5
BETA_TWO = 0.5
DECAY = 0.01
MOMENTUM = 0.99

MESH = pl.DeviceIdType.MESH
F32 = jnp.float32
BF16 = jnp.bfloat16


def step_rates():
    return [
        1.5 / math.sqrt(CIN),
        1.5 / math.sqrt(CIN),
        1.5 / math.sqrt(27 * R1),
        1.5 / math.sqrt(CIN),
        1.5 / math.sqrt(27 * R2),
        1.5 / math.sqrt(CIN),
        0.2,
        0.3,
    ]


def adamw(weight, moment_one, moment_two, gradient, step_rate):
    first_new = BETA_ONE * moment_one + (1.0 - BETA_ONE) * gradient
    second_new = BETA_TWO * moment_two + (1.0 - BETA_TWO) * gradient * gradient
    first_hat = first_new / (1.0 - BETA_ONE**STEP)
    second_hat = second_new / (1.0 - BETA_TWO**STEP)
    weight_new = weight - step_rate * (first_hat / (jnp.sqrt(second_hat) + 1e-08) + DECAY * weight)
    return (first_new, second_new, weight_new)


def window_of(r):
    start = CB * r
    tile, offset = divmod(start, 128)
    lanes = 256 if offset + CB <= 256 else 384
    return tile * 128, offset, lanes


def dot(a, b):
    return jnp.dot(a, b, preferred_element_type=F32)


def dot_t(a, b, ca, cb):
    return lax.dot_general(a, b, (((ca,), (cb,)), ((), ())), preferred_element_type=F32)


def send_to(src, dst, send, recv, target):
    return pltpu.make_async_remote_copy(
        src_ref=src, dst_ref=dst, send_sem=send, recv_sem=recv, device_id=target,
        device_id_type=MESH,
    )


def batch_peer(me, d):
    return {"batch": lax.rem(me + d, NB)}


def chan_peer(me, d):
    return {"chan": lax.rem(me + d, NC)}


def share_start(buf, me, send, recv):
    def one(d, carry):
        send_to(buf.at[me], buf.at[me], send.at[d], recv.at[d], batch_peer(me, d)).start()
        return carry

    lax.fori_loop(1, NB, one, 0)


def share_wait(buf, me, send, recv):
    def one(d, carry):
        src = lax.rem(me - d + NB, NB)
        send_to(buf.at[src], buf.at[src], send.at[d], recv.at[d], batch_peer(me, d)).wait_recv()
        return carry

    lax.fori_loop(1, NB, one, 0)

    def two(d, carry):
        send_to(buf.at[me], buf.at[me], send.at[d], recv.at[d], batch_peer(me, d)).wait_send()
        return carry

    lax.fori_loop(1, NB, two, 0)


def digit_of(me, stride, size):
    return lax.rem(me // stride, size)


def digit_peer(me, stride, size, d):
    digit = digit_of(me, stride, size)
    return {"batch": me + stride * (lax.rem(digit + d, size) - digit)}


def piece(tiles, start, width, dest, lane):
    tile, off = divmod(start, 128)
    v = tiles[tile]
    if off + width > 128:
        v = jnp.where(lane >= off, v, tiles[tile + 1])
    shift = (dest - off) % 128
    return pltpu.roll(v, shift, 1) if shift else v


def joined(parts, lane, count):
    out = []
    moved = []
    for value, src, start, width in parts:
        shift = (start - src) % 128
        moved.append((pltpu.roll(value, shift, 1) if shift else value, start, width))
    for i in range(count):
        acc = None
        for value, start, width in moved:
            lo, hi = max(0, start - 128 * i), min(128, start + width - 128 * i)
            if lo < hi:
                acc = value if acc is None else jnp.where(lane >= lo, value, acc)
        out.append(acc)
    return out


def lanes_of(v):
    return lax.broadcasted_iota(jnp.int32, v, 1)


def prepare_w1(flat, wn, wk, w1s):
    lane = lanes_of((208, 128))
    tiles = [flat["direct"][pl.ds(i, 208, stride=3), :] for i in range(3)]
    pool = flat["pooled"][...]
    for j in range(4):
        v = jnp.where(
            lane < 96, piece(tiles, 96 * j, 96, 0, lane), piece([pool], 32 * j, 32, 96, lane)
        )
        wn[0, pl.ds(j, 208, stride=4), :] = v
    lane = lanes_of((104, 128))
    tiles = [flat["squeeze"][pl.ds(i, 104, stride=3), :] for i in range(3)]
    for j in range(8):
        wn[1, pl.ds(j, 104, stride=8), :] = piece(tiles, 48 * j, 48, 0, lane)
    lane = lanes_of((26, 128))
    tiles = [flat["shrink"][pl.ds(i, 26, stride=3), :] for i in range(3)]
    for j in range(32):
        wk[pl.ds(j, 26, stride=32), :] = piece(tiles, 12 * j, 12, 48, lane)
    lane = lanes_of((CB, 128))
    for k in range(NC):
        rows = slice(k * CB, (k + 1) * CB)
        second = jnp.where(lane < 48, wn[1, rows, :], jnp.where(lane < 60, wk[rows, :], 0.0))
        both = jnp.concatenate([wn[0, rows, :], second], axis=1).astype(BF16)
        for r in range(8):
            _, off, _ = window_of(r)
            w1s[r, k, off : off + CB, :] = both


def prepare_conv(flat, tb, vn, wc, wct):
    lane = lanes_of((324, 128))
    for j in range(4):
        v = piece([flat["volume"][...]], 32 * j, 32, 96, lane)
        vn[pl.ds(j, 324, stride=4), :] = jnp.where(lane >= 96, v, 0.0)
    vn[pl.ds(1296, 8), :] = jnp.zeros((8, 128), F32)
    lane48 = lanes_of((48, 128))
    row16 = lax.broadcasted_iota(jnp.int32, (16, 128), 0)

    def one(q, carry):
        for dt in range(3):
            tap = dt * 9 + q
            tiles = [
                flat["spatial"][pl.ds(tap * 144 + i, 48, stride=3), :] for i in range(3)
            ]
            for j in range(4):
                v = piece(tiles, 96 * j, 96, 0, lane48)
                tb[pl.ds(j, 48, stride=4), :] = jnp.where(lane48 < 96, v, 0.0)
            for j in range(NC):
                at = slice(128 * dt, 128 * dt + 128)
                wc[q, 64 * j : 64 * j + 48, at] = tb[48 * j : 48 * j + 48, :].astype(BF16)
                v = vn[pl.ds(tap * 48 + 12 * j, 16), :]
                wc[q, 64 * j + 48 : 64 * j + 64, at] = jnp.where(row16 < 12, v, 0.0).astype(BF16)
        wct[q] = jnp.transpose(wc[q])
        return carry

    lax.fori_loop(0, 9, one, 0)


def prepare_readout(flat, rn, rp):
    lane = lanes_of((32, 128))
    tiles = [flat["readout"][pl.ds(i, 32, stride=25), :] for i in range(25)]
    for t in range(4):
        width = min(128, CLASSES - 128 * t)
        for j in range(8):
            v = piece(tiles, CLASSES * j + 128 * t, width, 0, lane)
            rn[t, pl.ds(j, 32, stride=8), :] = v if width == 128 else jnp.where(lane < width, v, 0.0)
        at = slice(128 * t, 128 * t + 128)
        for dst, src, count in ((0, 0, 96), (96, 224, 32), (128, 96, 96), (224, 192, 32)):
            rp[dst : dst + count, at] = rn[t, src : src + count, :].astype(BF16)


def prepare_affine(aff, out):
    a = [aff[:, 0:128], aff[:, 128:256]]
    a.append(jnp.concatenate([aff[:, 256:316], jnp.zeros((2, 68), F32)], axis=1))
    lane = lanes_of((2, 128))
    t0 = jnp.where(lane < 96, a[0], piece(a, 156, 32, 96, lane))
    t1 = jnp.where(lane < 60, piece(a, 96, 60, 0, lane), 0.0)
    t2 = piece(a, 188, 128, 0, lane)
    for i, t in enumerate((t0, t1, t2)):
        out[0:2, 128 * i : 128 * i + 128] = t


def flatten_96(src, rows, put):
    lane = lanes_of((rows, 128))
    for i, v in enumerate(joined([(src(j), 0, 96 * j, 96) for j in range(4)], lane, 3)):
        put(i, v)


def flatten_32(src, rows):
    lane = lanes_of((rows, 128))
    return joined([(src(j), 96, 32 * j, 32) for j in range(4)], lane, 1)[0]


def total_of(buf, count):
    acc = buf[0]
    for slot in range(1, count):
        acc = acc + buf[slot]
    return acc


def core_kernel(
    x_hbm, len_ref, lab_ref, direct_hbm, squeeze_hbm, spatial_hbm, shrink_hbm, volume_hbm,
    pooled_hbm, readout_hbm, affine_ref,
    gb_ref, late_ref, st_ref, sc_ref,
    x_ref, f_direct, f_squeeze, f_spatial, f_shrink, f_volume, f_pooled, f_readout,
    wn, wk, tb, vn, rn, wc_ref, wct_ref, r_ref, aff_ref,
    xf, xg, w1s, ynat, ypos, box, ob, msg, got, apad, acol, at, y2, dpre, dypad, dm, dgot, dnat,
    gw1_ref, gq, gr, g, gcore, r1, r2, lsend, lgot,
    lbuf, sbuf_a, sbuf_b, sbuf_c, sbuf_d,
    xin, win, xs, xr, ms, mr, ls, lr, ds_, dr,
    as_, ar, bs, br, cs, cr, es, er, fs, fr, hs, hr,
    co_s, co_r, s1s, s1r, s2s, s2r, g1s, g1r, g2s, g2r, g3s, g3r,
):
    me_b = lax.axis_index("batch")
    me = lax.axis_index("chan")

    barrier = pltpu.get_barrier_semaphore()

    cuts = [0, 79 * 1024, 158 * 1024, 237 * 1024, 326144]
    x_in = []
    for i in range(4):
        at_ = pl.ds(cuts[i], cuts[i + 1] - cuts[i])
        c = pltpu.make_async_copy(x_hbm.at[:, at_], x_ref.at[:, at_], xin.at[i])
        c.start()
        x_in.append(c)
    flat = dict(
        direct=f_direct, squeeze=f_squeeze, spatial=f_spatial, shrink=f_shrink, volume=f_volume,
        pooled=f_pooled, readout=f_readout,
    )
    w_in = []
    for i, (src, name) in enumerate(
        zip(
            (direct_hbm, squeeze_hbm, spatial_hbm, shrink_hbm, volume_hbm, pooled_hbm, readout_hbm),
            NAMES,
        )
    ):
        c = pltpu.make_async_copy(src, flat[name], win.at[i])
        c.start()
        w_in.append(c)

    def greet(d, carry):
        pl.semaphore_signal(barrier, inc=1, device_id=batch_peer(me_b, d), device_id_type=MESH)
        return carry

    lax.fori_loop(1, NB, greet, 0)
    for d in range(1, NC):
        pl.semaphore_signal(barrier, inc=1, device_id=chan_peer(me, d), device_id_type=MESH)

    def flat_rows(i, carry):
        v = x_ref[:, pl.ds(pl.multiple_of(i * 1024, 1024), 1024)].astype(F32)
        xf[pl.ds(pl.multiple_of(i * 8, 8), 8), :] = v.reshape(8, 128)
        return carry

    for i in range(4):
        x_in[i].wait()
        first = 79 * i
        lax.fori_loop(first, first + 79 if i < 3 else 318, flat_rows, 0, unroll=4)
    xf[pl.ds(2544, 4), :] = x_ref[:, 318 * 1024 : 318 * 1024 + 512].astype(F32).reshape(4, 128)
    xf[pl.ds(2548, 2704 - 2548), :] = jnp.zeros((2704 - 2548, 128), F32)
    for i in range(13):
        xg[me, :, 128 * i : 128 * i + 128] = xf[pl.ds(i, GPAD, stride=13), :].astype(BF16)

    pl.semaphore_wait(barrier, NB - 1 + NC - 1)

    right, left = chan_peer(me, 1), chan_peer(me, NC - 1)
    left_i, right_i = lax.rem(me + NC - 1, NC), lax.rem(me + 1, NC)
    cut = 112

    def part(who, low):
        return xg.at[who, 0:cut] if low else xg.at[who, cut:GPAD]

    hops = []
    for i, (low, to) in enumerate([(True, right), (False, left), (False, right), (True, left)]):
        c = send_to(part(me, low), part(me, low), xs.at[i], xr.at[i], to)
        c.start()
        hops.append(c)

    rowi = lax.broadcasted_iota(jnp.int32, (ROWS, 128), 0)
    lane = lax.broadcasted_iota(jnp.int32, (ROWS, 128), 1)
    clip = rowi // 4
    step = rowi - clip * 4
    lens = jnp.zeros((ROWS, 128), jnp.int32)
    for c in range(8):
        lens = jnp.where(clip == c, len_ref[c], lens)
    mask = (step < lens).astype(F32)
    has_prev = (step > 0).astype(F32)
    has_next = (step < 3).astype(F32)

    def prev_t(v):
        return pltpu.roll(v, 1, 0) * has_prev

    def next_t(v):
        return pltpu.roll(v, ROWS - 1, 0) * has_next

    n_t = mask + prev_t(mask) + next_t(mask)
    is_pool = lane >= 96
    low_half = lane < 64

    def zero_w(i, carry):
        w1s[i] = jnp.zeros((NC, 384, 256), BF16)
        return carry

    lax.fori_loop(0, 8, zero_w, 0)
    for c in w_in:
        c.wait()
    prepare_w1(flat, wn, wk, w1s)
    prepare_affine(affine_ref, aff_ref)
    prepare_readout(flat, rn, r_ref)

    def zero_pad(i, carry):
        apad[i] = jnp.zeros((ROWS, 256), BF16)
        dypad[i] = jnp.zeros((ROWS, 384), BF16)
        box[i] = jnp.zeros((ROWS, 128), F32)
        return carry

    lax.fori_loop(0, 81, zero_pad, 0)
    dnat[...] = jnp.zeros_like(dnat)
    prepare_conv(flat, tb, vn, wc_ref, wct_ref)

    hops[0].wait_recv()
    f0 = send_to(part(left_i, True), part(left_i, True), xs.at[4], xr.at[4], right)
    f0.start()
    hops[1].wait_recv()
    f1 = send_to(part(right_i, False), part(right_i, False), xs.at[5], xr.at[5], left)
    f1.start()
    hops[2].wait_recv()
    hops[3].wait_recv()
    f0.wait()
    f1.wait()
    for c in hops:
        c.wait_send()

    for r in range(8):
        first, _, lanes = window_of(r)
        acc = jnp.zeros((GPAD, 256), F32)
        for k in range(NC):
            acc = acc + dot(xg[k, :, first : first + lanes], w1s[r, k, 0:lanes, :])
        ynat[0, pl.ds(r, GPAD, stride=8), :] = acc[:, 0:128]
        ynat[1, pl.ds(r, GPAD, stride=8), :] = acc[:, 128:256]

    def padded(p):
        return (p // SIDE + 1) * 9 + lax.rem(p, SIDE) + 1

    def to_pos(p, carry):
        v = ynat[0, pl.ds(p, ROWS, stride=POS), :]
        ypos[p, :, 0:128] = v
        ypos[p, :, 128:256] = ynat[1, pl.ds(p, ROWS, stride=POS), :]
        mz = v * mask
        box[padded(p)] = mz + prev_t(mz) + next_t(mz)
        return carry

    lax.fori_loop(0, POS, to_pos, 0)

    def spread(p):
        h, w = p // SIDE, lax.rem(p, SIDE)
        acc = jnp.zeros((ROWS, 128), F32)
        for dh in range(3):
            for dw in range(3):
                acc = acc + box[(h + dh) * 9 + w + dw]
        n_h = 3 - (h == 0).astype(jnp.int32) - (h == SIDE - 1).astype(jnp.int32)
        n_w = 3 - (w == 0).astype(jnp.int32) - (w == SIDE - 1).astype(jnp.int32)
        return acc, (n_h * n_w).astype(F32)

    def pool(p, carry):
        s1, s2 = carry
        acc, n = spread(p)
        v = ypos[p]
        v0 = jnp.where(is_pool, acc / jnp.maximum(n_t * n, 1.0), v[:, 0:128])
        v1 = v[:, 128:256]
        ypos[p] = jnp.concatenate([v0, v1], axis=1)
        m0, m1 = v0 * mask, v1 * mask
        return (
            s1 + jnp.concatenate([m0, m1], axis=1),
            s2 + jnp.concatenate([m0 * v0, m1 * v1], axis=1),
        )

    zero256 = jnp.zeros((ROWS, 256), F32)
    zero128 = jnp.zeros((ROWS, 128), F32)
    s1, s2 = lax.fori_loop(0, POS, pool, (zero256, zero256))

    def col(v):
        return jnp.sum(v, axis=0, keepdims=True)

    def pack_rows(rows):
        fill = [jnp.zeros((1, 128), F32)] * (8 - len(rows))
        return jnp.concatenate(list(rows) + fill, axis=0)

    sbuf_a[me_b] = pack_rows(
        [col(s1[:, 0:128]), col(s1[:, 128:256]), col(s2[:, 0:128]), col(s2[:, 128:256]), col(mask)]
    )
    share_start(sbuf_a, me_b, as_, ar)
    share_wait(sbuf_a, me_b, as_, ar)
    tot = total_of(sbuf_a, NB)
    counted = tot[4:5, :]
    voxels = counted * float(POS)

    def norm_of(sum1, sum2, tile):
        avg = sum1 / voxels
        var = sum2 / voxels - avg * avg
        inv = lax.rsqrt(var + EPS)
        gain = aff_ref[0:1, 128 * tile : 128 * tile + 128]
        bias = aff_ref[1:2, 128 * tile : 128 * tile + 128]
        return avg, var, inv, gain, bias

    n0 = norm_of(tot[0:1], tot[2:3], 0)
    n1 = norm_of(tot[1:2], tot[3:4], 1)

    def forward(y, n):
        normed = (y - n[0]) * n[2]
        pre = n[3] * normed + n[4]
        sig = jax.nn.sigmoid(pre)
        return normed, pre, sig

    def act1(p, carry):
        _, pre, sig = forward(ypos[p][:, 128:256], n1)
        ob[p] = (mask * (pre * sig))
        return carry

    lax.fori_loop(0, POS, act1, 0)
    ob[POS] = zero128

    def to_msg(p, carry):
        msg[p] = jnp.where(low_half, ob[p], pltpu.roll(ob[p + HALF], 64, 1)).astype(BF16)
        return carry

    lax.fori_loop(0, HALF, to_msg, 0)
    ms_c = []
    for d in range(1, NC):
        c = send_to(msg, got.at[me], ms.at[d], mr.at[d], chan_peer(me, d))
        c.start()
        ms_c.append(c)
    got[me] = msg[...]

    def act0(p, carry):
        _, pre, sig = forward(ypos[p][:, 0:128], n0)
        return carry + mask * (pre * sig)

    feat0 = lax.fori_loop(0, POS, act0, zero128)

    for c in ms_c:
        c.wait_recv()

    def unpack(p, carry):
        g = [got[j, p].astype(F32) for j in range(NC)]
        rl = [pltpu.roll(v, 64, 1) for v in g]
        low = jnp.concatenate(
            [jnp.where(low_half, g[0], rl[1]), jnp.where(low_half, g[2], rl[3])], axis=1
        ).astype(BF16)
        apad[padded(p)] = low
        acol[p] = low
        high = jnp.concatenate(
            [jnp.where(low_half, rl[0], g[1]), jnp.where(low_half, rl[2], g[3])], axis=1
        ).astype(BF16)

        @pl.when(p < POS - HALF)
        def _():
            apad[padded(p + HALF)] = high
            acol[p + HALF] = high

        return carry

    lax.fori_loop(0, HALF, unpack, 0)

    def conv(h, carry):
        s1, s2 = carry
        acc = jnp.zeros((SIDE * ROWS, 384), F32)
        for q in range(9):
            dh, dw = divmod(q, 3)
            lhs = apad[pl.ds((h + dh) * 9 + dw, SIDE)].reshape(SIDE * ROWS, 256)
            acc = acc + dot(lhs, wc_ref[q])
        for w in range(SIDE):
            t = acc[w * ROWS : (w + 1) * ROWS]
            y = t[:, 128:256] + prev_t(t[:, 0:128]) + next_t(t[:, 256:384])
            y2[h * SIDE + w] = y
            m = y * mask
            s1 = s1 + m
            s2 = s2 + m * y
        return s1, s2

    s1, s2 = lax.fori_loop(0, SIDE, conv, (zero128, zero128))
    sbuf_b[me_b] = pack_rows([col(s1), col(s2)])
    share_start(sbuf_b, me_b, bs, br)
    at[...] = jnp.transpose(acol[...].reshape(VOX, 256))
    share_wait(sbuf_b, me_b, bs, br)
    totb = total_of(sbuf_b, NB)
    n2 = norm_of(totb[0:1], totb[1:2], 2)

    def act2(p, carry):
        _, pre, sig = forward(y2[p], n2)
        return carry + mask * (pre * sig)

    feat2 = lax.fori_loop(0, POS, act2, zero128)
    feature = (jnp.concatenate([feat0, feat2], axis=1) / float(POS)).astype(BF16)
    lbuf[me] = dot(feature, r_ref[...])
    ls_c = []
    for d in range(1, NC):
        c = send_to(lbuf.at[me], lbuf.at[me], ls.at[d], lr.at[d], chan_peer(me, d))
        c.start()
        ls_c.append(c)
    for c in ls_c:
        c.wait_recv()
    logits = total_of(lbuf, NC)
    cls = lax.broadcasted_iota(jnp.int32, (ROWS, 512), 1)
    row512 = lax.broadcasted_iota(jnp.int32, (ROWS, 512), 0)
    labs = jnp.zeros((ROWS, 512), jnp.int32)
    for i in range(ROWS):
        labs = jnp.where(row512 == i, lab_ref[i // 4, i % 4], labs)
    real = cls < CLASSES
    logits = jnp.where(real, logits, -1e30)
    peak = jnp.max(logits, axis=1, keepdims=True)
    ex = jnp.exp(logits - peak)
    se = jnp.sum(ex, axis=1, keepdims=True)
    logprob = logits - peak - jnp.log(se)
    mask1 = mask[:, 0:1]
    hit = cls == labs
    loss_rows = -jnp.sum(jnp.where(hit, logprob, 0.0), axis=1, keepdims=True) * mask1
    soft = jnp.where(real, jnp.exp(logprob), 0.0)
    dlog = ((soft - hit.astype(F32)) * mask1 / counted[:, 0:1]).astype(BF16)
    dfeat = dot_t(dlog, r_ref[...], 1, 1) / float(POS)
    df0, df2 = dfeat[:, 0:128], dfeat[:, 128:256]

    def back(y, n, dout):
        normed, pre, sig = forward(y, n)
        return dout * mask * sig * (1.0 + pre * (1.0 - sig)), normed

    def back02(p, carry):
        g0, b0, g2, b2 = carry
        d0, m0 = back(ypos[p][:, 0:128], n0, df0)
        d2, m2 = back(y2[p], n2, df2)
        dpre[p] = jnp.concatenate([d0, d2], axis=1)
        return g0 + d0 * m0, b0 + d0, g2 + d2 * m2, b2 + d2

    g0, b0, g2, b2 = lax.fori_loop(0, POS, back02, (zero128,) * 4)
    loss_row = jnp.broadcast_to(jnp.sum(loss_rows, axis=0, keepdims=True), (1, 128))
    sbuf_c[me_b] = pack_rows([col(g0), col(b0), col(g2), col(b2), loss_row])
    share_start(sbuf_c, me_b, cs, cr)
    grr = dot_t(feature, dlog, 0, 0)
    for t in range(4):
        for dst, src, count in ((0, 0, 96), (96, 224, 32), (128, 96, 96), (224, 192, 32)):
            gr[t, src : src + count, :] = grr[dst : dst + count, 128 * t : 128 * t + 128]
    lane32 = lanes_of((32, 128))
    parts = []
    for j in range(8):
        for t in range(4):
            parts.append(
                (gr[t, pl.ds(j, 32, stride=8), :], 0, CLASSES * j + 128 * t,
                 min(128, CLASSES - 128 * t))
            )
    for i, v in enumerate(joined(parts, lane32, 25)):
        g[pl.ds(BULK["readout"] + i, 32, stride=25), :] = v
    for c in ls_c:
        c.wait_send()
    for c in ms_c:
        c.wait_send()
    share_wait(sbuf_c, me_b, cs, cr)
    totc = total_of(sbuf_c, NB)

    def finish(y, n, d, gg, gb):
        normed = (y - n[0]) * n[2]
        return mask * n[3] * n[2] * (d - gb / voxels - normed * gg / voxels)

    def dy2_at(p, carry):
        d = dpre[p]
        v = finish(y2[p], n2, d[:, 128:256], totc[2:3], totc[3:4])
        dypad[padded(p)] = jnp.concatenate([next_t(v), v, prev_t(v)], axis=1).astype(BF16)
        return carry

    lax.fori_loop(0, POS, dy2_at, 0)

    def conv_back(h, carry):
        acc = jnp.zeros((SIDE * ROWS, 256), F32)
        for q in range(9):
            dh, dw = divmod(q, 3)
            lhs = dypad[pl.ds((h + 2 - dh) * 9 + 2 - dw, SIDE)].reshape(SIDE * ROWS, 384)
            acc = acc + dot(lhs, wct_ref[q])
        for t in range(2):
            ynat[t, pl.ds(pl.multiple_of(h * SIDE * ROWS, SIDE * ROWS), SIDE * ROWS), :] = acc[
                :, 128 * t : 128 * t + 128
            ]
        return carry

    lax.fori_loop(0, SIDE, conv_back, 0)

    def to_dm(p, carry):
        for j in range(NC):
            a = ynat[j // 2, pl.ds(pl.multiple_of(p * ROWS, ROWS), ROWS), :]
            b = ynat[j // 2, pl.ds(pl.multiple_of((p + HALF) * ROWS, ROWS), ROWS), :]
            if j % 2 == 0:
                dm[j, p] = jnp.where(low_half, a, pltpu.roll(b, 64, 1))
            else:
                dm[j, p] = jnp.where(low_half, pltpu.roll(a, 64, 1), b)
        return carry

    for t in range(2):
        ynat[t, pl.ds(VOX, ROWS), :] = zero128
    lax.fori_loop(0, HALF, to_dm, 0)
    ds_c = []
    for d in range(1, NC):
        to = lax.rem(me + d, NC)
        c = send_to(dm.at[to], dgot.at[me], ds_.at[d], dr.at[d], chan_peer(me, d))
        c.start()
        ds_c.append(c)
    dgot[me] = dm[me]

    def grad_conv(q, carry):
        dh = q // 3
        dw = q - dh * 3
        rhs = jnp.concatenate(
            [
                dypad[pl.ds((h + 2 - dh) * 9 + 2 - dw, SIDE)].reshape(SIDE * ROWS, 384)
                for h in range(SIDE)
            ],
            axis=0,
        )
        res = dot(at[...], rhs)
        for dt in range(3):
            tap = dt * 9 + q
            for j in range(NC):
                gq[48 * j : 48 * j + 48, :] = res[64 * j : 64 * j + 48, 128 * dt : 128 * dt + 128]
                vn[pl.ds(tap * 48 + 12 * j, 12), :] = res[
                    64 * j + 48 : 64 * j + 60, 128 * dt : 128 * dt + 128
                ]

            def put(i, v, tap=tap):
                g[pl.ds(BULK["spatial"] + tap * 144 + i, 48, stride=3), :] = v

            flatten_96(lambda j: gq[pl.ds(j, 48, stride=4), :], 48, put)
        return carry

    lax.fori_loop(0, 9, grad_conv, 0)
    g[BULK["volume"] : BULK["volume"] + 324, :] = flatten_32(
        lambda j: vn[pl.ds(j, 324, stride=4), :], 324
    )

    def dy0_at(p, carry):
        v = finish(ypos[p][:, 0:128], n0, dpre[p][:, 0:128], totc[0:1], totc[1:2])
        v = v.astype(BF16).astype(F32)
        h, w = p // SIDE, lax.rem(p, SIDE)
        n_h = 3 - (h == 0).astype(jnp.int32) - (h == SIDE - 1).astype(jnp.int32)
        n_w = 3 - (w == 0).astype(jnp.int32) - (w == SIDE - 1).astype(jnp.int32)
        share = v / jnp.maximum(n_t * (n_h * n_w).astype(F32), 1.0)
        box[padded(p)] = share + prev_t(share) + next_t(share)
        ypos[p, :, 0:128] = v
        return carry

    lax.fori_loop(0, POS, dy0_at, 0)

    def dy0_nat(p, carry):
        acc, _ = spread(p)
        v = jnp.where(is_pool, acc * mask, ypos[p][:, 0:128])
        lowv = v - v.astype(BF16).astype(F32)
        dnat[0, pl.ds(p, ROWS, stride=POS), :] = v
        dnat[1, pl.ds(p, ROWS, stride=POS), :] = lowv
        return carry

    lax.fori_loop(0, POS, dy0_nat, 0)

    for tile in range(2):
        gw1_ref[tile] = jnp.zeros((CIN, 128), F32)

    def grad_one(r, width, fold):
        first, off, lanes = window_of(r)
        rhs = jnp.concatenate(
            [dnat[t, pl.ds(r, GPAD, stride=8), :] for t in range(width // 128)], axis=1
        ).astype(BF16)
        for k in range(NC):
            res = dot_t(xg[k, :, first : first + lanes], rhs, 0, 0)[off : off + CB]
            if fold:
                gw1_ref[0, k * CB : (k + 1) * CB, :] += res[:, 0:128] + res[:, 128:256]
            else:
                gw1_ref[1, k * CB : (k + 1) * CB, :] += res

    for r in range(8):
        grad_one(r, 256, True)

    def put_direct(i, v):
        g[pl.ds(BULK["direct"] + i, 208, stride=3), :] = v

    flatten_96(lambda j: gw1_ref[0, pl.ds(j, 208, stride=4), :], 208, put_direct)
    g[BULK["pooled"] : BULK["pooled"] + 208, :] = flatten_32(
        lambda j: gw1_ref[0, pl.ds(j, 208, stride=4), :], 208
    )

    core_i = lax.rem(me_b, 2)
    mate = digit_peer(me_b, 1, 2, 1)
    half_at = pl.multiple_of(core_i * CORE_ROWS, CORE_ROWS)
    mate_at = pl.multiple_of((1 - core_i) * CORE_ROWS, CORE_ROWS)
    core_c = send_to(g.at[pl.ds(mate_at, CORE_ROWS)], gcore, co_s, co_r, mate)
    core_c.start()

    for c in ds_c:
        c.wait_recv()

    def back1(p, carry):
        g1, b1 = carry
        s = dgot[0, p] + dgot[1, p] + dgot[2, p] + dgot[3, p]
        d, m = back(ypos[p][:, 128:256], n1, jnp.where(low_half, s, 0.0))
        dpre[p, :, 0:128] = d
        g1, b1 = g1 + d * m, b1 + d
        q = jnp.minimum(p + HALF, POS - 1)
        live = (p < POS - HALF).astype(F32)
        d, m = back(ypos[q][:, 128:256], n1, jnp.where(low_half, pltpu.roll(s, 64, 1), 0.0) * live)

        @pl.when(p < POS - HALF)
        def _():
            dpre[p + HALF, :, 0:128] = d

        return g1 + d * m, b1 + d

    g1, b1 = lax.fori_loop(0, HALF, back1, (zero128, zero128))
    sbuf_d[me_b] = pack_rows([col(g1), col(b1)])
    share_start(sbuf_d, me_b, es, er)
    for c in ds_c:
        c.wait_send()

    along = ((2, 8), (8, 2))
    firsts = [digit_of(me_b, along[i][0], 4) for i in range(2)]
    seconds = [digit_of(me_b, along[i][1], 4) for i in range(2)]
    core_c.wait()

    def add_core(i, carry):
        at_ = pl.multiple_of(i * 96, 96)
        gcore[pl.ds(at_, 96), :] = gcore[pl.ds(at_, 96), :] + g[
            pl.ds(pl.multiple_of(half_at + at_, 96), 96), :
        ]
        return carry

    lax.fori_loop(0, CORE_ROWS // 96, add_core, 0)

    def first_at(i, digit):
        return pl.ds(pl.multiple_of(i * GROUP_ROWS + digit * FIRST_ROWS, FIRST_ROWS), FIRST_ROWS)

    one_c = []
    for i in range(2):
        for d in range(1, 4):
            c = send_to(
                gcore.at[first_at(i, lax.rem(firsts[i] + d, 4))], r1.at[i, firsts[i]],
                s1s.at[i, d], s1r.at[i, d], digit_peer(me_b, along[i][0], 4, d),
            )
            c.start()
            one_c.append(c)
        r1[i, firsts[i]] = gcore[first_at(i, firsts[i]), :]
    share_wait(sbuf_d, me_b, es, er)
    totd = total_of(sbuf_d, NB)

    def dy1_nat(p, carry):
        v = finish(ypos[p][:, 128:256], n1, dpre[p][:, 0:128], totd[0:1], totd[1:2])
        dnat[0, pl.ds(p, ROWS, stride=POS), :] = v
        return carry

    lax.fori_loop(0, POS, dy1_nat, 0)
    for r in range(8):
        grad_one(r, 128, False)

    lane104, lane26 = lanes_of((104, 128)), lanes_of((26, 128))
    lsend[pl.ds(384, 128), :] = jnp.zeros((128, 128), F32)
    parts = [(gw1_ref[1, pl.ds(j, 104, stride=8), :], 0, 48 * j, 48) for j in range(8)]
    for i, v in enumerate(joined(parts, lane104, 3)):
        lsend[pl.ds(LATE["squeeze"] + i, 104, stride=3), :] = v
    parts = [(gw1_ref[1, pl.ds(j, 26, stride=32), :], 48, 12 * j, 12) for j in range(32)]
    for i, v in enumerate(joined(parts, lane26, 3)):
        lsend[pl.ds(LATE["shrink"] + i, 26, stride=3), :] = v

    def late_at(i):
        return pl.ds(pl.multiple_of(i * LATE_ROWS, LATE_ROWS), LATE_ROWS)

    def late_copy(d):
        to = lax.rem(me_b + d, NB)
        return send_to(
            lsend.at[late_at(to)], lgot.at[me_b], fs.at[d], fr.at[d], batch_peer(me_b, d)
        )

    def late_start(d, carry):
        late_copy(d).start()
        return carry

    def late_wait(d, carry):
        late_copy(d).wait()
        return carry

    lax.fori_loop(1, NB, late_start, 0)
    lgot[me_b] = lsend[late_at(me_b), :]

    for c in one_c:
        c.wait()
    two_c = []
    for i in range(2):
        r1[i, 0] = total_of(r1.at[i], 4)
        for d in range(1, 4):
            to = lax.rem(seconds[i] + d, 4)
            c = send_to(
                r1.at[i, 0, pl.ds(pl.multiple_of(to * LAST_ROWS, LAST_ROWS), LAST_ROWS)],
                r2.at[i, seconds[i]], s2s.at[i, d], s2r.at[i, d],
                digit_peer(me_b, along[i][1], 4, d),
            )
            c.start()
            two_c.append(c)
        r2[i, seconds[i]] = r1[
            i, 0, pl.ds(pl.multiple_of(seconds[i] * LAST_ROWS, LAST_ROWS), LAST_ROWS), :
        ]
    for c in two_c:
        c.wait()

    all_c = []
    for i in range(2):
        at_ = pl.ds(
            pl.multiple_of(
                half_at + i * GROUP_ROWS + firsts[i] * FIRST_ROWS + seconds[i] * LAST_ROWS,
                LAST_ROWS,
            ),
            LAST_ROWS,
        )
        gb_ref[at_, :] = total_of(r2.at[i], 4)
        for d in range(1, 4):
            c = send_to(
                gb_ref.at[at_], gb_ref.at[at_], g1s.at[i, d], g1r.at[i, d],
                digit_peer(me_b, along[i][1], 4, d),
            )
            c.start()
            all_c.append(c)

    lax.fori_loop(1, NB, late_wait, 0)
    late_ref[me_b] = total_of(lgot, NB)
    share_start(late_ref, me_b, hs, hr)

    for c in all_c:
        c.wait()
    more_c = []
    for i in range(2):
        at_ = pl.ds(
            pl.multiple_of(half_at + i * GROUP_ROWS + firsts[i] * FIRST_ROWS, FIRST_ROWS),
            FIRST_ROWS,
        )
        for d in range(1, 4):
            c = send_to(
                gb_ref.at[at_], gb_ref.at[at_], g2s.at[i, d], g2r.at[i, d],
                digit_peer(me_b, along[i][0], 4, d),
            )
            c.start()
            more_c.append(c)

    fix = voxels / (voxels - 1.0)
    for tile, n, gg, gb in (
        (0, n0, totc[0:1], totc[1:2]),
        (1, n1, totd[0:1], totd[1:2]),
        (2, n2, totc[2:3], totc[3:4]),
    ):
        st_ref[:, 128 * tile : 128 * tile + 128] = pack_rows([gg, gb, n[0], n[1] * fix])
    sc_ref[...] = pack_rows([totc[4:5], counted])

    for c in more_c:
        c.wait()
    last_c = send_to(
        gb_ref.at[pl.ds(half_at, CORE_ROWS)], gb_ref.at[pl.ds(half_at, CORE_ROWS)], g3s, g3r, mate
    )
    last_c.start()
    share_wait(late_ref, me_b, hs, hr)
    last_c.wait()


def core(x, lengths, labels, weights, affine):
    vm = pl.BlockSpec(memory_space=pltpu.VMEM)
    sm = pl.BlockSpec(memory_space=pltpu.SMEM)
    hbm = pl.BlockSpec(memory_space=pl.ANY)
    dma = pltpu.SemaphoreType.DMA
    vmem = pltpu.VMEM
    return pl.pallas_call(
        core_kernel,
        out_shape=(
            jax.ShapeDtypeStruct((2 * CORE_ROWS, 128), F32),
            jax.ShapeDtypeStruct((NB, LATE_ROWS, 128), F32),
            jax.ShapeDtypeStruct((8, 384), F32),
            jax.ShapeDtypeStruct((8, 128), F32),
        ),
        in_specs=[hbm, sm, sm] + [hbm] * 7 + [vm],
        out_specs=(vm,) * 4,
        scratch_shapes=[
            vmem((1, 326144), BF16),
            *[vmem((FLAT[n], 128), F32) for n in NAMES],
            vmem((2, CIN, 128), F32),
            vmem((CIN, 128), F32),
            vmem((R1, 128), F32),
            vmem((1304, 128), F32),
            vmem((4, 256, 128), F32),
            vmem((9, 256, 384), BF16),
            vmem((9, 384, 256), BF16),
            vmem((256, 512), BF16),
            vmem((8, 384), F32),
            vmem((13 * GPAD, 128), F32),
            vmem((NC, GPAD, GW), BF16),
            vmem((8, NC, 384, 256), BF16),
            vmem((2, 8 * GPAD, 128), F32),
            vmem((POS, ROWS, 256), F32),
            vmem((81, ROWS, 128), F32),
            vmem((POS + 1, ROWS, 128), F32),
            vmem((HALF, ROWS, 128), BF16),
            vmem((NC, HALF, ROWS, 128), BF16),
            vmem((81, ROWS, 256), BF16),
            vmem((POS, ROWS, 256), BF16),
            vmem((256, VOX), BF16),
            vmem((POS, ROWS, 128), F32),
            vmem((POS, ROWS, 256), F32),
            vmem((81, ROWS, 384), BF16),
            vmem((NC, HALF, ROWS, 128), F32),
            vmem((NC, HALF, ROWS, 128), F32),
            vmem((2, 8 * GPAD, 128), F32),
            vmem((2, CIN, 128), F32),
            vmem((R1, 128), F32),
            vmem((4, 256, 128), F32),
            vmem((2 * CORE_ROWS, 128), F32),
            vmem((CORE_ROWS, 128), F32),
            vmem((2, 4, FIRST_ROWS, 128), F32),
            vmem((2, 4, LAST_ROWS, 128), F32),
            vmem((NB * LATE_ROWS, 128), F32),
            vmem((NB, LATE_ROWS, 128), F32),
            vmem((NC, ROWS, 512), F32),
            *[vmem((NB, 8, 128), F32)] * 4,
            dma((4,)), dma((7,)), dma((6,)), dma((6,)),
            *[dma((NC,))] * 6,
            *[dma((NB,))] * 12,
            dma, dma,
            *[dma((2, 4))] * 8,
            dma, dma,
        ],
        compiler_params=pltpu.CompilerParams(
            collective_id=0, has_side_effects=True, vmem_limit_bytes=58 << 20
        ),
        name="block",
    )(x, lengths, labels, *weights, affine)


def unlanes(tiles):
    t0, t1, t2 = tiles
    lane = lanes_of(t0.shape)
    parts = [(t0, 0, 0, 96), (t1, 0, 96, 60), (t0, 96, 156, 32), (t2, 0, 188, 128)]
    return joined(parts, lane, 3)


def adam_kernel(*refs):
    gb, late, st, sc, running = refs[0:5]
    w_in, m_in, v_in = refs[5:13], refs[13:21], refs[21:29]
    m_out, v_out, w_out = refs[29:37], refs[37:45], refs[45:53]
    run_out, loss_out, count_out, copies_out = refs[53:57]
    wb, mb, vb = refs[57:64], refs[64:71], refs[71:78]
    cb, insem, outsem, csem = refs[78:82]
    rates = step_rates()
    order = (2, 6, 0, 1, 4, 5, 3)
    ins = {}
    for i in order:
        for kind, (src, dst) in enumerate(((w_in[i], wb[i]), (m_in[i], mb[i]), (v_in[i], vb[i]))):
            c = pltpu.make_async_copy(src, dst, insem.at[i, kind])
            c.start()
            ins[i, kind] = c

    starts = []
    total = 0
    for name in NAMES:
        starts.append(total * 128)
        total += FLAT[name]
    outs = []
    for i in order:
        name = NAMES[i]
        rows = FLAT[name]
        for kind in range(3):
            ins[i, kind].wait()
        bulk = name in BULK

        def step(at, count, i=i, name=name, bulk=bulk):
            if bulk:
                grad = gb[pl.ds(BULK[name] + at, count), :]
            else:
                grad = late[pl.ds(LATE[name] + at, count), :]
            rows_ = pl.ds(at, count)
            m, v, w = adamw(wb[i][rows_, :], mb[i][rows_, :], vb[i][rows_, :], grad, rates[i])
            mb[i][rows_, :] = m
            vb[i][rows_, :] = v
            wb[i][rows_, :] = w
            cb[:, pl.ds(pl.multiple_of(starts[i] + at * 128, 128), count * 128)] = w.reshape(
                1, count * 128
            ).astype(BF16)

        block = 48 if bulk else 24
        loops = rows // block

        def body(j, carry, step=step, block=block):
            step(pl.multiple_of(j * block, block), block)
            return carry

        lax.fori_loop(0, loops, body, 0)
        at, rest = loops * block, rows - loops * block
        if rest // 8:
            step(at, rest // 8 * 8)
        if rest % 8:
            step(at + rest // 8 * 8, rest % 8)
        for kind, (src, dst) in enumerate(((wb[i], w_out[i]), (mb[i], m_out[i]), (vb[i], v_out[i]))):
            c = pltpu.make_async_copy(src, dst, outsem.at[i, kind])
            c.start()
            outs.append(c)
        at = pl.ds(starts[i], rows * 128)
        c = pltpu.make_async_copy(cb.at[:, at], copies_out.at[:, at], csem.at[i])
        c.start()
        outs.append(c)

    tiles = [st[:, 128 * t : 128 * t + 128] for t in range(3)]
    for t, v in enumerate(unlanes(tiles)):
        width = min(128, 316 - 128 * t)
        at = slice(128 * t, 128 * t + width)
        v = v[:, 0:width]
        m, s, w = adamw(w_in[7][:, at], m_in[7][:, at], v_in[7][:, at], v[0:2], rates[7])
        m_out[7][:, at] = m
        v_out[7][:, at] = s
        w_out[7][:, at] = w
        run_out[:, at] = MOMENTUM * running[:, at] + (1.0 - MOMENTUM) * v[2:4]
    loss_out[...] = sc[0:1, 0:1]
    count_out[...] = sc[1:2, 0:1]
    for c in outs:
        c.wait()


def adam(gb, late, st, sc, running, masters, firsts, seconds):
    vm = pl.BlockSpec(memory_space=pltpu.VMEM)
    hbm = pl.BlockSpec(memory_space=pl.ANY)
    dma = pltpu.SemaphoreType.DMA
    flats = [jax.ShapeDtypeStruct((FLAT[n], 128), F32) for n in NAMES]
    small = jax.ShapeDtypeStruct((2, 316), F32)
    total = sum(FLAT[n] for n in NAMES) * 128
    one = jax.ShapeDtypeStruct((1, 1), F32)
    specs = [hbm] * 7 + [vm]
    buffers = [pltpu.VMEM((FLAT[n], 128), F32) for n in NAMES]
    return pl.pallas_call(
        adam_kernel,
        out_shape=[*(flats + [small]) * 3, small, one, one, jax.ShapeDtypeStruct((1, total), BF16)],
        in_specs=[vm] * 5 + specs * 3,
        out_specs=[*specs * 3, vm, vm, vm, hbm],
        scratch_shapes=[
            *buffers * 3, pltpu.VMEM((1, total), BF16), dma((7, 3)), dma((7, 3)), dma((7,)),
        ],
        compiler_params=pltpu.CompilerParams(vmem_limit_bytes=40 << 20),
        name="adamw",
    )(gb, late, st, sc, running, *masters, *firsts, *seconds)


def per_device(
    features, lengths, labels, direct, squeeze, spatial, shrink, volume, pooled, readout, affine,
    first_direct, first_squeeze, first_spatial, first_shrink, first_volume, first_pooled,
    first_readout, first_affine, second_direct, second_squeeze, second_spatial, second_shrink,
    second_volume, second_pooled, second_readout, second_affine, running,
):
    masters = [direct, squeeze, spatial, shrink, volume, pooled, readout, affine]
    firsts = [
        first_direct, first_squeeze, first_spatial, first_shrink, first_volume, first_pooled,
        first_readout, first_affine,
    ]
    seconds = [
        second_direct, second_squeeze, second_spatial, second_shrink, second_volume,
        second_pooled, second_readout, second_affine,
    ]
    def rows(flat):
        return flat.reshape(-1, 128)

    masters, firsts, seconds = (
        [rows(a) for a in group[:7]] + [group[7]] for group in (masters, firsts, seconds)
    )
    gb, late, st, sc = core(features, lengths, labels, masters[:7], affine)
    out = adam(gb, late.reshape(NB * LATE_ROWS, 128), st, sc, running, masters, firsts, seconds)
    flat_out = [a if i % 8 == 7 else a.reshape(1, -1) for i, a in enumerate(out[:24])]
    return (*flat_out, out[24], out[25].reshape(()), out[26].reshape(()), out[27])


def solution(mesh):
    flat = P("chan", None)
    wide = P(None, "chan")
    weights = (flat,) * 7 + (wide,)
    return jax.shard_map(
        per_device,
        mesh=mesh,
        in_specs=(P("chan", "batch"), P("batch"), P("batch", None)) + weights * 3 + (wide,),
        out_specs=weights * 3 + (wide, P(), P(), flat),
        check_vma=False,
    )
```

```python
import math
from functools import partial

import jax
import jax.numpy as jnp
from jax import lax
from jax.experimental import pallas as pl
from jax.experimental.pallas import tpu as pltpu
from jax.sharding import PartitionSpec as P

CIN = 832
B0 = 384
R1 = 192
O1 = 384
R2 = 48
O2 = 128
B3 = 128
CLASSES = 400
SIDE = 7
STEP = 5
NC = 4
NB = 32
POS = SIDE * SIDE
ROWS = 32
VOX = POS * ROWS
GROUPS = VOX // 8
GPAD = 208
CB = CIN // NC
GW = 8 * CB
HALF = 25
SHIFT = 112
W1_ROWS = 448
TAPS = 27
FLAT = {"direct": 624, "squeeze": 312, "spatial": 3888, "shrink": 78, "volume": 324, "pooled": 208,
        "readout": 800}
NAMES = ("direct", "squeeze", "spatial", "shrink", "volume", "pooled", "readout")
BULK = {"spatial": 0, "volume": 3888, "direct": 4216, "pooled": 4840, "readout": 5048}
NARROW = ("shrink", "volume")
LATE = {"squeeze": 0, "shrink": 312}
CHUNKS = ((0, 64), (4096, 32))
BULK_ROWS = 6144
LATE_ROWS = 16
ADAM_ROWS = 648

EPS = 1e-05
BETA_ONE = 0.5
BETA_TWO = 0.5
DECAY = 0.01
MOMENTUM = 0.99

MESH = pl.DeviceIdType.MESH
F32 = jnp.float32
BF16 = jnp.bfloat16


def step_rates():
    return [
        1.5 / math.sqrt(CIN),
        1.5 / math.sqrt(CIN),
        1.5 / math.sqrt(27 * R1),
        1.5 / math.sqrt(CIN),
        1.5 / math.sqrt(27 * R2),
        1.5 / math.sqrt(CIN),
        0.2,
        0.3,
    ]


def adamw(weight, moment_one, moment_two, gradient, step_rate):
    first_new = BETA_ONE * moment_one + (1.0 - BETA_ONE) * gradient
    second_new = BETA_TWO * moment_two + (1.0 - BETA_TWO) * (gradient * gradient)
    scale_one = step_rate / (1.0 - BETA_ONE**STEP)
    scale_two = 1.0 / (1.0 - BETA_TWO**STEP)
    weight_new = weight * (1.0 - step_rate * DECAY) - scale_one * first_new / (
        jnp.sqrt(second_new * scale_two) + 1e-08
    )
    return (first_new, second_new, weight_new)


def window_of(r):
    start = CB * r
    tile, offset = divmod(start, 128)
    lanes = 256 if offset + CB <= 256 else 384
    return tile * 128, offset, lanes


def dot(a, b):
    return jnp.dot(a, b, preferred_element_type=F32)


def dot_t(a, b, ca, cb):
    return lax.dot_general(a, b, (((ca,), (cb,)), ((), ())), preferred_element_type=F32)


def send_to(src, dst, send, recv, target):
    return pltpu.make_async_remote_copy(
        src_ref=src, dst_ref=dst, send_sem=send, recv_sem=recv, device_id=target,
        device_id_type=MESH,
    )


def batch_peer(me, d):
    return {"batch": lax.rem(me + d, NB)}


def chan_peer(me, d):
    return {"chan": lax.rem(me + d, NC)}


def share_start(buf, me, send, recv):
    def one(d, carry):
        send_to(buf.at[me], buf.at[me], send, recv, batch_peer(me, d)).start()
        return carry

    lax.fori_loop(1, NB, one, 0)


def share_copy(buf, me, send, recv):
    others = buf.at[pl.ds(0, NB - 1)]
    return send_to(others, others, send, recv, batch_peer(me, 1))


def share_wait(buf, me, send, recv):
    share_copy(buf, me, send, recv).wait_recv()


def share_sent(buf, me, send, recv):
    share_copy(buf, me, send, recv).wait_send()


def digit_of(me, stride, size):
    return lax.rem(me // stride, size)


def digit_peer(me, stride, size, d):
    digit = digit_of(me, stride, size)
    return {"batch": me + stride * (lax.rem(digit + d, size) - digit)}


def piece(tiles, start, width, dest, lane):
    tile, off = divmod(start, 128)
    v = tiles[tile]
    if off + width > 128:
        v = jnp.where(lane >= off, v, tiles[tile + 1])
    shift = (dest - off) % 128
    return pltpu.roll(v, shift, 1) if shift else v


def joined(parts, lane, count):
    out = []
    moved = []
    for value, src, start, width in parts:
        shift = (start - src) % 128
        moved.append((pltpu.roll(value, shift, 1) if shift else value, start, width))
    for i in range(count):
        acc = None
        for value, start, width in moved:
            lo, hi = max(0, start - 128 * i), min(128, start + width - 128 * i)
            if lo < hi:
                acc = value if acc is None else jnp.where(lane >= lo, value, acc)
        out.append(acc)
    return out


def lanes_of(v):
    return lax.broadcasted_iota(jnp.int32, v, 1)


def prepare_w1(flat, wn, wk, w1p):
    lane = lanes_of((208, 128))
    tiles = [flat["direct"][pl.ds(i, 208, stride=3), :] for i in range(3)]
    pool = flat["pooled"][...]
    for j in range(4):
        v = jnp.where(
            lane < 96, piece(tiles, 96 * j, 96, 0, lane), piece([pool], 32 * j, 32, 96, lane)
        )
        wn[0, pl.ds(j, 208, stride=4), :] = v
    lane = lanes_of((104, 128))
    tiles = [flat["squeeze"][pl.ds(i, 104, stride=3), :] for i in range(3)]
    for j in range(8):
        wn[1, pl.ds(j, 104, stride=8), :] = piece(tiles, 48 * j, 48, 0, lane)
    lane = lanes_of((26, 128))
    tiles = [flat["shrink"][pl.ds(i, 26, stride=3), :] for i in range(3)]
    for j in range(32):
        wk[pl.ds(j, 26, stride=32), :] = piece(tiles, 12 * j, 12, 48, lane)
    lane = lanes_of((CB, 128))
    for k in range(NC):
        rows = slice(k * CB, (k + 1) * CB)
        second = jnp.where(lane < 48, wn[1, rows, :], jnp.where(lane < 60, wk[rows, :], 0.0))
        both = jnp.concatenate([wn[0, rows, :], second], axis=1).astype(BF16)
        w1p[k, 0:SHIFT, :] = jnp.zeros((SHIFT, 256), BF16)
        w1p[k, SHIFT : SHIFT + CB, :] = both
        w1p[k, SHIFT + CB : W1_ROWS, :] = jnp.zeros((W1_ROWS - SHIFT - CB, 256), BF16)


def prepare_conv(flat, tb, vn, wc, wct):
    lane = lanes_of((324, 128))
    for j in range(4):
        v = piece([flat["volume"][...]], 32 * j, 32, 96, lane)
        vn[pl.ds(j, 324, stride=4), :] = jnp.where(lane >= 96, v, 0.0)
    vn[pl.ds(1296, 8), :] = jnp.zeros((8, 128), F32)
    lane48 = lanes_of((48, 128))
    row16 = lax.broadcasted_iota(jnp.int32, (16, 128), 0)

    def one(q, carry):
        for dt in range(3):
            tap = dt * 9 + q
            tiles = [
                flat["spatial"][pl.ds(tap * 144 + i, 48, stride=3), :] for i in range(3)
            ]
            for j in range(4):
                v = piece(tiles, 96 * j, 96, 0, lane48)
                tb[pl.ds(j, 48, stride=4), :] = jnp.where(lane48 < 96, v, 0.0)
            for j in range(NC):
                at = slice(128 * dt, 128 * dt + 128)
                wc[q, 64 * j : 64 * j + 48, at] = tb[48 * j : 48 * j + 48, :].astype(BF16)
                v = vn[pl.ds(tap * 48 + 12 * j, 16), :]
                wc[q, 64 * j + 48 : 64 * j + 64, at] = jnp.where(row16 < 12, v, 0.0).astype(BF16)
        wct[q] = jnp.transpose(wc[q])
        return carry

    lax.fori_loop(0, 9, one, 0)


def prepare_readout(flat, rn, rp):
    lane = lanes_of((32, 128))
    tiles = [flat["readout"][pl.ds(i, 32, stride=25), :] for i in range(25)]
    for t in range(4):
        width = min(128, CLASSES - 128 * t)
        for j in range(8):
            v = piece(tiles, CLASSES * j + 128 * t, width, 0, lane)
            rn[t, pl.ds(j, 32, stride=8), :] = v if width == 128 else jnp.where(lane < width, v, 0.0)
        at = slice(128 * t, 128 * t + 128)
        for dst, src, count in ((0, 0, 96), (96, 224, 32), (128, 96, 96), (224, 192, 32)):
            rp[dst : dst + count, at] = rn[t, src : src + count, :].astype(BF16)


def prepare_affine(aff, out):
    a = [aff[:, 0:128], aff[:, 128:256]]
    a.append(jnp.concatenate([aff[:, 256:316], jnp.zeros((2, 68), F32)], axis=1))
    lane = lanes_of((2, 128))
    t0 = jnp.where(lane < 96, a[0], piece(a, 156, 32, 96, lane))
    t1 = jnp.where(lane < 60, piece(a, 96, 60, 0, lane), 0.0)
    t2 = piece(a, 188, 128, 0, lane)
    for i, t in enumerate((t0, t1, t2)):
        out[0:2, 128 * i : 128 * i + 128] = t


def flatten_96(src, rows, put):
    lane = lanes_of((rows, 128))
    for i, v in enumerate(joined([(src(j), 0, 96 * j, 96) for j in range(4)], lane, 3)):
        put(i, v)


def flatten_32(src, rows):
    lane = lanes_of((rows, 128))
    return joined([(src(j), 96, 32 * j, 32) for j in range(4)], lane, 1)[0]


def total_of(buf, count):
    acc = buf[0]
    for slot in range(1, count):
        acc = acc + buf[slot]
    return acc


def core_kernel(
    x_hbm, len_ref, lab_ref, direct_hbm, squeeze_hbm, spatial_hbm, shrink_hbm, volume_hbm,
    pooled_hbm, readout_hbm, affine_ref,
    gb_ref, late_ref, st_ref, sc_ref,
    x_ref, n_shrink, n_volume,
    wn, wk, tb, vn, rn, wc_ref, wct_ref, r_ref, aff_ref,
    xf, xg, w1p, ynat, ypos, box, ob, got, apad, acol, at, y2, dpre, dypad, dm, dgot, dnat,
    gw1_ref, gq, gr, g, gca, gcb, r1a, r1b, r2a, r2b, lsend, lgot,
    lbuf, sbuf_a, sbuf_b, sbuf_c, sbuf_d,
    xin, win, xs, xr, ms, mr, ls, lr, ds_, dr,
    as_, ar, bs, br, cs, cr, es, er, fs, fr, hs, hr,
    co_s, co_r, s1s, s1r, s2s, s2r, g1s, g1r, g2s, g2r, g3s, g3r,
):
    me_b = lax.axis_index("batch")
    me = lax.axis_index("chan")

    barrier = pltpu.get_barrier_semaphore()

    cuts = [0, 91 * 1024, 182 * 1024, 250 * 1024, 326144]
    x_in = []
    for i in range(4):
        at_ = pl.ds(cuts[i], cuts[i + 1] - cuts[i])
        c = pltpu.make_async_copy(x_hbm.at[:, at_], x_ref.at[:, at_], xin.at[i])
        c.start()
        x_in.append(c)
    flat = {n: g.at[at_ : at_ + FLAT[n]] for n, at_ in BULK.items()}
    flat.update({n: lsend.at[at_ : at_ + FLAT[n]] for n, at_ in LATE.items()})
    w_in = []
    for i, (src, name) in enumerate(
        zip(
            (direct_hbm, squeeze_hbm, spatial_hbm, shrink_hbm, volume_hbm, pooled_hbm, readout_hbm),
            NAMES,
        )
    ):
        dst = {"shrink": n_shrink, "volume": n_volume}.get(name, flat[name])
        c = pltpu.make_async_copy(src, dst, win.at[i])
        c.start()
        w_in.append(c)

    def greet(d, carry):
        pl.semaphore_signal(barrier, inc=1, device_id=batch_peer(me_b, d), device_id_type=MESH)
        return carry

    lax.fori_loop(1, NB, greet, 0)
    for d in range(1, NC):
        pl.semaphore_signal(barrier, inc=1, device_id=chan_peer(me, d), device_id_type=MESH)

    def flat_rows(i, carry):
        v = x_ref[:, pl.ds(pl.multiple_of(i * 1024, 1024), 1024)].astype(F32)
        xf[pl.ds(pl.multiple_of(i * 8, 8), 8), :] = v.reshape(8, 128)
        return carry

    right, left = chan_peer(me, 1), chan_peer(me, NC - 1)
    left_i, right_i = lax.rem(me + NC - 1, NC), lax.rem(me + 1, NC)
    split = 112

    def part(who, low):
        return xg.at[who, 0:split] if low else xg.at[who, split:GPAD]

    hops = [
        send_to(part(me, low), part(me, low), xs.at[i], xr.at[i], to)
        for i, (low, to) in enumerate([(True, right), (True, left), (False, right), (False, left)])
    ]
    xf[pl.ds(2548, 2704 - 2548), :] = jnp.zeros((2704 - 2548, 128), F32)
    for i in range(2):
        x_in[i].wait()
        lax.fori_loop(91 * i, 91 * i + 91, flat_rows, 0, unroll=7)
    for i in range(13):
        xg[me, 0:split, 128 * i : 128 * i + 128] = xf[pl.ds(i, split, stride=13), :].astype(BF16)
    pl.semaphore_wait(barrier, NB - 1 + NC - 1)
    hops[0].start()
    hops[1].start()
    x_in[2].wait()
    lax.fori_loop(182, 250, flat_rows, 0, unroll=4)
    x_in[3].wait()
    lax.fori_loop(250, 318, flat_rows, 0, unroll=4)
    xf[pl.ds(2544, 4), :] = x_ref[:, 318 * 1024 : 318 * 1024 + 512].astype(F32).reshape(4, 128)
    for i in range(13):
        xg[me, split:GPAD, 128 * i : 128 * i + 128] = xf[
            pl.ds(13 * split + i, GPAD - split, stride=13), :
        ].astype(BF16)
    hops[2].start()
    hops[3].start()

    rowi = lax.broadcasted_iota(jnp.int32, (ROWS, 128), 0)
    lane = lax.broadcasted_iota(jnp.int32, (ROWS, 128), 1)
    clip = rowi // 4
    step = rowi - clip * 4
    lens = jnp.zeros((ROWS, 128), jnp.int32)
    for c in range(8):
        lens = jnp.where(clip == c, len_ref[c], lens)
    mask = (step < lens).astype(F32)
    has_prev = (step > 0).astype(F32)
    has_next = (step < 3).astype(F32)

    def prev_t(v):
        return pltpu.roll(v, 1, 0) * has_prev

    def next_t(v):
        return pltpu.roll(v, ROWS - 1, 0) * has_next

    n_t = mask + prev_t(mask) + next_t(mask)
    is_pool = lane >= 96
    low_half = lane < 64

    for c in w_in:
        c.wait()
    for src, dst in ((n_shrink, flat["shrink"]), (n_volume, flat["volume"])):
        count = dst.shape[0]
        whole = count // 8 * 8
        dst[0:whole, :] = src[:, 0 : whole * 128].reshape(whole, 128)
        dst[whole:count, :] = src[:, whole * 128 : count * 128].reshape(count - whole, 128)
    prepare_w1(flat, wn, wk, w1p)
    prepare_affine(affine_ref, aff_ref)
    prepare_readout(flat, rn, r_ref)

    def zero_pad(i, carry):
        apad[i] = jnp.zeros((ROWS, 256), BF16)
        dypad[i] = jnp.zeros((ROWS, 384), BF16)
        box[i] = jnp.zeros((ROWS, 128), F32)
        return carry

    lax.fori_loop(0, 81, zero_pad, 0)
    dnat[...] = jnp.zeros_like(dnat)
    prepare_conv(flat, tb, vn, wc_ref, wct_ref)

    hops[0].wait_recv()
    f0 = send_to(part(left_i, True), part(left_i, True), xs.at[4], xr.at[4], right)
    f0.start()
    hops[3].wait_recv()
    f1 = send_to(part(right_i, False), part(right_i, False), xs.at[5], xr.at[5], left)
    f1.start()
    hops[1].wait_recv()
    hops[2].wait_recv()
    f0.wait()
    f1.wait()
    for c in hops:
        c.wait_send()

    for r in range(8):
        first, off, lanes = window_of(r)
        acc = jnp.zeros((GPAD, 256), F32)
        for k in range(NC):
            acc = acc + dot(xg[k, :, first : first + lanes], w1p[k, SHIFT - off : SHIFT - off + lanes, :])
        ynat[0, pl.ds(r, GPAD, stride=8), :] = acc[:, 0:128]
        ynat[1, pl.ds(r, GPAD, stride=8), :] = acc[:, 128:256]

    def padded(p):
        return (p // SIDE + 1) * 9 + lax.rem(p, SIDE) + 1

    def to_pos(p, carry):
        v = ynat[0, pl.ds(p, ROWS, stride=POS), :]
        ypos[p, :, 0:128] = v
        ypos[p, :, 128:256] = ynat[1, pl.ds(p, ROWS, stride=POS), :]
        mz = v * mask
        box[padded(p)] = mz + prev_t(mz) + next_t(mz)
        return carry

    lax.fori_loop(0, POS, to_pos, 0)

    def spread(p):
        h, w = p // SIDE, lax.rem(p, SIDE)
        acc = jnp.zeros((ROWS, 128), F32)
        for dh in range(3):
            for dw in range(3):
                acc = acc + box[(h + dh) * 9 + w + dw]
        n_h = 3 - (h == 0).astype(jnp.int32) - (h == SIDE - 1).astype(jnp.int32)
        n_w = 3 - (w == 0).astype(jnp.int32) - (w == SIDE - 1).astype(jnp.int32)
        return acc, (n_h * n_w).astype(F32)

    def pool(p, carry):
        s1, s2 = carry
        acc, n = spread(p)
        v = ypos[p]
        v0 = jnp.where(is_pool, acc / jnp.maximum(n_t * n, 1.0), v[:, 0:128])
        v1 = v[:, 128:256]
        ypos[p] = jnp.concatenate([v0, v1], axis=1)
        m0, m1 = v0 * mask, v1 * mask
        return (
            s1 + jnp.concatenate([m0, m1], axis=1),
            s2 + jnp.concatenate([m0 * v0, m1 * v1], axis=1),
        )

    zero256 = jnp.zeros((ROWS, 256), F32)
    zero128 = jnp.zeros((ROWS, 128), F32)
    s1, s2 = lax.fori_loop(0, POS, pool, (zero256, zero256))

    def col(v):
        return jnp.sum(v, axis=0, keepdims=True)

    def pack_rows(rows, count=8):
        fill = [jnp.zeros((1, 128), F32)] * (count - len(rows))
        return jnp.concatenate(list(rows) + fill, axis=0)

    sbuf_a[me_b] = pack_rows(
        [col(s1[:, 0:128]), col(s1[:, 128:256]), col(s2[:, 0:128]), col(s2[:, 128:256]), col(mask)]
    )
    share_start(sbuf_a, me_b, as_, ar)
    share_wait(sbuf_a, me_b, as_, ar)
    tot = total_of(sbuf_a, NB)
    counted = tot[4:5, :]
    voxels = counted * float(POS)

    def norm_of(sum1, sum2, tile):
        avg = sum1 / voxels
        var = sum2 / voxels - avg * avg
        inv = lax.rsqrt(var + EPS)
        gain = aff_ref[0:1, 128 * tile : 128 * tile + 128]
        bias = aff_ref[1:2, 128 * tile : 128 * tile + 128]
        return avg, var, inv, gain, bias

    n0 = norm_of(tot[0:1], tot[2:3], 0)
    n1 = norm_of(tot[1:2], tot[3:4], 1)

    def forward(y, n):
        normed = (y - n[0]) * n[2]
        pre = n[3] * normed + n[4]
        sig = jax.nn.sigmoid(pre)
        return normed, pre, sig

    def act1(p, carry):
        _, pre, sig = forward(ypos[p][:, 128:256], n1)
        ob[p] = (mask * (pre * sig))
        return carry

    lax.fori_loop(0, POS, act1, 0)
    ob[POS] = zero128

    def to_msg(p, carry):
        got[me, p] = jnp.where(low_half, ob[p], pltpu.roll(ob[p + HALF], 64, 1)).astype(BF16)
        return carry

    lax.fori_loop(0, HALF, to_msg, 0)
    near = 12

    def half(who, low):
        return got.at[who, 0:near] if low else got.at[who, near:HALF]

    ms_c = []
    for i, (low, to) in enumerate([(True, right), (False, left), (False, right), (True, left)]):
        c = send_to(half(me, low), half(me, low), ms.at[i], mr.at[i], to)
        c.start()
        ms_c.append(c)

    def act0(p, carry):
        _, pre, sig = forward(ypos[p][:, 0:128], n0)
        return carry + mask * (pre * sig)

    feat0 = lax.fori_loop(0, POS, act0, zero128)

    for i, (who, low, to) in enumerate([(left_i, True, right), (right_i, False, left)]):
        ms_c[i].wait_recv()
        c = send_to(half(who, low), half(who, low), ms.at[4 + i], mr.at[4 + i], to)
        c.start()
        ms_c.append(c)
    for c in ms_c[2:]:
        c.wait_recv()

    def unpack(p, carry):
        g = [got[j, p].astype(F32) for j in range(NC)]
        rl = [pltpu.roll(v, 64, 1) for v in g]
        low = jnp.concatenate(
            [jnp.where(low_half, g[0], rl[1]), jnp.where(low_half, g[2], rl[3])], axis=1
        ).astype(BF16)
        apad[padded(p)] = low
        acol[p] = low
        high = jnp.concatenate(
            [jnp.where(low_half, rl[0], g[1]), jnp.where(low_half, rl[2], g[3])], axis=1
        ).astype(BF16)

        @pl.when(p < POS - HALF)
        def _():
            apad[padded(p + HALF)] = high
            acol[p + HALF] = high

        return carry

    lax.fori_loop(0, HALF, unpack, 0)

    def conv(h, carry):
        s1, s2 = carry
        acc = jnp.zeros((SIDE * ROWS, 384), F32)
        for q in range(9):
            dh, dw = divmod(q, 3)
            lhs = apad[pl.ds((h + dh) * 9 + dw, SIDE)].reshape(SIDE * ROWS, 256)
            acc = acc + dot(lhs, wc_ref[q])
        for w in range(SIDE):
            t = acc[w * ROWS : (w + 1) * ROWS]
            y = t[:, 128:256] + prev_t(t[:, 0:128]) + next_t(t[:, 256:384])
            y2[h * SIDE + w] = y
            m = y * mask
            s1 = s1 + m
            s2 = s2 + m * y
        return s1, s2

    s1, s2 = lax.fori_loop(0, SIDE, conv, (zero128, zero128))
    sbuf_b[me_b] = pack_rows([col(s1), col(s2)], 2)
    share_start(sbuf_b, me_b, bs, br)
    at[...] = jnp.transpose(acol[...].reshape(VOX, 256))
    share_wait(sbuf_b, me_b, bs, br)
    totb = total_of(sbuf_b, NB)
    n2 = norm_of(totb[0:1], totb[1:2], 2)

    def act2(p, carry):
        _, pre, sig = forward(y2[p], n2)
        return carry + mask * (pre * sig)

    feat2 = lax.fori_loop(0, POS, act2, zero128)
    feature = (jnp.concatenate([feat0, feat2], axis=1) / float(POS)).astype(BF16)
    lbuf[me] = dot(feature, r_ref[...])
    ls_c = []
    for d in range(1, NC):
        c = send_to(lbuf.at[me], lbuf.at[me], ls.at[d], lr.at[d], chan_peer(me, d))
        c.start()
        ls_c.append(c)
    for c in ls_c:
        c.wait_recv()
    logits = total_of(lbuf, NC)
    cls = lax.broadcasted_iota(jnp.int32, (ROWS, 512), 1)
    row512 = lax.broadcasted_iota(jnp.int32, (ROWS, 512), 0)
    labs = jnp.zeros((ROWS, 512), jnp.int32)
    for i in range(ROWS):
        labs = jnp.where(row512 == i, lab_ref[i % 4, i // 4], labs)
    real = cls < CLASSES
    logits = jnp.where(real, logits, -1e30)
    peak = jnp.max(logits, axis=1, keepdims=True)
    ex = jnp.exp(logits - peak)
    se = jnp.sum(ex, axis=1, keepdims=True)
    logprob = logits - peak - jnp.log(se)
    mask1 = mask[:, 0:1]
    hit = cls == labs
    loss_rows = -jnp.sum(jnp.where(hit, logprob, 0.0), axis=1, keepdims=True) * mask1
    soft = jnp.where(real, jnp.exp(logprob), 0.0)
    dlog = ((soft - hit.astype(F32)) * mask1 / counted[:, 0:1]).astype(BF16)
    dfeat = dot_t(dlog, r_ref[...], 1, 1) / float(POS)
    df0, df2 = dfeat[:, 0:128], dfeat[:, 128:256]

    def back(y, n, dout):
        normed, pre, sig = forward(y, n)
        return dout * mask * sig * (1.0 + pre * (1.0 - sig)), normed

    def back02(p, carry):
        g0, b0, g2, b2 = carry
        d0, m0 = back(ypos[p][:, 0:128], n0, df0)
        d2, m2 = back(y2[p], n2, df2)
        dpre[p] = jnp.concatenate([d0, d2], axis=1)
        return g0 + d0 * m0, b0 + d0, g2 + d2 * m2, b2 + d2

    g0, b0, g2, b2 = lax.fori_loop(0, POS, back02, (zero128,) * 4)
    loss_row = jnp.broadcast_to(jnp.sum(loss_rows, axis=0, keepdims=True), (1, 128))
    sbuf_c[me_b] = pack_rows([col(g0), col(b0), col(g2), col(b2), loss_row])
    share_start(sbuf_c, me_b, cs, cr)
    grr = dot_t(feature, dlog, 0, 0)
    for t in range(4):
        for dst, src, count in ((0, 0, 96), (96, 224, 32), (128, 96, 96), (224, 192, 32)):
            gr[t, src : src + count, :] = grr[dst : dst + count, 128 * t : 128 * t + 128]
    lane32 = lanes_of((32, 128))
    parts = []
    for j in range(8):
        for t in range(4):
            parts.append(
                (gr[t, pl.ds(j, 32, stride=8), :], 0, CLASSES * j + 128 * t,
                 min(128, CLASSES - 128 * t))
            )
    for i, v in enumerate(joined(parts, lane32, 25)):
        g[pl.ds(BULK["readout"] + i, 32, stride=25), :] = v
    for c in ls_c:
        c.wait_send()
    for c in ms_c:
        c.wait_send()
    share_wait(sbuf_c, me_b, cs, cr)
    totc = total_of(sbuf_c, NB)

    def finish(y, n, d, gg, gb):
        normed = (y - n[0]) * n[2]
        return mask * n[3] * n[2] * (d - gb / voxels - normed * gg / voxels)

    def dy2_at(p, carry):
        d = dpre[p]
        v = finish(y2[p], n2, d[:, 128:256], totc[2:3], totc[3:4])
        dypad[padded(p)] = jnp.concatenate([next_t(v), v, prev_t(v)], axis=1).astype(BF16)
        return carry

    lax.fori_loop(0, POS, dy2_at, 0)

    def conv_back(h, carry):
        acc = jnp.zeros((SIDE * ROWS, 256), F32)
        for q in range(9):
            dh, dw = divmod(q, 3)
            lhs = dypad[pl.ds((h + 2 - dh) * 9 + 2 - dw, SIDE)].reshape(SIDE * ROWS, 384)
            acc = acc + dot(lhs, wct_ref[q])
        for t in range(2):
            ynat[t, pl.ds(pl.multiple_of(h * SIDE * ROWS, SIDE * ROWS), SIDE * ROWS), :] = acc[
                :, 128 * t : 128 * t + 128
            ]
        return carry

    lax.fori_loop(0, SIDE, conv_back, 0)

    def to_dm(p, carry):
        for j in range(NC):
            a = ynat[j // 2, pl.ds(pl.multiple_of(p * ROWS, ROWS), ROWS), :]
            b = ynat[j // 2, pl.ds(pl.multiple_of((p + HALF) * ROWS, ROWS), ROWS), :]
            if j % 2 == 0:
                dm[j, p] = jnp.where(low_half, a, pltpu.roll(b, 64, 1)).astype(BF16)
            else:
                dm[j, p] = jnp.where(low_half, pltpu.roll(a, 64, 1), b).astype(BF16)
        return carry

    for t in range(2):
        ynat[t, pl.ds(VOX, ROWS), :] = zero128
    lax.fori_loop(0, HALF, to_dm, 0)
    far_i = lax.rem(me + 2, NC)
    lo_, hi_ = pl.ds(0, near), pl.ds(near, HALF - near)

    def far_copy(i):
        rows_, to = ((lo_, right), (hi_, left))[i]
        return send_to(dm.at[far_i, rows_], dgot.at[2, rows_], ds_.at[i], dr.at[i], to)

    def near_copy(i):
        who, rows_, to, slot = (
            (right_i, hi_, right, 0), (left_i, lo_, left, 1), (right_i, lo_, right, 0),
            (left_i, hi_, left, 1),
        )[i]
        return send_to(
            dm.at[who, rows_], dgot.at[slot, rows_], ds_.at[2 + i], dr.at[2 + i], to
        )

    far_c = [far_copy(i) for i in range(2)]
    near_c = [near_copy(i) for i in range(4)]
    for c in far_c + near_c[0:2]:
        c.start()

    def grad_conv(q, carry):
        dh = q // 3
        dw = q - dh * 3
        rhs = jnp.concatenate(
            [
                dypad[pl.ds((h + 2 - dh) * 9 + 2 - dw, SIDE)].reshape(SIDE * ROWS, 384)
                for h in range(SIDE)
            ],
            axis=0,
        )
        res = dot(at[...], rhs)
        for dt in range(3):
            tap = dt * 9 + q
            for j in range(NC):
                gq[48 * j : 48 * j + 48, :] = res[64 * j : 64 * j + 48, 128 * dt : 128 * dt + 128]
                vn[pl.ds(tap * 48 + 12 * j, 12), :] = res[
                    64 * j + 48 : 64 * j + 60, 128 * dt : 128 * dt + 128
                ]

            def put(i, v, tap=tap):
                g[pl.ds(BULK["spatial"] + tap * 144 + i, 48, stride=3), :] = v

            flatten_96(lambda j: gq[pl.ds(j, 48, stride=4), :], 48, put)
        return carry

    lax.fori_loop(0, 4, grad_conv, 0)
    for c in far_c:
        c.wait_recv()

    def add_far(p, carry):
        who = jnp.where(p < near, right_i, left_i)
        dm[who, p] = (dm[who, p].astype(F32) + dgot[2, p].astype(F32)).astype(dm.dtype)
        return carry

    lax.fori_loop(0, HALF, add_far, 0)
    for c in near_c[2:4]:
        c.start()
    lax.fori_loop(4, 9, grad_conv, 0)
    g[BULK["volume"] : BULK["volume"] + 324, :] = flatten_32(
        lambda j: vn[pl.ds(j, 324, stride=4), :], 324
    )

    core_i = lax.rem(me_b, 2)
    mate = digit_peer(me_b, 1, 2, 1)
    along = ((2, 8), (8, 2))
    digits = [[digit_of(me_b, along[i][s], 4) for i in range(2)] for s in range(2)]

    class Chunk:
        def __init__(self, index):
            self.base, self.last = CHUNKS[index]
            self.k = index
            self.first = 4 * self.last
            self.group = 4 * self.first
            self.half = 2 * self.group
            self.own = pl.multiple_of(self.base + core_i * self.half, self.last)
            self.r1 = (r1a, r1b)[index]
            self.r2 = (r2a, r2b)[index]
            self.gc = (gca, gcb)[index]

        def rows(self, at, count):
            return pl.ds(pl.multiple_of(at, self.last), count)

        def core_start(self):
            theirs = self.rows(self.base + (1 - core_i) * self.half, self.half)
            self.c0 = send_to(g.at[theirs], self.gc, co_s.at[self.k], co_r.at[self.k], mate)
            self.c0.start()

        def one_start(self):
            self.c0.wait()
            n = self.last

            def add(i, carry):
                at_ = self.rows(i * n, n)
                self.gc[at_, :] = self.gc[at_, :] + g[self.rows(self.own + i * n, n), :]
                return carry

            lax.fori_loop(0, self.half // n, add, 0)
            self.c1 = []
            for i in range(2):
                mine = digits[0][i]
                for d in range(1, 4):
                    to = lax.rem(mine + d, 4)
                    c = send_to(
                        self.gc.at[self.rows(i * self.group + to * self.first, self.first)],
                        self.r1.at[i, mine], s1s.at[self.k, i, d], s1r.at[self.k, i, d],
                        digit_peer(me_b, along[i][0], 4, d),
                    )
                    c.start()
                    self.c1.append(c)
                self.r1[i, mine] = self.gc[
                    self.rows(i * self.group + mine * self.first, self.first), :
                ]

        def two_start(self):
            for c in self.c1:
                c.wait()
            self.c2 = []
            for i in range(2):
                mine = digits[1][i]
                self.r1[i, 0] = total_of(self.r1.at[i], 4)
                for d in range(1, 4):
                    to = lax.rem(mine + d, 4)
                    c = send_to(
                        self.r1.at[i, 0, self.rows(to * self.last, self.last)],
                        self.r2.at[i, mine], s2s.at[self.k, i, d], s2r.at[self.k, i, d],
                        digit_peer(me_b, along[i][1], 4, d),
                    )
                    c.start()
                    self.c2.append(c)
                self.r2[i, mine] = self.r1[i, 0, self.rows(mine * self.last, self.last), :]

        def gather_start(self):
            for c in self.c2:
                c.wait()
            self.c3 = []
            for i in range(2):
                at_ = self.rows(
                    self.own + i * self.group + digits[0][i] * self.first
                    + digits[1][i] * self.last,
                    self.last,
                )
                gb_ref[at_, :] = total_of(self.r2.at[i], 4)
                for d in range(1, 4):
                    c = send_to(
                        gb_ref.at[at_], gb_ref.at[at_], g1s.at[self.k, i, d],
                        g1r.at[self.k, i, d], digit_peer(me_b, along[i][1], 4, d),
                    )
                    c.start()
                    self.c3.append(c)

        def spread_start(self):
            for c in self.c3:
                c.wait()
            self.c4 = []
            self.c5 = []
            for i in range(2):
                mine = digits[0][i]
                at_ = self.rows(self.own + i * self.group + mine * self.first, self.first)
                for d in range(1, 4):
                    c = send_to(
                        gb_ref.at[at_], gb_ref.at[at_], g2s.at[self.k, i, d],
                        g2r.at[self.k, i, d], digit_peer(me_b, along[i][0], 4, d),
                    )
                    c.start()
                    self.c4.append((c, i, d))
                self.mate_start(i, 0)

        def mate_start(self, i, d):
            digit = lax.rem(digits[0][i] - d + 4, 4)
            at_ = self.rows(self.own + i * self.group + digit * self.first, self.first)
            c = send_to(
                gb_ref.at[at_], gb_ref.at[at_], g3s.at[self.k, i, d], g3r.at[self.k, i, d], mate
            )
            c.start()
            self.c5.append(c)

        def mate_rest(self):
            for c, i, d in self.c4:
                c.wait_recv()
                self.mate_start(i, d)

        def finish(self):
            for c, i, d in self.c4:
                c.wait_send()
            for c in self.c5:
                c.wait()

    first_chunk, second_chunk = Chunk(0), Chunk(1)
    first_chunk.core_start()

    for c in near_c:
        c.wait_recv()

    def back1(p, carry):
        g1, b1 = carry
        s = dm[me, p].astype(F32) + dgot[0, p].astype(F32) + dgot[1, p].astype(F32)
        d, m = back(ypos[p][:, 128:256], n1, jnp.where(low_half, s, 0.0))
        ob[p] = d
        g1, b1 = g1 + d * m, b1 + d
        q = jnp.minimum(p + HALF, POS - 1)
        live = (p < POS - HALF).astype(F32)
        d, m = back(ypos[q][:, 128:256], n1, jnp.where(low_half, pltpu.roll(s, 64, 1), 0.0) * live)

        @pl.when(p < POS - HALF)
        def _():
            ob[p + HALF] = d

        return g1 + d * m, b1 + d

    g1, b1 = lax.fori_loop(0, HALF, back1, (zero128, zero128))
    sbuf_d[me_b] = pack_rows([col(g1), col(b1)], 2)
    share_start(sbuf_d, me_b, es, er)
    for c in far_c + near_c:
        c.wait_send()
    first_chunk.one_start()

    def dy0_at(p, carry):
        v = finish(ypos[p][:, 0:128], n0, dpre[p][:, 0:128], totc[0:1], totc[1:2])
        v = v.astype(BF16).astype(F32)
        h, w = p // SIDE, lax.rem(p, SIDE)
        n_h = 3 - (h == 0).astype(jnp.int32) - (h == SIDE - 1).astype(jnp.int32)
        n_w = 3 - (w == 0).astype(jnp.int32) - (w == SIDE - 1).astype(jnp.int32)
        share = v / jnp.maximum(n_t * (n_h * n_w).astype(F32), 1.0)
        box[padded(p)] = share + prev_t(share) + next_t(share)
        ypos[p, :, 0:128] = v
        return carry

    lax.fori_loop(0, POS, dy0_at, 0)

    def dy0_nat(p, carry):
        acc, _ = spread(p)
        v = jnp.where(is_pool, acc * mask, ypos[p][:, 0:128])
        lowv = v - v.astype(BF16).astype(F32)
        dnat[0, pl.ds(p, ROWS, stride=POS), :] = v
        dnat[1, pl.ds(p, ROWS, stride=POS), :] = lowv
        return carry

    lax.fori_loop(0, POS, dy0_nat, 0)

    for tile in range(2):
        gw1_ref[tile] = jnp.zeros((CIN, 128), F32)

    def grad_one(r, width, fold):
        first, off, lanes = window_of(r)
        rhs = jnp.concatenate(
            [dnat[t, pl.ds(r, GPAD, stride=8), :] for t in range(width // 128)], axis=1
        ).astype(BF16)
        for k in range(NC):
            res = dot_t(xg[k, :, first : first + lanes], rhs, 0, 0)[off : off + CB]
            if fold:
                gw1_ref[0, k * CB : (k + 1) * CB, :] += res[:, 0:128] + res[:, 128:256]
            else:
                gw1_ref[1, k * CB : (k + 1) * CB, :] += res

    for r in range(8):
        grad_one(r, 256, True)

    def put_direct(i, v):
        g[pl.ds(BULK["direct"] + i, 208, stride=3), :] = v

    flatten_96(lambda j: gw1_ref[0, pl.ds(j, 208, stride=4), :], 208, put_direct)
    g[BULK["pooled"] : BULK["pooled"] + 208, :] = flatten_32(
        lambda j: gw1_ref[0, pl.ds(j, 208, stride=4), :], 208
    )

    second_chunk.core_start()
    share_wait(sbuf_d, me_b, es, er)
    totd = total_of(sbuf_d, NB)

    def dy1_nat(p, carry):
        v = finish(ypos[p][:, 128:256], n1, ob[p], totd[0:1], totd[1:2])
        dnat[0, pl.ds(p, ROWS, stride=POS), :] = v
        return carry

    lax.fori_loop(0, POS, dy1_nat, 0)
    for r in range(8):
        grad_one(r, 128, False)

    lane104, lane26 = lanes_of((104, 128)), lanes_of((26, 128))
    lsend[pl.ds(384, 128), :] = jnp.zeros((128, 128), F32)
    parts = [(gw1_ref[1, pl.ds(j, 104, stride=8), :], 0, 48 * j, 48) for j in range(8)]
    for i, v in enumerate(joined(parts, lane104, 3)):
        lsend[pl.ds(LATE["squeeze"] + i, 104, stride=3), :] = v
    parts = [(gw1_ref[1, pl.ds(j, 26, stride=32), :], 48, 12 * j, 12) for j in range(32)]
    for i, v in enumerate(joined(parts, lane26, 3)):
        lsend[pl.ds(LATE["shrink"] + i, 26, stride=3), :] = v

    def late_at(i):
        return pl.ds(pl.multiple_of(i * LATE_ROWS, LATE_ROWS), LATE_ROWS)

    def late_copy(d):
        to = lax.rem(me_b + d, NB)
        return send_to(
            lsend.at[late_at(to)], lgot.at[me_b], fs, fr, batch_peer(me_b, d)
        )

    def late_start(d, carry):
        late_copy(d).start()
        return carry

    lax.fori_loop(1, NB, late_start, 0)
    lgot[me_b] = lsend[late_at(me_b), :]

    first_chunk.two_start()
    second_chunk.one_start()
    first_chunk.gather_start()
    share_wait(lgot, me_b, fs, fr)
    late_ref[me_b] = total_of(lgot, NB)
    share_start(late_ref, me_b, hs, hr)
    second_chunk.two_start()
    first_chunk.spread_start()
    second_chunk.gather_start()

    fix = voxels / (voxels - 1.0)
    for tile, n, gg, gb in (
        (0, n0, totc[0:1], totc[1:2]),
        (1, n1, totd[0:1], totd[1:2]),
        (2, n2, totc[2:3], totc[3:4]),
    ):
        st_ref[:, 128 * tile : 128 * tile + 128] = pack_rows([gg, gb, n[0], n[1] * fix])
    sc_ref[...] = pack_rows([totc[4:5], counted])

    for buf, send, recv in (
        (sbuf_a, as_, ar), (sbuf_b, bs, br), (sbuf_c, cs, cr), (sbuf_d, es, er), (lgot, fs, fr),
    ):
        share_sent(buf, me_b, send, recv)
    second_chunk.spread_start()
    first_chunk.mate_rest()
    second_chunk.mate_rest()
    share_wait(late_ref, me_b, hs, hr)
    share_sent(late_ref, me_b, hs, hr)
    first_chunk.finish()
    second_chunk.finish()


def core(x, lengths, labels, weights, affine):
    vm = pl.BlockSpec(memory_space=pltpu.VMEM)
    sm = pl.BlockSpec(memory_space=pltpu.SMEM)
    hbm = pl.BlockSpec(memory_space=pltpu.HBM)
    dma = pltpu.SemaphoreType.DMA
    vmem = pltpu.VMEM
    return pl.pallas_call(
        core_kernel,
        out_shape=(
            jax.ShapeDtypeStruct((BULK_ROWS, 128), F32),
            jax.ShapeDtypeStruct((NB, LATE_ROWS, 128), F32),
            jax.ShapeDtypeStruct((8, 384), F32),
            jax.ShapeDtypeStruct((8, 128), F32),
        ),
        in_specs=[hbm, sm, sm] + [hbm] * 7 + [vm],
        out_specs=(vm,) * 4,
        scratch_shapes=[
            vmem((1, 326144), BF16),
            *[vmem((1, FLAT[n] * 128), F32) for n in NARROW],
            vmem((2, CIN, 128), F32),
            vmem((CIN, 128), F32),
            vmem((R1, 128), F32),
            vmem((1304, 128), F32),
            vmem((4, 256, 128), F32),
            vmem((9, 256, 384), BF16),
            vmem((9, 384, 256), BF16),
            vmem((256, 512), BF16),
            vmem((8, 384), F32),
            vmem((13 * GPAD, 128), F32),
            vmem((NC, GPAD, GW), BF16),
            vmem((NC, W1_ROWS, 256), BF16),
            vmem((2, 8 * GPAD, 128), F32),
            vmem((POS, ROWS, 256), F32),
            vmem((81, ROWS, 128), F32),
            vmem((POS + 1, ROWS, 128), F32),
            vmem((NC, HALF, ROWS, 128), BF16),
            vmem((81, ROWS, 256), BF16),
            vmem((POS, ROWS, 256), BF16),
            vmem((256, VOX), BF16),
            vmem((POS, ROWS, 128), F32),
            vmem((POS, ROWS, 256), F32),
            vmem((81, ROWS, 384), BF16),
            vmem((NC, HALF, ROWS, 128), BF16),
            vmem((3, HALF, ROWS, 128), BF16),
            vmem((2, 8 * GPAD, 128), F32),
            vmem((2, CIN, 128), F32),
            vmem((R1, 128), F32),
            vmem((4, 256, 128), F32),
            vmem((BULK_ROWS, 128), F32),
            *[vmem((32 * n, 128), F32) for _, n in CHUNKS],
            *[vmem((2, 4, 4 * n, 128), F32) for _, n in CHUNKS],
            *[vmem((2, 4, n, 128), F32) for _, n in CHUNKS],
            vmem((NB * LATE_ROWS, 128), F32),
            vmem((NB, LATE_ROWS, 128), F32),
            vmem((NC, ROWS, 512), F32),
            *[vmem((NB, n, 128), F32) for n in (8, 2, 8, 2)],
            dma((4,)), dma((7,)), dma((6,)), dma((6,)),
            dma((6,)), dma((6,)), dma((NC,)), dma((NC,)), dma((6,)), dma((6,)),
            *[dma] * 12,
            dma((2,)), dma((2,)),
            *[dma((2, 2, 4))] * 10,
        ],
        compiler_params=pltpu.CompilerParams(
            collective_id=0, has_side_effects=True, vmem_limit_bytes=63 << 20
        ),
        name="block",
    )(x, lengths, labels, *weights, affine)


def unlanes(tiles):
    t0, t1, t2 = tiles
    lane = lanes_of(t0.shape)
    parts = [(t0, 0, 0, 96), (t1, 0, 96, 60), (t0, 96, 156, 32), (t2, 0, 188, 128)]
    return joined(parts, lane, 3)


def adam_kernel(*refs):
    gb_in, late, st, sc, running = refs[0:5]
    w_in, m_in, v_in = refs[5:13], refs[13:21], refs[21:29]
    m_out, v_out, w_out = refs[29:37], refs[37:45], refs[45:53]
    run_out, loss_out, count_out, copies_out = refs[53:57]
    wb, mb, vb = refs[57:64], refs[64:71], refs[71:78]
    cb, gb, insem, gsem, outsem, csem = refs[78:84]
    rates = step_rates()
    parts = []
    for i in (4, 3, 5, 1, 0, 6):
        parts.append((i, 0, FLAT[NAMES[i]]))
    for first in range(0, FLAT["spatial"], ADAM_ROWS):
        parts.append((2, first, ADAM_ROWS))

    def at_rows(ref, i, first, count):
        if NAMES[i] in NARROW:
            return ref.at[:, pl.ds(first * 128, count * 128)]
        return ref.at[pl.ds(first, count)]

    ins = []
    for n, (i, first, count) in enumerate(parts):
        mine = []
        for kind, (src, dst) in enumerate(((w_in[i], wb[i]), (m_in[i], mb[i]), (v_in[i], vb[i]))):
            c = pltpu.make_async_copy(
                at_rows(src, i, first, count), at_rows(dst, i, first, count), insem.at[n, kind]
            )
            c.start()
            mine.append(c)
        if NAMES[i] in BULK:
            at = pl.ds(BULK[NAMES[i]] + first, count)
            c = pltpu.make_async_copy(gb_in.at[at], gb.at[at], gsem.at[n])
            c.start()
            mine.append(c)
        ins.append(mine)

    starts = []
    total = 0
    for name in NAMES:
        starts.append(total * 128)
        total += FLAT[name]
    outs = []
    for n, (i, first, rows) in enumerate(parts):
        name = NAMES[i]
        for c in ins[n]:
            c.wait()

        def step(at, count, i=i, name=name):
            if name in BULK:
                grad = gb[pl.ds(BULK[name] + at, count), :]
            else:
                grad = late[pl.ds(LATE[name] + at, count), :]
            wide = pl.ds(pl.multiple_of(at * 128, 128), count * 128)
            narrow = name in NARROW

            def load(ref):
                if narrow:
                    return ref[:, wide].reshape(count, 128)
                return ref[pl.ds(at, count), :]

            def store(ref, v):
                if narrow:
                    ref[:, wide] = v.reshape(1, count * 128)
                else:
                    ref[pl.ds(at, count), :] = v

            m, v, w = adamw(load(wb[i]), load(mb[i]), load(vb[i]), grad, rates[i])
            store(mb[i], m)
            store(vb[i], v)
            store(wb[i], w)
            cb[:, pl.ds(pl.multiple_of(starts[i] + at * 128, 128), count * 128)] = w.reshape(
                1, count * 128
            ).astype(BF16)

        block = {"spatial": 72, "readout": 80, "direct": 48, "pooled": 104, "squeeze": 104}.get(
            name, 24
        )
        loops = rows // block

        def body(j, carry, step=step, block=block, first=first):
            step(pl.multiple_of(first + j * block, 8), block)
            return carry

        lax.fori_loop(0, loops, body, 0)
        at, rest = first + loops * block, rows - loops * block
        if rest // 8:
            step(at, rest // 8 * 8)
        if rest % 8:
            step(at + rest // 8 * 8, rest % 8)
        for kind, (src, dst) in enumerate(((wb[i], w_out[i]), (mb[i], m_out[i]), (vb[i], v_out[i]))):
            c = pltpu.make_async_copy(
                at_rows(src, i, first, rows), at_rows(dst, i, first, rows), outsem.at[n, kind]
            )
            c.start()
            outs.append(c)
        at = pl.ds(starts[i] + first * 128, rows * 128)
        c = pltpu.make_async_copy(cb.at[:, at], copies_out.at[:, at], csem.at[n])
        c.start()
        outs.append(c)

    tiles = [st[:, 128 * t : 128 * t + 128] for t in range(3)]
    for t, v in enumerate(unlanes(tiles)):
        width = min(128, 316 - 128 * t)
        at = slice(128 * t, 128 * t + width)
        v = v[:, 0:width]
        m, s, w = adamw(w_in[7][:, at], m_in[7][:, at], v_in[7][:, at], v[0:2], rates[7])
        m_out[7][:, at] = m
        v_out[7][:, at] = s
        w_out[7][:, at] = w
        run_out[:, at] = MOMENTUM * running[:, at] + (1.0 - MOMENTUM) * v[2:4]
    loss_out[...] = sc[0:1, 0:1]
    count_out[...] = sc[1:2, 0:1]
    for c in outs:
        c.wait()


def adam(gb, late, st, sc, running, masters, firsts, seconds):
    vm = pl.BlockSpec(memory_space=pltpu.VMEM)
    hbm = pl.BlockSpec(memory_space=pltpu.HBM)
    dma = pltpu.SemaphoreType.DMA
    shapes = [(1, FLAT[n] * 128) if n in NARROW else (FLAT[n], 128) for n in NAMES]
    flats = [jax.ShapeDtypeStruct(shape, F32) for shape in shapes]
    small = jax.ShapeDtypeStruct((2, 316), F32)
    total = sum(FLAT[n] for n in NAMES) * 128
    one = jax.ShapeDtypeStruct((1, 1), F32)
    specs = [hbm] * 7 + [vm]
    buffers = [pltpu.VMEM(shape, F32) for shape in shapes]
    count = 6 + FLAT["spatial"] // ADAM_ROWS
    return pl.pallas_call(
        adam_kernel,
        out_shape=[*(flats + [small]) * 3, small, one, one, jax.ShapeDtypeStruct((1, total), BF16)],
        in_specs=[hbm] + [vm] * 4 + specs * 3,
        out_specs=[*specs * 3, vm, vm, vm, hbm],
        scratch_shapes=[
            *buffers * 3, pltpu.VMEM((1, total), BF16), pltpu.VMEM((BULK_ROWS, 128), F32),
            dma((count, 3)), dma((count,)), dma((count, 3)), dma((count,)),
        ],
        compiler_params=pltpu.CompilerParams(vmem_limit_bytes=63 << 20),
        name="adamw",
    )(gb, late, st, sc, running, *masters, *firsts, *seconds)


def per_device(
    features, lengths, labels, direct, squeeze, spatial, shrink, volume, pooled, readout, affine,
    first_direct, first_squeeze, first_spatial, first_shrink, first_volume, first_pooled,
    first_readout, first_affine, second_direct, second_squeeze, second_spatial, second_shrink,
    second_volume, second_pooled, second_readout, second_affine, running,
):
    masters = [direct, squeeze, spatial, shrink, volume, pooled, readout, affine]
    firsts = [
        first_direct, first_squeeze, first_spatial, first_shrink, first_volume, first_pooled,
        first_readout, first_affine,
    ]
    seconds = [
        second_direct, second_squeeze, second_spatial, second_shrink, second_volume,
        second_pooled, second_readout, second_affine,
    ]
    def rows(flat, name):
        return flat if name in NARROW else flat.reshape(-1, 128)

    masters, firsts, seconds = (
        [rows(a, n) for a, n in zip(group, NAMES)] + [group[7]]
        for group in (masters, firsts, seconds)
    )
    gb, late, st, sc = core(features, lengths, labels.T, masters[:7], affine)
    out = adam(gb, late.reshape(NB * LATE_ROWS, 128), st, sc, running, masters, firsts, seconds)
    flat_out = [a if i % 8 == 7 else a.reshape(1, -1) for i, a in enumerate(out[:24])]
    return (*flat_out, out[24], out[25].reshape(()), out[26].reshape(()), out[27])


def solution(mesh):
    flat = P("chan", None)
    wide = P(None, "chan")
    weights = (flat,) * 7 + (wide,)
    return jax.shard_map(
        per_device,
        mesh=mesh,
        in_specs=(P("chan", "batch"), P("batch"), P("batch", None)) + weights * 3 + (wide,),
        out_specs=weights * 3 + (wide, P(), P(), flat),
        check_vma=False,
    )
```

```python
import math
from functools import partial

import jax
import jax.numpy as jnp
from jax import lax
from jax.experimental import pallas as pl
from jax.experimental.pallas import tpu as pltpu
from jax.sharding import PartitionSpec as P

CIN = 832
B0 = 384
R1 = 192
O1 = 384
R2 = 48
O2 = 128
B3 = 128
CLASSES = 400
SIDE = 7
STEP = 5
NC = 4
NB = 32
POS = SIDE * SIDE
ROWS = 32
VOX = POS * ROWS
GROUPS = VOX // 8
GPAD = 208
CB = CIN // NC
GW = 8 * CB
HALF = 25
SHIFT = 112
W1_ROWS = 448
TAPS = 27
FLAT = {"direct": 624, "squeeze": 312, "spatial": 3888, "shrink": 78, "volume": 324, "pooled": 208,
        "readout": 800}
NAMES = ("direct", "squeeze", "spatial", "shrink", "volume", "pooled", "readout")
HELD = {"spatial": 0, "volume": 3888, "direct": 4216, "pooled": 4840, "readout": 5048}
BULK = {"volume": 4720, "direct": 5120, "pooled": 5744, "readout": 1728}
EARLY_TAPS = 4
NARROW = ("shrink", "volume")
LATE = {"squeeze": 0, "shrink": 312}
CHUNKS = ((0, 40), (2560, 40))
DIRECT_AT = 5120
DIRECT_ROWS = 32
BULK_ROWS = 6144
LATE_ROWS = 16
ADAM_ROWS = 648
ADAM_ORDER = (3, 1, 5, 0, 6, 4)

EPS = 1e-05
BETA_ONE = 0.5
BETA_TWO = 0.5
DECAY = 0.01
MOMENTUM = 0.99

MESH = pl.DeviceIdType.MESH
F32 = jnp.float32
BF16 = jnp.bfloat16


def step_rates():
    return [
        1.5 / math.sqrt(CIN),
        1.5 / math.sqrt(CIN),
        1.5 / math.sqrt(27 * R1),
        1.5 / math.sqrt(CIN),
        1.5 / math.sqrt(27 * R2),
        1.5 / math.sqrt(CIN),
        0.2,
        0.3,
    ]


def adamw(weight, moment_one, moment_two, gradient, step_rate):
    first_new = BETA_ONE * moment_one + (1.0 - BETA_ONE) * gradient
    second_new = BETA_TWO * moment_two + (1.0 - BETA_TWO) * (gradient * gradient)
    scale_one = step_rate / (1.0 - BETA_ONE**STEP)
    scale_two = 1.0 / (1.0 - BETA_TWO**STEP)
    weight_new = weight * (1.0 - step_rate * DECAY) - scale_one * first_new / (
        jnp.sqrt(second_new * scale_two) + 1e-08
    )
    return (first_new, second_new, weight_new)


def window_of(r):
    start = CB * r
    tile, offset = divmod(start, 128)
    lanes = 256 if offset + CB <= 256 else 384
    return tile * 128, offset, lanes


def dot(a, b):
    return jnp.dot(a, b, preferred_element_type=F32)


def dot_t(a, b, ca, cb):
    return lax.dot_general(a, b, (((ca,), (cb,)), ((), ())), preferred_element_type=F32)


def send_to(src, dst, send, recv, target):
    return pltpu.make_async_remote_copy(
        src_ref=src, dst_ref=dst, send_sem=send, recv_sem=recv, device_id=target,
        device_id_type=MESH,
    )


def batch_peer(me, d):
    return {"batch": lax.rem(me + d, NB)}


def chan_peer(me, d):
    return {"chan": lax.rem(me + d, NC)}


def share_start(buf, me, send, recv):
    def one(d, carry):
        send_to(buf.at[me], buf.at[me], send, recv, batch_peer(me, d)).start()
        return carry

    lax.fori_loop(1, NB, one, 0)


def share_copy(buf, me, send, recv):
    others = buf.at[pl.ds(0, NB - 1)]
    return send_to(others, others, send, recv, batch_peer(me, 1))


def share_wait(buf, me, send, recv):
    share_copy(buf, me, send, recv).wait_recv()


def share_sent(buf, me, send, recv):
    share_copy(buf, me, send, recv).wait_send()


def digit_of(me, stride, size):
    return lax.rem(me // stride, size)


def digit_peer(me, stride, size, d):
    digit = digit_of(me, stride, size)
    return {"batch": me + stride * (lax.rem(digit + d, size) - digit)}


def piece(tiles, start, width, dest, lane):
    tile, off = divmod(start, 128)
    v = tiles[tile]
    if off + width > 128:
        v = jnp.where(lane >= off, v, tiles[tile + 1])
    shift = (dest - off) % 128
    return pltpu.roll(v, shift, 1) if shift else v


def joined(parts, lane, count):
    out = []
    moved = []
    for value, src, start, width in parts:
        shift = (start - src) % 128
        moved.append((pltpu.roll(value, shift, 1) if shift else value, start, width))
    for i in range(count):
        acc = None
        for value, start, width in moved:
            lo, hi = max(0, start - 128 * i), min(128, start + width - 128 * i)
            if lo < hi:
                acc = value if acc is None else jnp.where(lane >= lo, value, acc)
        out.append(acc)
    return out


def lanes_of(v):
    return lax.broadcasted_iota(jnp.int32, v, 1)


def tap_rows(dt, q):
    return q * 432 + jnp.where(q >= EARLY_TAPS, 832, 0) + dt * 144


def prepare_w1(flat, wn, wk, w1p):
    lane = lanes_of((208, 128))
    tiles = [flat["direct"][pl.ds(i, 208, stride=3), :] for i in range(3)]
    pool = flat["pooled"][...]
    for j in range(4):
        v = jnp.where(
            lane < 96, piece(tiles, 96 * j, 96, 0, lane), piece([pool], 32 * j, 32, 96, lane)
        )
        wn[0, pl.ds(j, 208, stride=4), :] = v
    lane = lanes_of((104, 128))
    tiles = [flat["squeeze"][pl.ds(i, 104, stride=3), :] for i in range(3)]
    for j in range(8):
        wn[1, pl.ds(j, 104, stride=8), :] = piece(tiles, 48 * j, 48, 0, lane)
    lane = lanes_of((26, 128))
    tiles = [flat["shrink"][pl.ds(i, 26, stride=3), :] for i in range(3)]
    for j in range(32):
        wk[pl.ds(j, 26, stride=32), :] = piece(tiles, 12 * j, 12, 48, lane)
    lane = lanes_of((CB, 128))
    for k in range(NC):
        rows = slice(k * CB, (k + 1) * CB)
        second = jnp.where(lane < 48, wn[1, rows, :], jnp.where(lane < 60, wk[rows, :], 0.0))
        both = jnp.concatenate([wn[0, rows, :], second], axis=1).astype(BF16)
        w1p[k, 0:SHIFT, :] = jnp.zeros((SHIFT, 256), BF16)
        w1p[k, SHIFT : SHIFT + CB, :] = both
        w1p[k, SHIFT + CB : W1_ROWS, :] = jnp.zeros((W1_ROWS - SHIFT - CB, 256), BF16)


def prepare_conv(flat, tb, vn, wc, wct):
    lane = lanes_of((324, 128))
    for j in range(4):
        v = piece([flat["volume"][...]], 32 * j, 32, 96, lane)
        vn[pl.ds(j, 324, stride=4), :] = jnp.where(lane >= 96, v, 0.0)
    vn[pl.ds(1296, 8), :] = jnp.zeros((8, 128), F32)
    lane48 = lanes_of((48, 128))
    row16 = lax.broadcasted_iota(jnp.int32, (16, 128), 0)

    def one(q, carry):
        for dt in range(3):
            tap = dt * 9 + q
            tiles = [
                flat["spatial"][pl.ds(tap * 144 + i, 48, stride=3), :] for i in range(3)
            ]
            for j in range(4):
                v = piece(tiles, 96 * j, 96, 0, lane48)
                tb[pl.ds(j, 48, stride=4), :] = jnp.where(lane48 < 96, v, 0.0)
            for j in range(NC):
                at = slice(128 * dt, 128 * dt + 128)
                wc[q, 64 * j : 64 * j + 48, at] = tb[48 * j : 48 * j + 48, :].astype(BF16)
                v = vn[pl.ds(tap * 48 + 12 * j, 16), :]
                wc[q, 64 * j + 48 : 64 * j + 64, at] = jnp.where(row16 < 12, v, 0.0).astype(BF16)
        wct[q] = jnp.transpose(wc[q])
        return carry

    lax.fori_loop(0, 9, one, 0)


def prepare_readout(flat, rn, rp):
    lane = lanes_of((32, 128))
    tiles = [flat["readout"][pl.ds(i, 32, stride=25), :] for i in range(25)]
    for t in range(4):
        width = min(128, CLASSES - 128 * t)
        for j in range(8):
            v = piece(tiles, CLASSES * j + 128 * t, width, 0, lane)
            rn[t, pl.ds(j, 32, stride=8), :] = v if width == 128 else jnp.where(lane < width, v, 0.0)
        at = slice(128 * t, 128 * t + 128)
        for dst, src, count in ((0, 0, 96), (96, 224, 32), (128, 96, 96), (224, 192, 32)):
            rp[dst : dst + count, at] = rn[t, src : src + count, :].astype(BF16)


def prepare_affine(aff, out):
    a = [aff[:, 0:128], aff[:, 128:256]]
    a.append(jnp.concatenate([aff[:, 256:316], jnp.zeros((2, 68), F32)], axis=1))
    lane = lanes_of((2, 128))
    t0 = jnp.where(lane < 96, a[0], piece(a, 156, 32, 96, lane))
    t1 = jnp.where(lane < 60, piece(a, 96, 60, 0, lane), 0.0)
    t2 = piece(a, 188, 128, 0, lane)
    for i, t in enumerate((t0, t1, t2)):
        out[0:2, 128 * i : 128 * i + 128] = t


def flatten_96(src, rows, put):
    lane = lanes_of((rows, 128))
    for i, v in enumerate(joined([(src(j), 0, 96 * j, 96) for j in range(4)], lane, 3)):
        put(i, v)


def flatten_32(src, rows):
    lane = lanes_of((rows, 128))
    return joined([(src(j), 96, 32 * j, 32) for j in range(4)], lane, 1)[0]


def total_of(buf, count):
    acc = buf[0]
    for slot in range(1, count):
        acc = acc + buf[slot]
    return acc


def core_kernel(
    x_hbm, len_ref, lab_ref, direct_hbm, squeeze_hbm, spatial_hbm, shrink_hbm, volume_hbm,
    pooled_hbm, readout_hbm, affine_ref,
    gb_ref, late_ref, st_ref, sc_ref,
    x_ref, n_shrink, n_volume,
    wn, wk, tb, vn, rn, wc_ref, wct_ref, r_ref, aff_ref,
    xf, xg, xt, cols, w1p, ynat, ypos, box, ob, got, apad, acol, at, y2, dpre, dypad, dm, dgot, dnat,
    gw1_ref, gq, gr, g, gca, gcb, gcc, r1a, r1b, r2a, r2b, rc, lsend, lgot, psend, pgot,
    lbuf, sbuf_a, sbuf_b, sbuf_c, sbuf_d,
    xin, win, xs, xr, ms, mr, ls, lr, ds_, dr,
    as_, ar, bs, br, cs, cr, es, er, fs, fr, hs, hr,
    co_s, co_r, s1s, s1r, s2s, s2r, g1s, g1r, g2s, g2r, g3s, g3r, ps, pr, d1s, d1r, d2s, d2r, d3s, d3r,
):
    me_b = lax.axis_index("batch")
    me = lax.axis_index("chan")

    barrier = pltpu.get_barrier_semaphore()

    loops = (0, 104, 182, 260, 318)
    cuts = [1024 * n for n in loops[:4]] + [326144]
    x_in = []
    for i in range(4):
        at_ = pl.ds(cuts[i], cuts[i + 1] - cuts[i])
        c = pltpu.make_async_copy(x_hbm.at[:, at_], x_ref.at[:, at_], xin.at[i])
        c.start()
        x_in.append(c)
    flat = {n: g.at[at_ : at_ + FLAT[n]] for n, at_ in HELD.items()}
    flat.update({n: lsend.at[at_ : at_ + FLAT[n]] for n, at_ in LATE.items()})
    w_in = []
    for i, (src, name) in enumerate(
        zip(
            (direct_hbm, squeeze_hbm, spatial_hbm, shrink_hbm, volume_hbm, pooled_hbm, readout_hbm),
            NAMES,
        )
    ):
        dst = {"shrink": n_shrink, "volume": n_volume}.get(name, flat[name])
        c = pltpu.make_async_copy(src, dst, win.at[i])
        c.start()
        w_in.append(c)

    def greet(d, carry):
        pl.semaphore_signal(barrier, inc=1, device_id=batch_peer(me_b, d), device_id_type=MESH)
        return carry

    lax.fori_loop(1, NB, greet, 0)
    for d in range(1, NC):
        pl.semaphore_signal(barrier, inc=1, device_id=chan_peer(me, d), device_id_type=MESH)

    def flat_rows(i, carry):
        v = x_ref[:, pl.ds(pl.multiple_of(i * 1024, 1024), 1024)].astype(F32)
        xf[pl.ds(pl.multiple_of(i * 8, 8), 8), :] = v.reshape(8, 128)
        return carry

    right, left = chan_peer(me, 1), chan_peer(me, NC - 1)
    left_i, right_i = lax.rem(me + NC - 1, NC), lax.rem(me + 1, NC)
    bounds = (0, 64, 112, 160, GPAD)

    def part(who, i):
        return xg.at[who, bounds[i] : bounds[i + 1]]

    def hop(i, side):
        return send_to(
            part(me, i), part(me, i), xs.at[4 * side + i], xr.at[4 * side + i], (right, left)[side]
        )

    def pass_on(i):
        who, to = ((left_i, right), (right_i, left))[i // 2]
        return send_to(part(who, i), part(who, i), xs.at[8 + i], xr.at[8 + i], to)

    xf[pl.ds(2548, 2704 - 2548), :] = jnp.zeros((2704 - 2548, 128), F32)
    for i in range(4):
        x_in[i].wait()
        lax.fori_loop(loops[i], loops[i + 1], flat_rows, 0, unroll=(8, 6, 6, 2)[i])
        if i == 3:
            xf[pl.ds(2544, 4), :] = x_ref[:, 318 * 1024 : 318 * 1024 + 512].astype(F32).reshape(
                4, 128
            )
        low, count = bounds[i], bounds[i + 1] - bounds[i]
        for t in range(13):
            xg[me, low : low + count, 128 * t : 128 * t + 128] = xf[
                pl.ds(13 * low + t, count, stride=13), :
            ].astype(BF16)
        if i == 0:
            pl.semaphore_wait(barrier, NB - 1 + NC - 1)
        for side in range(2):
            hop(i, side).start()

    rowi = lax.broadcasted_iota(jnp.int32, (ROWS, 128), 0)
    lane = lax.broadcasted_iota(jnp.int32, (ROWS, 128), 1)
    clip = rowi // 4
    step = rowi - clip * 4
    lens = jnp.zeros((ROWS, 128), jnp.int32)
    for c in range(8):
        lens = jnp.where(clip == c, len_ref[c], lens)
    mask = (step < lens).astype(F32)
    has_prev = (step > 0).astype(F32)
    has_next = (step < 3).astype(F32)

    def prev_t(v):
        return pltpu.roll(v, 1, 0) * has_prev

    def next_t(v):
        return pltpu.roll(v, ROWS - 1, 0) * has_next

    n_t = mask + prev_t(mask) + next_t(mask)
    is_pool = lane >= 96
    low_half = lane < 64

    for c in w_in:
        c.wait()
    for src, dst in ((n_shrink, flat["shrink"]), (n_volume, flat["volume"])):
        count = dst.shape[0]
        whole = count // 8 * 8
        dst[0:whole, :] = src[:, 0 : whole * 128].reshape(whole, 128)
        dst[whole:count, :] = src[:, whole * 128 : count * 128].reshape(count - whole, 128)
    prepare_w1(flat, wn, wk, w1p)
    prepare_affine(affine_ref, aff_ref)
    prepare_readout(flat, rn, r_ref)

    def zero_pad(i, carry):
        apad[i] = jnp.zeros((ROWS, 256), BF16)
        dypad[i] = jnp.zeros((ROWS, 384), BF16)
        box[i] = jnp.zeros((ROWS, 128), F32)
        return carry

    lax.fori_loop(0, 81, zero_pad, 0, unroll=9)
    dnat[...] = jnp.zeros_like(dnat)
    prepare_conv(flat, tb, vn, wc_ref, wct_ref)

    for i in range(4):
        hop(i, i // 2).wait_recv()
        pass_on(i).start()
    for i in range(4):
        hop(i, 1 - i // 2).wait_recv()

    far_i = lax.rem(me + 2, NC)

    def one_by_one(r, blocks):
        first, off, lanes = window_of(r)
        acc = None
        for k in blocks:
            v = dot(
                xg[k, :, first : first + lanes], w1p[k, SHIFT - off : SHIFT - off + lanes, :]
            )
            acc = v if acc is None else acc + v
        return acc

    for r in range(8):
        acc = one_by_one(r, (me, left_i, right_i))
        for t in range(2):
            ynat[t, pl.ds(r, GPAD, stride=8), :] = acc[:, 128 * t : 128 * t + 128]
    for i in range(4):
        pass_on(i).wait_recv()
    for r in range(8):
        acc = one_by_one(r, (far_i,))
        for t in range(2):
            at_ = pl.ds(r, GPAD, stride=8)
            ynat[t, at_, :] = ynat[t, at_, :] + acc[:, 128 * t : 128 * t + 128]
    for i in range(4):
        pass_on(i).wait_send()
        for side in range(2):
            hop(i, side).wait_send()

    def padded(p):
        return (p // SIDE + 1) * 9 + lax.rem(p, SIDE) + 1

    def to_pos(p, carry):
        v = ynat[0, pl.ds(p, ROWS, stride=POS), :]
        ypos[p, :, 0:128] = v
        ypos[p, :, 128:256] = ynat[1, pl.ds(p, ROWS, stride=POS), :]
        mz = v * mask
        box[padded(p)] = mz + prev_t(mz) + next_t(mz)
        return carry

    lax.fori_loop(0, POS, to_pos, 0, unroll=7)

    def spread(p):
        h, w = p // SIDE, lax.rem(p, SIDE)
        acc = jnp.zeros((ROWS, 128), F32)
        for dh in range(3):
            for dw in range(3):
                acc = acc + box[(h + dh) * 9 + w + dw]
        n_h = 3 - (h == 0).astype(jnp.int32) - (h == SIDE - 1).astype(jnp.int32)
        n_w = 3 - (w == 0).astype(jnp.int32) - (w == SIDE - 1).astype(jnp.int32)
        return acc, (n_h * n_w).astype(F32)

    def pool(p, carry):
        s1, s2 = carry
        acc, n = spread(p)
        v = ypos[p]
        v0 = jnp.where(is_pool, acc / jnp.maximum(n_t * n, 1.0), v[:, 0:128])
        v1 = v[:, 128:256]
        ypos[p] = jnp.concatenate([v0, v1], axis=1)
        m0, m1 = v0 * mask, v1 * mask
        return (
            s1 + jnp.concatenate([m0, m1], axis=1),
            s2 + jnp.concatenate([m0 * v0, m1 * v1], axis=1),
        )

    zero256 = jnp.zeros((ROWS, 256), F32)
    zero128 = jnp.zeros((ROWS, 128), F32)
    s1, s2 = lax.fori_loop(0, POS, pool, (zero256, zero256), unroll=7)

    def col(v):
        return jnp.sum(v, axis=0, keepdims=True)

    def pack_rows(rows, count=8):
        fill = [jnp.zeros((1, 128), F32)] * (count - len(rows))
        return jnp.concatenate(list(rows) + fill, axis=0)

    sbuf_a[me_b] = pack_rows(
        [col(s1[:, 0:128]), col(s1[:, 128:256]), col(s2[:, 0:128]), col(s2[:, 128:256]), col(mask)]
    )
    share_start(sbuf_a, me_b, as_, ar)
    cols[...] = jnp.zeros_like(cols)
    for k in range(NC):
        xt[k, :, GPAD:256] = jnp.zeros((GW, 256 - GPAD), BF16)
        xt[k, :, 0:GPAD] = jnp.transpose(xg[k])
    share_wait(sbuf_a, me_b, as_, ar)
    tot = total_of(sbuf_a, NB)
    counted = tot[4:5, :]
    voxels = counted * float(POS)

    def norm_of(sum1, sum2, tile):
        avg = sum1 / voxels
        var = sum2 / voxels - avg * avg
        inv = lax.rsqrt(var + EPS)
        gain = aff_ref[0:1, 128 * tile : 128 * tile + 128]
        bias = aff_ref[1:2, 128 * tile : 128 * tile + 128]
        return avg, var, inv, gain, bias

    n0 = norm_of(tot[0:1], tot[2:3], 0)
    n1 = norm_of(tot[1:2], tot[3:4], 1)

    def forward(y, n):
        normed = (y - n[0]) * n[2]
        pre = n[3] * normed + n[4]
        sig = jax.nn.sigmoid(pre)
        return normed, pre, sig

    def act1(p, carry):
        _, pre, sig = forward(ypos[p][:, 128:256], n1)
        ob[p] = (mask * (pre * sig))
        return carry

    lax.fori_loop(0, POS, act1, 0, unroll=7)
    ob[POS] = zero128

    def to_msg(p, carry):
        got[me, p] = jnp.where(low_half, ob[p], pltpu.roll(ob[p + HALF], 64, 1)).astype(BF16)
        return carry

    lax.fori_loop(0, HALF, to_msg, 0, unroll=5)
    near = 12

    def half(who, low):
        return got.at[who, 0:near] if low else got.at[who, near:HALF]

    ms_c = []
    for i, (low, to) in enumerate([(True, right), (False, left), (False, right), (True, left)]):
        c = send_to(half(me, low), half(me, low), ms.at[i], mr.at[i], to)
        c.start()
        ms_c.append(c)

    def act0(p, carry):
        _, pre, sig = forward(ypos[p][:, 0:128], n0)
        return carry + mask * (pre * sig)

    feat0 = lax.fori_loop(0, POS, act0, zero128, unroll=7)

    def products(width):
        for r in range(8):
            for t in range(width // 128):
                cols[r, 0:GPAD, 128 * t : 128 * t + 128] = dnat[
                    t, pl.ds(r, GPAD, stride=8), :
                ].astype(BF16)
        rhs = cols[:, :, 0:width].reshape(8 * 256, width)
        for k in range(NC):
            lhs = jnp.concatenate([xt[k, CB * r : CB * r + CB, :] for r in range(8)], axis=1)
            yield slice(k * CB, (k + 1) * CB), dot(lhs, rhs)

    def put_late(dst):
        lane104, lane26 = lanes_of((104, 128)), lanes_of((26, 128))
        parts = [(gw1_ref[1, pl.ds(j, 104, stride=8), :], 0, 48 * j, 48) for j in range(8)]
        for i, v in enumerate(joined(parts, lane104, 3)):
            dst[pl.ds(LATE["squeeze"] + i, 104, stride=3), :] = v
        parts = [(gw1_ref[1, pl.ds(j, 26, stride=32), :], 48, 12 * j, 12) for j in range(32)]
        for i, v in enumerate(joined(parts, lane26, 3)):
            dst[pl.ds(LATE["shrink"] + i, 26, stride=3), :] = v

    def late_at(i):
        return pl.ds(pl.multiple_of(i * LATE_ROWS, LATE_ROWS), LATE_ROWS)

    def normed_nat(p, carry):
        normed, _, _ = forward(ypos[p][:, 128:256], n1)
        v = jnp.where(lane < 60, normed * mask, jnp.where(lane == 64, mask, 0.0))
        dnat[0, pl.ds(p, ROWS, stride=POS), :] = v
        return carry

    def early_products():
        lax.fori_loop(0, POS, normed_nat, 0, unroll=7)
        for at_, v in products(128):
            gw1_ref[1, at_, :] = v
        psend[...] = jnp.zeros_like(psend)
        put_late(psend.at[0])
        for k in range(NC):
            at_ = slice(k * CB, (k + 1) * CB)
            gw1_ref[1, at_, :] = jnp.broadcast_to(gw1_ref[1, at_, 64:65], (CB, 128))
        put_late(psend.at[1])

    def early_copy(d):
        to = lax.rem(me_b + d, NB)
        return send_to(psend.at[:, late_at(to)], pgot.at[me_b], ps, pr, batch_peer(me_b, d))

    def early_start():
        def one(d, carry):
            early_copy(d).start()
            return carry

        lax.fori_loop(1, NB, one, 0)
        pgot[me_b] = psend[:, late_at(me_b), :]

    early_products()
    for i, (who, low, to) in enumerate([(left_i, True, right), (right_i, False, left)]):
        ms_c[i].wait_recv()
        c = send_to(half(who, low), half(who, low), ms.at[4 + i], mr.at[4 + i], to)
        c.start()
        ms_c.append(c)
    for c in ms_c[2:]:
        c.wait_recv()

    def unpack(p, carry):
        g = [got[j, p].astype(F32) for j in range(NC)]
        rl = [pltpu.roll(v, 64, 1) for v in g]
        low = jnp.concatenate(
            [jnp.where(low_half, g[0], rl[1]), jnp.where(low_half, g[2], rl[3])], axis=1
        ).astype(BF16)
        apad[padded(p)] = low
        acol[p] = low
        high = jnp.concatenate(
            [jnp.where(low_half, rl[0], g[1]), jnp.where(low_half, rl[2], g[3])], axis=1
        ).astype(BF16)

        @pl.when(p < POS - HALF)
        def _():
            apad[padded(p + HALF)] = high
            acol[p + HALF] = high

        return carry

    lax.fori_loop(0, HALF, unpack, 0, unroll=5)

    early_start()

    def conv(h, carry):
        s1, s2 = carry
        acc = jnp.zeros((SIDE * ROWS, 384), F32)
        for q in range(9):
            dh, dw = divmod(q, 3)
            lhs = apad[pl.ds((h + dh) * 9 + dw, SIDE)].reshape(SIDE * ROWS, 256)
            acc = acc + dot(lhs, wc_ref[q])
        for w in range(SIDE):
            t = acc[w * ROWS : (w + 1) * ROWS]
            y = t[:, 128:256] + prev_t(t[:, 0:128]) + next_t(t[:, 256:384])
            y2[h * SIDE + w] = y
            m = y * mask
            s1 = s1 + m
            s2 = s2 + m * y
        return s1, s2

    s1, s2 = lax.fori_loop(0, SIDE, conv, (zero128, zero128))
    sbuf_b[me_b] = pack_rows([col(s1), col(s2)], 2)
    share_start(sbuf_b, me_b, bs, br)
    at[...] = jnp.transpose(acol[...].reshape(VOX, 256))
    share_wait(sbuf_b, me_b, bs, br)
    totb = total_of(sbuf_b, NB)
    n2 = norm_of(totb[0:1], totb[1:2], 2)

    def act2(p, carry):
        _, pre, sig = forward(y2[p], n2)
        return carry + mask * (pre * sig)

    feat2 = lax.fori_loop(0, POS, act2, zero128, unroll=7)
    feature = (jnp.concatenate([feat0, feat2], axis=1) / float(POS)).astype(BF16)
    lbuf[me] = dot(feature, r_ref[...])
    ls_c = []
    for d in range(1, NC):
        c = send_to(lbuf.at[me], lbuf.at[me], ls.at[d], lr.at[d], chan_peer(me, d))
        c.start()
        ls_c.append(c)
    for c in ls_c:
        c.wait_recv()
    logits = total_of(lbuf, NC)
    cls = lax.broadcasted_iota(jnp.int32, (ROWS, 512), 1)
    row512 = lax.broadcasted_iota(jnp.int32, (ROWS, 512), 0)
    labs = jnp.zeros((ROWS, 512), jnp.int32)
    for i in range(ROWS):
        labs = jnp.where(row512 == i, lab_ref[i % 4, i // 4], labs)
    real = cls < CLASSES
    logits = jnp.where(real, logits, -1e30)
    peak = jnp.max(logits, axis=1, keepdims=True)
    ex = jnp.exp(logits - peak)
    se = jnp.sum(ex, axis=1, keepdims=True)
    logprob = logits - peak - jnp.log(se)
    mask1 = mask[:, 0:1]
    hit = cls == labs
    loss_rows = -jnp.sum(jnp.where(hit, logprob, 0.0), axis=1, keepdims=True) * mask1
    soft = jnp.where(real, jnp.exp(logprob), 0.0)
    dlog = ((soft - hit.astype(F32)) * mask1 / counted[:, 0:1]).astype(BF16)
    dfeat = dot_t(dlog, r_ref[...], 1, 1) / float(POS)
    df0, df2 = dfeat[:, 0:128], dfeat[:, 128:256]

    def back(y, n, dout):
        normed, pre, sig = forward(y, n)
        return dout * mask * sig * (1.0 + pre * (1.0 - sig)), normed

    def back02(p, carry):
        g0, b0, g2, b2 = carry
        d0, m0 = back(ypos[p][:, 0:128], n0, df0)
        d2, m2 = back(y2[p], n2, df2)
        dpre[p] = jnp.concatenate([d0, d2], axis=1)
        return g0 + d0 * m0, b0 + d0, g2 + d2 * m2, b2 + d2

    g0, b0, g2, b2 = lax.fori_loop(0, POS, back02, (zero128,) * 4, unroll=7)
    loss_row = jnp.broadcast_to(jnp.sum(loss_rows, axis=0, keepdims=True), (1, 128))
    sbuf_c[me_b] = pack_rows([col(g0), col(b0), col(g2), col(b2), loss_row])
    share_start(sbuf_c, me_b, cs, cr)
    grr = dot_t(feature, dlog, 0, 0)
    for t in range(4):
        for dst, src, count in ((0, 0, 96), (96, 224, 32), (128, 96, 96), (224, 192, 32)):
            gr[t, src : src + count, :] = grr[dst : dst + count, 128 * t : 128 * t + 128]
    lane32 = lanes_of((32, 128))
    parts = []
    for j in range(8):
        for t in range(4):
            parts.append(
                (gr[t, pl.ds(j, 32, stride=8), :], 0, CLASSES * j + 128 * t,
                 min(128, CLASSES - 128 * t))
            )
    for i, v in enumerate(joined(parts, lane32, 25)):
        g[pl.ds(BULK["readout"] + i, 32, stride=25), :] = v
    for c in ls_c:
        c.wait_send()
    for c in ms_c:
        c.wait_send()
    share_wait(sbuf_c, me_b, cs, cr)
    totc = total_of(sbuf_c, NB)

    def finish(y, n, d, gg, gb):
        normed = (y - n[0]) * n[2]
        return mask * n[3] * n[2] * (d - gb / voxels - normed * gg / voxels)

    def dy2_at(p, carry):
        d = dpre[p]
        v = finish(y2[p], n2, d[:, 128:256], totc[2:3], totc[3:4])
        dypad[padded(p)] = jnp.concatenate([next_t(v), v, prev_t(v)], axis=1).astype(BF16)
        return carry

    lax.fori_loop(0, POS, dy2_at, 0, unroll=7)

    core_i = lax.rem(me_b, 2)
    mate = digit_peer(me_b, 1, 2, 1)
    along = ((2, 8), (8, 2))
    digits = [[digit_of(me_b, along[i][s], 4) for i in range(2)] for s in range(2)]

    class Chunk:
        def __init__(self, index):
            self.base, self.last = CHUNKS[index]
            self.k = index
            self.first = 4 * self.last
            self.group = 4 * self.first
            self.half = 2 * self.group
            self.own = pl.multiple_of(self.base + core_i * self.half, self.last)
            self.r1 = (r1a, r1b)[index]
            self.r2 = (r2a, r2b)[index]
            self.gc = (gca, gcb)[index]

        def rows(self, at, count):
            return pl.ds(pl.multiple_of(at, self.last), count)

        def core_start(self):
            theirs = self.rows(self.base + (1 - core_i) * self.half, self.half)
            self.c0 = send_to(g.at[theirs], self.gc, co_s.at[self.k], co_r.at[self.k], mate)
            self.c0.start()

        def one_start(self):
            self.c0.wait()
            n = self.first

            def add(i, carry):
                at_ = self.rows(i * n, n)
                self.gc[at_, :] = self.gc[at_, :] + g[self.rows(self.own + i * n, n), :]
                return carry

            lax.fori_loop(0, self.half // n, add, 0)
            self.c1 = []
            for i in range(2):
                mine = digits[0][i]
                for d in range(1, 4):
                    to = lax.rem(mine + d, 4)
                    c = send_to(
                        self.gc.at[self.rows(i * self.group + to * self.first, self.first)],
                        self.r1.at[i, mine], s1s.at[self.k, i, d], s1r.at[self.k, i, d],
                        digit_peer(me_b, along[i][0], 4, d),
                    )
                    c.start()
                    self.c1.append(c)
                self.r1[i, mine] = self.gc[
                    self.rows(i * self.group + mine * self.first, self.first), :
                ]

        def two_start(self):
            for c in self.c1:
                c.wait()
            self.c2 = []
            for i in range(2):
                mine = digits[1][i]
                self.r1[i, 0] = total_of(self.r1.at[i], 4)
                for d in range(1, 4):
                    to = lax.rem(mine + d, 4)
                    c = send_to(
                        self.r1.at[i, 0, self.rows(to * self.last, self.last)],
                        self.r2.at[i, mine], s2s.at[self.k, i, d], s2r.at[self.k, i, d],
                        digit_peer(me_b, along[i][1], 4, d),
                    )
                    c.start()
                    self.c2.append(c)
                self.r2[i, mine] = self.r1[i, 0, self.rows(mine * self.last, self.last), :]

        def gather_start(self):
            for c in self.c2:
                c.wait()
            self.c3 = []
            for i in range(2):
                at_ = self.rows(
                    self.own + i * self.group + digits[0][i] * self.first
                    + digits[1][i] * self.last,
                    self.last,
                )
                gb_ref[at_, :] = total_of(self.r2.at[i], 4)
                for d in range(1, 4):
                    c = send_to(
                        gb_ref.at[at_], gb_ref.at[at_], g1s.at[self.k, i, d],
                        g1r.at[self.k, i, d], digit_peer(me_b, along[i][1], 4, d),
                    )
                    c.start()
                    self.c3.append(c)

        def spread_start(self):
            for c in self.c3:
                c.wait()
            self.c4 = []
            self.c5 = []
            for i in range(2):
                mine = digits[0][i]
                at_ = self.rows(self.own + i * self.group + mine * self.first, self.first)
                for d in range(1, 4):
                    c = send_to(
                        gb_ref.at[at_], gb_ref.at[at_], g2s.at[self.k, i, d],
                        g2r.at[self.k, i, d], digit_peer(me_b, along[i][0], 4, d),
                    )
                    c.start()
                    self.c4.append((c, i, d))
                self.mate_start(i, 0)

        def mate_start(self, i, d):
            digit = lax.rem(digits[0][i] - d + 4, 4)
            at_ = self.rows(self.own + i * self.group + digit * self.first, self.first)
            c = send_to(
                gb_ref.at[at_], gb_ref.at[at_], g3s.at[self.k, i, d], g3r.at[self.k, i, d], mate
            )
            c.start()
            self.c5.append(c)

        def mate_rest(self):
            for c, i, d in self.c4:
                c.wait_recv()
                self.mate_start(i, d)

        def finish(self):
            for c, i, d in self.c4:
                c.wait_send()
            for c in self.c5:
                c.wait()

    chip = me_b // 2

    def chip_peer(d):
        return {"batch": lax.rem(chip + d, 16) * 2 + core_i}

    class Direct:
        half = 16 * DIRECT_ROWS

        def rows(self, at_, count=DIRECT_ROWS):
            return pl.ds(pl.multiple_of(at_, DIRECT_ROWS), count)

        def core_start(self):
            theirs = self.rows(DIRECT_AT + (1 - core_i) * self.half, self.half)
            self.c0 = send_to(g.at[theirs], gcc, co_s.at[2], co_r.at[2], mate)
            self.c0.start()

        def one_start(self):
            self.c0.wait()
            own = DIRECT_AT + core_i * self.half
            gcc[...] = gcc[...] + g[self.rows(own, self.half), :]

            def one(d, carry):
                to = lax.rem(chip + d, 16)
                send_to(
                    gcc.at[self.rows(to * DIRECT_ROWS)], rc.at[chip], d1s, d1r, chip_peer(d)
                ).start()
                return carry

            lax.fori_loop(1, 16, one, 0)
            rc[chip] = gcc[self.rows(chip * DIRECT_ROWS), :]

        def all_of(self, send, recv):
            some = rc.at[pl.ds(0, 15)]
            return send_to(some, some, send, recv, chip_peer(1))

        def two_start(self):
            self.all_of(d1s, d1r).wait_recv()
            mine = self.rows(DIRECT_AT + core_i * self.half + chip * DIRECT_ROWS)
            gb_ref[mine, :] = total_of(rc, 16)

            def one(d, carry):
                send_to(gb_ref.at[mine], gb_ref.at[mine], d2s, d2r, chip_peer(d)).start()
                return carry

            lax.fori_loop(1, 16, one, 0)

        def mate_rest(self):
            self.all_of(d2s, d2r).wait_recv()
            mine = self.rows(DIRECT_AT + core_i * self.half, self.half)
            self.c3 = send_to(gb_ref.at[mine], gb_ref.at[mine], d3s, d3r, mate)
            self.c3.start()

        def finish(self):
            self.all_of(d1s, d1r).wait_send()
            self.all_of(d2s, d2r).wait_send()
            self.c3.wait()

    a_, b_, c_ = Chunk(0), Chunk(1), Direct()

    def grad_conv(q, carry):
        dh = q // 3
        dw = q - dh * 3
        rhs = jnp.concatenate(
            [
                dypad[pl.ds((h + 2 - dh) * 9 + 2 - dw, SIDE)].reshape(SIDE * ROWS, 384)
                for h in range(SIDE)
            ],
            axis=0,
        )
        res = dot(at[...], rhs)
        for dt in range(3):
            tap = dt * 9 + q
            for j in range(NC):
                gq[48 * j : 48 * j + 48, :] = res[64 * j : 64 * j + 48, 128 * dt : 128 * dt + 128]
                vn[pl.ds(tap * 48 + 12 * j, 12), :] = res[
                    64 * j + 48 : 64 * j + 60, 128 * dt : 128 * dt + 128
                ]

            def put(i, v, base=tap_rows(dt, q)):
                g[pl.ds(base + i, 48, stride=3), :] = v

            flatten_96(lambda j: gq[pl.ds(j, 48, stride=4), :], 48, put)
        return carry

    lax.fori_loop(0, EARLY_TAPS, grad_conv, 0)
    a_.core_start()
    lax.fori_loop(EARLY_TAPS, 9, grad_conv, 0)
    g[BULK["volume"] : BULK["volume"] + 324, :] = flatten_32(
        lambda j: vn[pl.ds(j, 324, stride=4), :], 324
    )

    b_.core_start()
    a_.one_start()

    def conv_back(h, carry):
        acc = jnp.zeros((SIDE * ROWS, 256), F32)
        for q in range(9):
            dh, dw = divmod(q, 3)
            lhs = dypad[pl.ds((h + 2 - dh) * 9 + 2 - dw, SIDE)].reshape(SIDE * ROWS, 384)
            acc = acc + dot(lhs, wct_ref[q])
        for t in range(2):
            ynat[t, pl.ds(pl.multiple_of(h * SIDE * ROWS, SIDE * ROWS), SIDE * ROWS), :] = acc[
                :, 128 * t : 128 * t + 128
            ]
        return carry

    lax.fori_loop(0, 5, conv_back, 0)
    b_.one_start()
    lax.fori_loop(5, SIDE, conv_back, 0)

    def to_dm(p, carry):
        for j in range(NC):
            a = ynat[j // 2, pl.ds(pl.multiple_of(p * ROWS, ROWS), ROWS), :]
            b = ynat[j // 2, pl.ds(pl.multiple_of((p + HALF) * ROWS, ROWS), ROWS), :]
            if j % 2 == 0:
                dm[j, p] = jnp.where(low_half, a, pltpu.roll(b, 64, 1)).astype(BF16)
            else:
                dm[j, p] = jnp.where(low_half, pltpu.roll(a, 64, 1), b).astype(BF16)
        return carry

    for t in range(2):
        ynat[t, pl.ds(VOX, ROWS), :] = zero128
    lax.fori_loop(0, HALF, to_dm, 0, unroll=5)
    lo_, hi_ = pl.ds(0, near), pl.ds(near, HALF - near)

    def far_copy(i):
        rows_, to = ((lo_, right), (hi_, left))[i]
        return send_to(dm.at[far_i, rows_], dgot.at[2, rows_], ds_.at[i], dr.at[i], to)

    def near_copy(i):
        who, rows_, to, slot = (
            (right_i, hi_, right, 0), (left_i, lo_, left, 1), (right_i, lo_, right, 0),
            (left_i, hi_, left, 1),
        )[i]
        return send_to(
            dm.at[who, rows_], dgot.at[slot, rows_], ds_.at[2 + i], dr.at[2 + i], to
        )

    far_c = [far_copy(i) for i in range(2)]
    near_c = [near_copy(i) for i in range(4)]
    for c in far_c + near_c[0:2]:
        c.start()

    a_.two_start()

    def dy0_at(p, carry):
        v = finish(ypos[p][:, 0:128], n0, dpre[p][:, 0:128], totc[0:1], totc[1:2])
        v = v.astype(BF16).astype(F32)
        h, w = p // SIDE, lax.rem(p, SIDE)
        n_h = 3 - (h == 0).astype(jnp.int32) - (h == SIDE - 1).astype(jnp.int32)
        n_w = 3 - (w == 0).astype(jnp.int32) - (w == SIDE - 1).astype(jnp.int32)
        share = v / jnp.maximum(n_t * (n_h * n_w).astype(F32), 1.0)
        box[padded(p)] = share + prev_t(share) + next_t(share)
        ypos[p, :, 0:128] = v
        return carry

    lax.fori_loop(0, POS, dy0_at, 0, unroll=7)

    def dy0_nat(p, carry):
        acc, _ = spread(p)
        v = jnp.where(is_pool, acc * mask, ypos[p][:, 0:128])
        lowv = v - v.astype(BF16).astype(F32)
        dnat[0, pl.ds(p, ROWS, stride=POS), :] = v
        dnat[1, pl.ds(p, ROWS, stride=POS), :] = lowv
        return carry

    lax.fori_loop(0, POS, dy0_nat, 0, unroll=7)

    for c in far_c:
        c.wait_recv()

    def add_far(p, carry):
        who = jnp.where(p < near, right_i, left_i)
        dm[who, p] = (dm[who, p].astype(F32) + dgot[2, p].astype(F32)).astype(dm.dtype)
        return carry

    lax.fori_loop(0, HALF, add_far, 0, unroll=5)
    for c in near_c[2:4]:
        c.start()
    for at_, v in products(256):
        gw1_ref[0, at_, :] = v[:, 0:128] + v[:, 128:256]

    def put_direct(i, v):
        g[pl.ds(BULK["direct"] + i, 208, stride=3), :] = v

    flatten_96(lambda j: gw1_ref[0, pl.ds(j, 208, stride=4), :], 208, put_direct)
    g[BULK["pooled"] : BULK["pooled"] + 208, :] = flatten_32(
        lambda j: gw1_ref[0, pl.ds(j, 208, stride=4), :], 208
    )

    c_.core_start()
    a_.gather_start()
    b_.two_start()

    for c in near_c:
        c.wait_recv()


    def back1(p, carry):
        g1, b1 = carry
        s = dm[me, p].astype(F32) + dgot[0, p].astype(F32) + dgot[1, p].astype(F32)
        d, m = back(ypos[p][:, 128:256], n1, jnp.where(low_half, s, 0.0))
        ob[p] = d
        g1, b1 = g1 + d * m, b1 + d
        q = jnp.minimum(p + HALF, POS - 1)
        live = (p < POS - HALF).astype(F32)
        d, m = back(ypos[q][:, 128:256], n1, jnp.where(low_half, pltpu.roll(s, 64, 1), 0.0) * live)

        @pl.when(p < POS - HALF)
        def _():
            ob[p + HALF] = d

        return g1 + d * m, b1 + d

    g1, b1 = lax.fori_loop(0, HALF, back1, (zero128, zero128), unroll=5)
    sbuf_d[me_b] = pack_rows([col(g1), col(b1)], 2)
    share_start(sbuf_d, me_b, es, er)

    def dy1_nat(p, carry):
        d = ob[p]
        top = d.astype(BF16).astype(F32)
        dnat[0, pl.ds(p, ROWS, stride=POS), :] = top + pltpu.roll(d - top, 64, 1)
        return carry

    lax.fori_loop(0, POS, dy1_nat, 0, unroll=7)
    for at_, v in products(128):
        gw1_ref[1, at_, :] = v + pltpu.roll(v, 64, 1)
    lsend[pl.ds(384, 128), :] = jnp.zeros((128, 128), F32)
    put_late(lsend)

    def late_copy(d):
        to = lax.rem(me_b + d, NB)
        return send_to(lsend.at[late_at(to)], lgot.at[me_b], fs, fr, batch_peer(me_b, d))

    def late_start(d, carry):
        late_copy(d).start()
        return carry

    lax.fori_loop(1, NB, late_start, 0)
    lgot[me_b] = lsend[late_at(me_b), :]
    for c in far_c + near_c:
        c.wait_send()
    c_.one_start()
    a_.spread_start()
    b_.gather_start()
    share_wait(sbuf_d, me_b, es, er)
    totd = total_of(sbuf_d, NB)

    rowl = lax.broadcasted_iota(jnp.int32, (LATE_ROWS, 128), 0) + me_b * LATE_ROWS
    third = lax.rem(rowl, 3)

    def late_lanes(v):
        lane1 = lanes_of((1, 128))
        sq = joined([(v, 0, 48 * j, 48) for j in range(8)], lane1, 3)
        sh = joined([(v, 48, 12 * j, 12) for j in range(32)], lane1, 3)
        pick = [jnp.where(rowl < LATE["shrink"], a, b) for a, b in zip(sq, sh)]
        return jnp.where(third == 0, pick[0], jnp.where(third == 1, pick[1], pick[2]))

    scale_l = late_lanes(n1[3] * n1[2])
    bias_l = late_lanes(totd[1:2] / voxels)
    gain_l = late_lanes(totd[0:1] / voxels)
    share_wait(pgot, me_b, ps, pr)
    c_.two_start()
    share_wait(lgot, me_b, fs, fr)
    both = total_of(pgot, NB)
    late_ref[me_b] = scale_l * (total_of(lgot, NB) - bias_l * both[1] - gain_l * both[0])
    share_start(late_ref, me_b, hs, hr)
    b_.spread_start()
    a_.mate_rest()
    b_.mate_rest()

    fix = voxels / (voxels - 1.0)
    for tile, n, gg, gb in (
        (0, n0, totc[0:1], totc[1:2]),
        (1, n1, totd[0:1], totd[1:2]),
        (2, n2, totc[2:3], totc[3:4]),
    ):
        st_ref[:, 128 * tile : 128 * tile + 128] = pack_rows([gg, gb, n[0], n[1] * fix])
    sc_ref[...] = pack_rows([totc[4:5], counted])

    for buf, send, recv in (
        (sbuf_a, as_, ar), (sbuf_b, bs, br), (sbuf_c, cs, cr), (sbuf_d, es, er), (lgot, fs, fr),
        (pgot, ps, pr),
    ):
        share_sent(buf, me_b, send, recv)
    c_.mate_rest()
    share_wait(late_ref, me_b, hs, hr)
    share_sent(late_ref, me_b, hs, hr)
    for chunk in (a_, b_, c_):
        chunk.finish()


def core(x, lengths, labels, weights, affine):
    vm = pl.BlockSpec(memory_space=pltpu.VMEM)
    sm = pl.BlockSpec(memory_space=pltpu.SMEM)
    hbm = pl.BlockSpec(memory_space=pltpu.HBM)
    dma = pltpu.SemaphoreType.DMA
    vmem = pltpu.VMEM
    return pl.pallas_call(
        core_kernel,
        out_shape=(
            pltpu.VMEM((BULK_ROWS, 128), F32),
            jax.ShapeDtypeStruct((NB, LATE_ROWS, 128), F32),
            jax.ShapeDtypeStruct((8, 384), F32),
            jax.ShapeDtypeStruct((8, 128), F32),
        ),
        in_specs=[hbm, sm, sm] + [hbm] * 7 + [vm],
        out_specs=(vm,) * 4,
        scratch_shapes=[
            vmem((1, 326144), BF16),
            *[vmem((1, FLAT[n] * 128), F32) for n in NARROW],
            vmem((2, CIN, 128), F32),
            vmem((CIN, 128), F32),
            vmem((R1, 128), F32),
            vmem((1304, 128), F32),
            vmem((4, 256, 128), F32),
            vmem((9, 256, 384), BF16),
            vmem((9, 384, 256), BF16),
            vmem((256, 512), BF16),
            vmem((8, 384), F32),
            vmem((13 * GPAD, 128), F32),
            vmem((NC, GPAD, GW), BF16),
            vmem((NC, GW, 256), BF16),
            vmem((8, 256, 256), BF16),
            vmem((NC, W1_ROWS, 256), BF16),
            vmem((2, 8 * GPAD, 128), F32),
            vmem((POS, ROWS, 256), F32),
            vmem((81, ROWS, 128), F32),
            vmem((POS + 1, ROWS, 128), F32),
            vmem((NC, HALF, ROWS, 128), BF16),
            vmem((81, ROWS, 256), BF16),
            vmem((POS, ROWS, 256), BF16),
            vmem((256, VOX), BF16),
            vmem((POS, ROWS, 128), F32),
            vmem((POS, ROWS, 256), F32),
            vmem((81, ROWS, 384), BF16),
            vmem((NC, HALF, ROWS, 128), BF16),
            vmem((3, HALF, ROWS, 128), BF16),
            vmem((2, 8 * GPAD, 128), F32),
            vmem((2, CIN, 128), F32),
            vmem((R1, 128), F32),
            vmem((4, 256, 128), F32),
            vmem((BULK_ROWS, 128), F32),
            *[vmem((32 * n, 128), F32) for _, n in CHUNKS],
            vmem((16 * DIRECT_ROWS, 128), F32),
            *[vmem((2, 4, 4 * n, 128), F32) for _, n in CHUNKS],
            *[vmem((2, 4, n, 128), F32) for _, n in CHUNKS],
            vmem((16, DIRECT_ROWS, 128), F32),
            vmem((NB * LATE_ROWS, 128), F32),
            vmem((NB, LATE_ROWS, 128), F32),
            vmem((2, NB * LATE_ROWS, 128), F32),
            vmem((NB, 2, LATE_ROWS, 128), F32),
            vmem((NC, ROWS, 512), F32),
            *[vmem((NB, n, 128), F32) for n in (8, 2, 8, 2)],
            dma((4,)), dma((7,)), dma((12,)), dma((12,)),
            dma((6,)), dma((6,)), dma((NC,)), dma((NC,)), dma((6,)), dma((6,)),
            *[dma] * 12,
            dma((3,)), dma((3,)),
            *[dma((2, 2, 4))] * 10,
            *[dma] * 8,
        ],
        compiler_params=pltpu.CompilerParams(
            collective_id=0, has_side_effects=True, vmem_limit_bytes=47 << 20
        ),
        name="block",
    )(x, lengths, labels, *weights, affine)


def unlanes(tiles):
    t0, t1, t2 = tiles
    lane = lanes_of(t0.shape)
    parts = [(t0, 0, 0, 96), (t1, 0, 96, 60), (t0, 96, 156, 32), (t2, 0, 188, 128)]
    return joined(parts, lane, 3)


def adam_kernel(*refs):
    gb, late, st, sc, running = refs[0:5]
    w_in, m_in, v_in = refs[5:13], refs[13:21], refs[21:29]
    m_out, v_out, w_out = refs[29:37], refs[37:45], refs[45:53]
    run_out, loss_out, count_out, copies_out = refs[53:57]
    wb, mb, vb = refs[57:64], refs[64:71], refs[71:78]
    cb, insem, outsem, csem = refs[78:82]
    rates = step_rates()
    parts = []
    for i in ADAM_ORDER:
        parts.append((i, 0, FLAT[NAMES[i]]))
    for first in range(0, FLAT["spatial"], ADAM_ROWS):
        parts.append((2, first, ADAM_ROWS))

    def at_rows(ref, i, first, count):
        if NAMES[i] in NARROW:
            return ref.at[:, pl.ds(first * 128, count * 128)]
        return ref.at[pl.ds(first, count)]

    ins = []
    for n, (i, first, count) in enumerate(parts):
        mine = []
        for kind, (src, dst) in enumerate(((w_in[i], wb[i]), (m_in[i], mb[i]), (v_in[i], vb[i]))):
            if NAMES[i] == "spatial" and kind < 2:
                continue
            c = pltpu.make_async_copy(
                at_rows(src, i, first, count), at_rows(dst, i, first, count), insem.at[n, kind]
            )
            c.start()
            mine.append(c)
        ins.append(mine)

    starts = []
    total = 0
    for name in NAMES:
        starts.append(total * 128)
        total += FLAT[name]
    outs = []
    for n, (i, first, rows) in enumerate(parts):
        name = NAMES[i]
        for c in ins[n]:
            c.wait()

        def step(at, count, i=i, name=name, first=first):
            if name == "spatial":
                tap = at // 144
                row = tap_rows(tap // 9, lax.rem(tap, 9)) + lax.rem(at, 144)
                grad = gb[pl.ds(pl.multiple_of(row, 8), count), :]
            elif name in BULK:
                grad = gb[pl.ds(BULK[name] + at, count), :]
            else:
                grad = late[pl.ds(LATE[name] + at, count), :]
            wide = pl.ds(pl.multiple_of(at * 128, 128), count * 128)
            narrow = name in NARROW

            def load(ref):
                if narrow:
                    return ref[:, wide].reshape(count, 128)
                return ref[pl.ds(at, count), :]

            def store(ref, v):
                if narrow:
                    ref[:, wide] = v.reshape(1, count * 128)
                else:
                    ref[pl.ds(at, count), :] = v

            old = (w_in, m_in, vb) if name == "spatial" else (wb, mb, vb)
            m, v, w = adamw(*(load(group[i]) for group in old), grad, rates[i])
            store(mb[i], m)
            store(vb[i], v)
            store(wb[i], w)
            cb[:, pl.ds(pl.multiple_of(starts[i] + at * 128, 128), count * 128)] = w.astype(
                BF16
            ).reshape(1, count * 128)

        block = {"spatial": 72, "readout": 80, "direct": 48, "pooled": 104, "squeeze": 104}.get(
            name, 24
        )
        loops = rows // block

        def body(j, carry, step=step, block=block, first=first):
            step(pl.multiple_of(first + j * block, 8), block)
            return carry

        lax.fori_loop(0, loops, body, 0, unroll=3)
        at, rest = first + loops * block, rows - loops * block
        if rest // 8:
            step(at, rest // 8 * 8)
        if rest % 8:
            step(at + rest // 8 * 8, rest % 8)
        for kind, (src, dst) in enumerate(((wb[i], w_out[i]), (mb[i], m_out[i]), (vb[i], v_out[i]))):
            c = pltpu.make_async_copy(
                at_rows(src, i, first, rows), at_rows(dst, i, first, rows), outsem.at[n, kind]
            )
            c.start()
            outs.append(c)
        at = pl.ds(starts[i] + first * 128, rows * 128)
        c = pltpu.make_async_copy(cb.at[:, at], copies_out.at[:, at], csem.at[n])
        c.start()
        outs.append(c)

    tiles = [st[:, 128 * t : 128 * t + 128] for t in range(3)]
    for t, v in enumerate(unlanes(tiles)):
        width = min(128, 316 - 128 * t)
        at = slice(128 * t, 128 * t + width)
        v = v[:, 0:width]
        m, s, w = adamw(w_in[7][:, at], m_in[7][:, at], v_in[7][:, at], v[0:2], rates[7])
        m_out[7][:, at] = m
        v_out[7][:, at] = s
        w_out[7][:, at] = w
        run_out[:, at] = MOMENTUM * running[:, at] + (1.0 - MOMENTUM) * v[2:4]
    loss_out[...] = sc[0:1, 0:1]
    count_out[...] = sc[1:2, 0:1]
    for c in outs:
        c.wait()


def adam(gb, late, st, sc, running, masters, firsts, seconds):
    vm = pl.BlockSpec(memory_space=pltpu.VMEM)
    hbm = pl.BlockSpec(memory_space=pltpu.HBM)
    dma = pltpu.SemaphoreType.DMA
    shapes = [(1, FLAT[n] * 128) if n in NARROW else (FLAT[n], 128) for n in NAMES]
    flats = [jax.ShapeDtypeStruct(shape, F32) for shape in shapes]
    small = jax.ShapeDtypeStruct((2, 316), F32)
    total = sum(FLAT[n] for n in NAMES) * 128
    one = jax.ShapeDtypeStruct((1, 1), F32)
    specs = [hbm] * 7 + [vm]
    buffers = [pltpu.VMEM(shape, F32) for shape in shapes]
    count = 6 + FLAT["spatial"] // ADAM_ROWS
    return pl.pallas_call(
        adam_kernel,
        out_shape=[*(flats + [small]) * 3, small, one, one, jax.ShapeDtypeStruct((1, total), BF16)],
        in_specs=[vm] * 5 + ([hbm] * 2 + [vm] + [hbm] * 4 + [vm]) * 2 + specs,
        out_specs=[*specs * 3, vm, vm, vm, hbm],
        scratch_shapes=[
            *buffers * 3, pltpu.VMEM((1, total), BF16), dma((count, 3)), dma((count, 3)), dma((count,)),
        ],
        compiler_params=pltpu.CompilerParams(vmem_limit_bytes=20 << 20),
        name="adamw",
    )(gb, late, st, sc, running, *masters, *firsts, *seconds)


def per_device(
    features, lengths, labels, direct, squeeze, spatial, shrink, volume, pooled, readout, affine,
    first_direct, first_squeeze, first_spatial, first_shrink, first_volume, first_pooled,
    first_readout, first_affine, second_direct, second_squeeze, second_spatial, second_shrink,
    second_volume, second_pooled, second_readout, second_affine, running,
):
    masters = [direct, squeeze, spatial, shrink, volume, pooled, readout, affine]
    firsts = [
        first_direct, first_squeeze, first_spatial, first_shrink, first_volume, first_pooled,
        first_readout, first_affine,
    ]
    seconds = [
        second_direct, second_squeeze, second_spatial, second_shrink, second_volume,
        second_pooled, second_readout, second_affine,
    ]
    def rows(flat, name):
        return flat if name in NARROW else flat.reshape(-1, 128)

    masters, firsts, seconds = (
        [rows(a, n) for a, n in zip(group, NAMES)] + [group[7]]
        for group in (masters, firsts, seconds)
    )
    def put(arrays, space):
        return [pltpu.with_memory_space_constraint(a, space) for a in arrays]

    x, lens, labs, aff = put([features, lengths, labels.T, affine], pltpu.HBM)
    gb, late, st, sc = core(x, lens, labs, put(masters[:7], pltpu.HBM), aff)
    (gb,) = put([gb], pltpu.VMEM)
    masters, firsts, seconds = (
        put(group[:2], pltpu.HBM) + put(group[2:3], space) + put(group[3:7], pltpu.HBM)
        + [group[7]]
        for group, space in ((masters, pltpu.VMEM), (firsts, pltpu.VMEM), (seconds, pltpu.HBM))
    )
    out = adam(gb, late.reshape(NB * LATE_ROWS, 128), st, sc, running, masters, firsts, seconds)
    flat_out = [a if i % 8 == 7 else a.reshape(1, -1) for i, a in enumerate(out[:24])]
    return (*flat_out, out[24], out[25].reshape(()), out[26].reshape(()), out[27])


def solution(mesh):
    flat = P("chan", None)
    wide = P(None, "chan")
    weights = (flat,) * 7 + (wide,)
    return jax.shard_map(
        per_device,
        mesh=mesh,
        in_specs=(P("chan", "batch"), P("batch"), P("batch", None)) + weights * 3 + (wide,),
        out_specs=weights * 3 + (wide, P(), P(), flat),
        check_vma=False,
    )
```

```python
import math
from functools import partial

import jax
import jax.numpy as jnp
from jax import lax
from jax.experimental import pallas as pl
from jax.experimental.pallas import tpu as pltpu
from jax.sharding import PartitionSpec as P

CIN = 832
B0 = 384
R1 = 192
O1 = 384
R2 = 48
O2 = 128
B3 = 128
CLASSES = 400
SIDE = 7
STEP = 5
NC = 4
NB = 32
POS = SIDE * SIDE
ROWS = 32
VOX = POS * ROWS
GROUPS = VOX // 8
GPAD = 208
CB = CIN // NC
GW = 8 * CB
HALF = 25
SHIFT = 112
W1_ROWS = 448
TAPS = 27
FLAT = {"direct": 624, "squeeze": 312, "spatial": 3888, "shrink": 78, "volume": 324, "pooled": 208,
        "readout": 800}
NAMES = ("direct", "squeeze", "spatial", "shrink", "volume", "pooled", "readout")
HELD = {"spatial": 0, "volume": 3888, "direct": 4216, "pooled": 4840, "readout": 5048}
BULK = {"volume": 4720, "direct": 5120, "pooled": 5744, "readout": 1728}
EARLY_TAPS = 4
NARROW = ("shrink", "volume")
LATE = {"squeeze": 0, "shrink": 312}
CHUNKS = ((0, 40), (2560, 40))
DIRECT_AT = 5120
DIRECT_ROWS = 32
BULK_ROWS = 6144
LATE_ROWS = 16
ADAM_ROWS = 648
ADAM_ORDER = (3, 1, 5, 0, 6, 4)

EPS = 1e-05
BETA_ONE = 0.5
BETA_TWO = 0.5
DECAY = 0.01
MOMENTUM = 0.99

MESH = pl.DeviceIdType.MESH
F32 = jnp.float32
BF16 = jnp.bfloat16


def step_rates():
    return [
        1.5 / math.sqrt(CIN),
        1.5 / math.sqrt(CIN),
        1.5 / math.sqrt(27 * R1),
        1.5 / math.sqrt(CIN),
        1.5 / math.sqrt(27 * R2),
        1.5 / math.sqrt(CIN),
        0.2,
        0.3,
    ]


def adamw(weight, moment_one, moment_two, gradient, step_rate):
    first_new = BETA_ONE * moment_one + (1.0 - BETA_ONE) * gradient
    second_new = BETA_TWO * moment_two + (1.0 - BETA_TWO) * (gradient * gradient)
    scale_one = step_rate / (1.0 - BETA_ONE**STEP)
    scale_two = 1.0 / (1.0 - BETA_TWO**STEP)
    weight_new = weight * (1.0 - step_rate * DECAY) - scale_one * first_new / (
        jnp.sqrt(second_new * scale_two) + 1e-08
    )
    return (first_new, second_new, weight_new)


def window_of(r):
    start = CB * r
    tile, offset = divmod(start, 128)
    lanes = 256 if offset + CB <= 256 else 384
    return tile * 128, offset, lanes


def dot(a, b):
    return jnp.dot(a, b, preferred_element_type=F32)


def dot_t(a, b, ca, cb):
    return lax.dot_general(a, b, (((ca,), (cb,)), ((), ())), preferred_element_type=F32)


def send_to(src, dst, send, recv, target):
    return pltpu.make_async_remote_copy(
        src_ref=src, dst_ref=dst, send_sem=send, recv_sem=recv, device_id=target,
        device_id_type=MESH,
    )


def batch_peer(me, d):
    return {"batch": lax.rem(me + d, NB)}


def chan_peer(me, d):
    return {"chan": lax.rem(me + d, NC)}


def share_start(buf, me, send, recv):
    def one(d, carry):
        send_to(buf.at[me], buf.at[me], send, recv, batch_peer(me, d)).start()
        return carry

    lax.fori_loop(1, NB, one, 0)


def share_copy(buf, me, send, recv):
    others = buf.at[pl.ds(0, NB - 1)]
    return send_to(others, others, send, recv, batch_peer(me, 1))


def share_wait(buf, me, send, recv):
    share_copy(buf, me, send, recv).wait_recv()


def share_sent(buf, me, send, recv):
    share_copy(buf, me, send, recv).wait_send()


def digit_of(me, stride, size):
    return lax.rem(me // stride, size)


def digit_peer(me, stride, size, d):
    digit = digit_of(me, stride, size)
    return {"batch": me + stride * (lax.rem(digit + d, size) - digit)}


def piece(tiles, start, width, dest, lane):
    tile, off = divmod(start, 128)
    v = tiles[tile]
    if off + width > 128:
        v = jnp.where(lane >= off, v, tiles[tile + 1])
    shift = (dest - off) % 128
    return pltpu.roll(v, shift, 1) if shift else v


def joined(parts, lane, count):
    out = []
    moved = []
    for value, src, start, width in parts:
        shift = (start - src) % 128
        moved.append((pltpu.roll(value, shift, 1) if shift else value, start, width))
    for i in range(count):
        acc = None
        for value, start, width in moved:
            lo, hi = max(0, start - 128 * i), min(128, start + width - 128 * i)
            if lo < hi:
                acc = value if acc is None else jnp.where(lane >= lo, value, acc)
        out.append(acc)
    return out


def lanes_of(v):
    return lax.broadcasted_iota(jnp.int32, v, 1)


def tap_rows(dt, q):
    return q * 432 + jnp.where(q >= EARLY_TAPS, 832, 0) + dt * 144


def prepare_w1(flat, wn, wk, w1p):
    lane = lanes_of((208, 128))
    tiles = [flat["direct"][pl.ds(i, 208, stride=3), :] for i in range(3)]
    pool = flat["pooled"][...]
    for j in range(4):
        v = jnp.where(
            lane < 96, piece(tiles, 96 * j, 96, 0, lane), piece([pool], 32 * j, 32, 96, lane)
        )
        wn[0, pl.ds(j, 208, stride=4), :] = v
    lane = lanes_of((104, 128))
    tiles = [flat["squeeze"][pl.ds(i, 104, stride=3), :] for i in range(3)]
    for j in range(8):
        wn[1, pl.ds(j, 104, stride=8), :] = piece(tiles, 48 * j, 48, 0, lane)
    lane = lanes_of((26, 128))
    tiles = [flat["shrink"][pl.ds(i, 26, stride=3), :] for i in range(3)]
    for j in range(32):
        wk[pl.ds(j, 26, stride=32), :] = piece(tiles, 12 * j, 12, 48, lane)
    lane = lanes_of((CB, 128))
    for k in range(NC):
        rows = slice(k * CB, (k + 1) * CB)
        second = jnp.where(lane < 48, wn[1, rows, :], jnp.where(lane < 60, wk[rows, :], 0.0))
        both = jnp.concatenate([wn[0, rows, :], second], axis=1).astype(BF16)
        w1p[k, 0:SHIFT, :] = jnp.zeros((SHIFT, 256), BF16)
        w1p[k, SHIFT : SHIFT + CB, :] = both
        w1p[k, SHIFT + CB : W1_ROWS, :] = jnp.zeros((W1_ROWS - SHIFT - CB, 256), BF16)


def prepare_conv(flat, tb, vn, wc, wct):
    lane = lanes_of((324, 128))
    for j in range(4):
        v = piece([flat["volume"][...]], 32 * j, 32, 96, lane)
        vn[pl.ds(j, 324, stride=4), :] = jnp.where(lane >= 96, v, 0.0)
    vn[pl.ds(1296, 8), :] = jnp.zeros((8, 128), F32)
    lane48 = lanes_of((48, 128))
    row16 = lax.broadcasted_iota(jnp.int32, (16, 128), 0)

    def one(q, carry):
        for dt in range(3):
            tap = dt * 9 + q
            tiles = [
                flat["spatial"][pl.ds(tap * 144 + i, 48, stride=3), :] for i in range(3)
            ]
            for j in range(4):
                v = piece(tiles, 96 * j, 96, 0, lane48)
                tb[pl.ds(j, 48, stride=4), :] = jnp.where(lane48 < 96, v, 0.0)
            for j in range(NC):
                at = slice(128 * dt, 128 * dt + 128)
                wc[q, 64 * j : 64 * j + 48, at] = tb[48 * j : 48 * j + 48, :].astype(BF16)
                v = vn[pl.ds(tap * 48 + 12 * j, 16), :]
                wc[q, 64 * j + 48 : 64 * j + 64, at] = jnp.where(row16 < 12, v, 0.0).astype(BF16)
        wct[q] = jnp.transpose(wc[q])
        return carry

    lax.fori_loop(0, 9, one, 0)


def prepare_readout(flat, rn, rp):
    lane = lanes_of((32, 128))
    tiles = [flat["readout"][pl.ds(i, 32, stride=25), :] for i in range(25)]
    for t in range(4):
        width = min(128, CLASSES - 128 * t)
        for j in range(8):
            v = piece(tiles, CLASSES * j + 128 * t, width, 0, lane)
            rn[t, pl.ds(j, 32, stride=8), :] = v if width == 128 else jnp.where(lane < width, v, 0.0)
        at = slice(128 * t, 128 * t + 128)
        for dst, src, count in ((0, 0, 96), (96, 224, 32), (128, 96, 96), (224, 192, 32)):
            rp[dst : dst + count, at] = rn[t, src : src + count, :].astype(BF16)


def prepare_affine(aff, out):
    a = [aff[:, 0:128], aff[:, 128:256]]
    a.append(jnp.concatenate([aff[:, 256:316], jnp.zeros((2, 68), F32)], axis=1))
    lane = lanes_of((2, 128))
    t0 = jnp.where(lane < 96, a[0], piece(a, 156, 32, 96, lane))
    t1 = jnp.where(lane < 60, piece(a, 96, 60, 0, lane), 0.0)
    t2 = piece(a, 188, 128, 0, lane)
    for i, t in enumerate((t0, t1, t2)):
        out[0:2, 128 * i : 128 * i + 128] = t


def flatten_96(src, rows, put):
    lane = lanes_of((rows, 128))
    for i, v in enumerate(joined([(src(j), 0, 96 * j, 96) for j in range(4)], lane, 3)):
        put(i, v)


def flatten_32(src, rows):
    lane = lanes_of((rows, 128))
    return joined([(src(j), 96, 32 * j, 32) for j in range(4)], lane, 1)[0]


def total_of(buf, count):
    acc = buf[0]
    for slot in range(1, count):
        acc = acc + buf[slot]
    return acc


def core_kernel(
    x_hbm, len_ref, lab_ref, direct_hbm, squeeze_hbm, spatial_hbm, shrink_hbm, volume_hbm,
    pooled_hbm, readout_hbm, affine_ref,
    gb_ref, late_ref, st_ref, sc_ref,
    x_ref, n_shrink, n_volume,
    wn, wk, tb, vn, rn, wc_ref, wct_ref, r_ref, aff_ref,
    xf, xg, xt, cols, w1p, ynat, ypos, box, ob, got, apad, acol, at, y2, dpre, dypad, dm, dgot, dnat,
    gw1_ref, gq, gr, g, gca, gcb, gcc, r1a, r1b, r2a, r2b, rc, lsend, lgot, psend, pgot,
    lbuf, sbuf_a, sbuf_b, sbuf_c, sbuf_d,
    xin, win, xs, xr, ms, mr, ls, lr, ds_, dr,
    as_, ar, bs, br, cs, cr, es, er, fs, fr, hs, hr,
    co_s, co_r, s1s, s1r, s2s, s2r, g1sa, g1sb, g1ra, g1rb, g3s, g3r, ps, pr, d1s, d1r, d2s, d2r, d3s, d3r,
):
    me_b = lax.axis_index("batch")
    me = lax.axis_index("chan")

    barrier = pltpu.get_barrier_semaphore()

    loops = (0, 104, 182, 260, 318)
    cuts = [1024 * n for n in loops[:4]] + [326144]
    x_in = []
    for i in range(4):
        at_ = pl.ds(cuts[i], cuts[i + 1] - cuts[i])
        c = pltpu.make_async_copy(x_hbm.at[:, at_], x_ref.at[:, at_], xin.at[i])
        c.start()
        x_in.append(c)
    flat = {n: g.at[at_ : at_ + FLAT[n]] for n, at_ in HELD.items()}
    flat.update({n: lsend.at[at_ : at_ + FLAT[n]] for n, at_ in LATE.items()})
    w_in = []
    for i, (src, name) in enumerate(
        zip(
            (direct_hbm, squeeze_hbm, spatial_hbm, shrink_hbm, volume_hbm, pooled_hbm, readout_hbm),
            NAMES,
        )
    ):
        dst = {"shrink": n_shrink, "volume": n_volume}.get(name, flat[name])
        c = pltpu.make_async_copy(src, dst, win.at[i])
        c.start()
        w_in.append(c)

    def greet(d, carry):
        pl.semaphore_signal(barrier, inc=1, device_id=batch_peer(me_b, d), device_id_type=MESH)
        return carry

    lax.fori_loop(1, NB, greet, 0)
    for d in range(1, NC):
        pl.semaphore_signal(barrier, inc=1, device_id=chan_peer(me, d), device_id_type=MESH)

    def flat_rows(i, carry):
        v = x_ref[:, pl.ds(pl.multiple_of(i * 1024, 1024), 1024)].astype(F32)
        xf[pl.ds(pl.multiple_of(i * 8, 8), 8), :] = v.reshape(8, 128)
        return carry

    right, left = chan_peer(me, 1), chan_peer(me, NC - 1)
    left_i, right_i = lax.rem(me + NC - 1, NC), lax.rem(me + 1, NC)
    bounds = (0, 64, 112, 160, GPAD)

    def part(who, i):
        return xg.at[who, bounds[i] : bounds[i + 1]]

    def hop(i, side):
        return send_to(
            part(me, i), part(me, i), xs.at[4 * side + i], xr.at[4 * side + i], (right, left)[side]
        )

    def pass_on(i):
        who, to = ((left_i, right), (right_i, left))[i // 2]
        return send_to(part(who, i), part(who, i), xs.at[8 + i], xr.at[8 + i], to)

    xf[pl.ds(2548, 2704 - 2548), :] = jnp.zeros((2704 - 2548, 128), F32)
    for i in range(4):
        x_in[i].wait()
        lax.fori_loop(loops[i], loops[i + 1], flat_rows, 0, unroll=(8, 6, 6, 2)[i])
        if i == 3:
            xf[pl.ds(2544, 4), :] = x_ref[:, 318 * 1024 : 318 * 1024 + 512].astype(F32).reshape(
                4, 128
            )
        low, count = bounds[i], bounds[i + 1] - bounds[i]
        for t in range(13):
            xg[me, low : low + count, 128 * t : 128 * t + 128] = xf[
                pl.ds(13 * low + t, count, stride=13), :
            ].astype(BF16)
        if i == 0:
            pl.semaphore_wait(barrier, NB - 1 + NC - 1)
        for side in range(2):
            hop(i, side).start()

    rowi = lax.broadcasted_iota(jnp.int32, (ROWS, 128), 0)
    lane = lax.broadcasted_iota(jnp.int32, (ROWS, 128), 1)
    clip = rowi // 4
    step = rowi - clip * 4
    lens = jnp.zeros((ROWS, 128), jnp.int32)
    for c in range(8):
        lens = jnp.where(clip == c, len_ref[c], lens)
    mask = (step < lens).astype(F32)
    has_prev = (step > 0).astype(F32)
    has_next = (step < 3).astype(F32)

    def prev_t(v):
        return pltpu.roll(v, 1, 0) * has_prev

    def next_t(v):
        return pltpu.roll(v, ROWS - 1, 0) * has_next

    n_t = mask + prev_t(mask) + next_t(mask)
    is_pool = lane >= 96
    low_half = lane < 64

    for c in w_in:
        c.wait()
    for src, dst in ((n_shrink, flat["shrink"]), (n_volume, flat["volume"])):
        count = dst.shape[0]
        whole = count // 8 * 8
        dst[0:whole, :] = src[:, 0 : whole * 128].reshape(whole, 128)
        dst[whole:count, :] = src[:, whole * 128 : count * 128].reshape(count - whole, 128)
    prepare_w1(flat, wn, wk, w1p)
    prepare_affine(affine_ref, aff_ref)
    prepare_readout(flat, rn, r_ref)

    def zero_pad(i, carry):
        apad[i] = jnp.zeros((ROWS, 256), BF16)
        dypad[i] = jnp.zeros((ROWS, 384), BF16)
        box[i] = jnp.zeros((ROWS, 128), F32)
        return carry

    lax.fori_loop(0, 81, zero_pad, 0, unroll=9)
    dnat[...] = jnp.zeros_like(dnat)
    prepare_conv(flat, tb, vn, wc_ref, wct_ref)

    for i in range(4):
        hop(i, i // 2).wait_recv()
        pass_on(i).start()
    for i in range(4):
        hop(i, 1 - i // 2).wait_recv()

    far_i = lax.rem(me + 2, NC)

    def one_by_one(r, blocks):
        first, off, lanes = window_of(r)
        acc = None
        for k in blocks:
            v = dot(
                xg[k, :, first : first + lanes], w1p[k, SHIFT - off : SHIFT - off + lanes, :]
            )
            acc = v if acc is None else acc + v
        return acc

    for r in range(8):
        acc = one_by_one(r, (me, left_i, right_i))
        for t in range(2):
            ynat[t, pl.ds(r, GPAD, stride=8), :] = acc[:, 128 * t : 128 * t + 128]
    for i in range(4):
        pass_on(i).wait_recv()
    for r in range(8):
        acc = one_by_one(r, (far_i,))
        for t in range(2):
            at_ = pl.ds(r, GPAD, stride=8)
            ynat[t, at_, :] = ynat[t, at_, :] + acc[:, 128 * t : 128 * t + 128]
    for i in range(4):
        pass_on(i).wait_send()
        for side in range(2):
            hop(i, side).wait_send()

    def padded(p):
        return (p // SIDE + 1) * 9 + lax.rem(p, SIDE) + 1

    def to_pos(p, carry):
        v = ynat[0, pl.ds(p, ROWS, stride=POS), :]
        ypos[p, :, 0:128] = v
        ypos[p, :, 128:256] = ynat[1, pl.ds(p, ROWS, stride=POS), :]
        mz = v * mask
        box[padded(p)] = mz + prev_t(mz) + next_t(mz)
        return carry

    lax.fori_loop(0, POS, to_pos, 0, unroll=7)

    def spread(p):
        h, w = p // SIDE, lax.rem(p, SIDE)
        acc = jnp.zeros((ROWS, 128), F32)
        for dh in range(3):
            for dw in range(3):
                acc = acc + box[(h + dh) * 9 + w + dw]
        n_h = 3 - (h == 0).astype(jnp.int32) - (h == SIDE - 1).astype(jnp.int32)
        n_w = 3 - (w == 0).astype(jnp.int32) - (w == SIDE - 1).astype(jnp.int32)
        return acc, (n_h * n_w).astype(F32)

    def pool(p, carry):
        s1, s2 = carry
        acc, n = spread(p)
        v = ypos[p]
        v0 = jnp.where(is_pool, acc / jnp.maximum(n_t * n, 1.0), v[:, 0:128])
        v1 = v[:, 128:256]
        ypos[p] = jnp.concatenate([v0, v1], axis=1)
        m0, m1 = v0 * mask, v1 * mask
        return (
            s1 + jnp.concatenate([m0, m1], axis=1),
            s2 + jnp.concatenate([m0 * v0, m1 * v1], axis=1),
        )

    zero256 = jnp.zeros((ROWS, 256), F32)
    zero128 = jnp.zeros((ROWS, 128), F32)
    s1, s2 = lax.fori_loop(0, POS, pool, (zero256, zero256), unroll=7)

    def col(v):
        return jnp.sum(v, axis=0, keepdims=True)

    def pack_rows(rows, count=8):
        fill = [jnp.zeros((1, 128), F32)] * (count - len(rows))
        return jnp.concatenate(list(rows) + fill, axis=0)

    sbuf_a[me_b] = pack_rows(
        [col(s1[:, 0:128]), col(s1[:, 128:256]), col(s2[:, 0:128]), col(s2[:, 128:256]), col(mask)]
    )
    share_start(sbuf_a, me_b, as_, ar)
    cols[...] = jnp.zeros_like(cols)
    for k in range(NC):
        xt[k, :, GPAD:256] = jnp.zeros((GW, 256 - GPAD), BF16)
        xt[k, :, 0:GPAD] = jnp.transpose(xg[k])
    share_wait(sbuf_a, me_b, as_, ar)
    tot = total_of(sbuf_a, NB)
    counted = tot[4:5, :]
    voxels = counted * float(POS)

    def norm_of(sum1, sum2, tile):
        avg = sum1 / voxels
        var = sum2 / voxels - avg * avg
        inv = lax.rsqrt(var + EPS)
        gain = aff_ref[0:1, 128 * tile : 128 * tile + 128]
        bias = aff_ref[1:2, 128 * tile : 128 * tile + 128]
        return avg, var, inv, gain, bias

    n0 = norm_of(tot[0:1], tot[2:3], 0)
    n1 = norm_of(tot[1:2], tot[3:4], 1)

    def forward(y, n):
        normed = (y - n[0]) * n[2]
        pre = n[3] * normed + n[4]
        sig = jax.nn.sigmoid(pre)
        return normed, pre, sig

    def act1(p, carry):
        _, pre, sig = forward(ypos[p][:, 128:256], n1)
        ob[p] = (mask * (pre * sig))
        return carry

    lax.fori_loop(0, POS, act1, 0, unroll=7)
    ob[POS] = zero128

    def to_msg(p, carry):
        got[me, p] = jnp.where(low_half, ob[p], pltpu.roll(ob[p + HALF], 64, 1)).astype(BF16)
        return carry

    lax.fori_loop(0, HALF, to_msg, 0, unroll=5)
    near = 12

    def half(who, low):
        return got.at[who, 0:near] if low else got.at[who, near:HALF]

    ms_c = []
    for i, (low, to) in enumerate([(True, right), (False, left), (False, right), (True, left)]):
        c = send_to(half(me, low), half(me, low), ms.at[i], mr.at[i], to)
        c.start()
        ms_c.append(c)

    def act0(p, carry):
        _, pre, sig = forward(ypos[p][:, 0:128], n0)
        return carry + mask * (pre * sig)

    feat0 = lax.fori_loop(0, POS, act0, zero128, unroll=7)

    def products(width):
        for r in range(8):
            for t in range(width // 128):
                cols[r, 0:GPAD, 128 * t : 128 * t + 128] = dnat[
                    t, pl.ds(r, GPAD, stride=8), :
                ].astype(BF16)
        rhs = cols[:, :, 0:width].reshape(8 * 256, width)
        for k in range(NC):
            lhs = jnp.concatenate([xt[k, CB * r : CB * r + CB, :] for r in range(8)], axis=1)
            yield slice(k * CB, (k + 1) * CB), dot(lhs, rhs)

    def put_late(dst):
        lane104, lane26 = lanes_of((104, 128)), lanes_of((26, 128))
        parts = [(gw1_ref[1, pl.ds(j, 104, stride=8), :], 0, 48 * j, 48) for j in range(8)]
        for i, v in enumerate(joined(parts, lane104, 3)):
            dst[pl.ds(LATE["squeeze"] + i, 104, stride=3), :] = v
        parts = [(gw1_ref[1, pl.ds(j, 26, stride=32), :], 48, 12 * j, 12) for j in range(32)]
        for i, v in enumerate(joined(parts, lane26, 3)):
            dst[pl.ds(LATE["shrink"] + i, 26, stride=3), :] = v

    def late_at(i):
        return pl.ds(pl.multiple_of(i * LATE_ROWS, LATE_ROWS), LATE_ROWS)

    def normed_nat(p, carry):
        normed, _, _ = forward(ypos[p][:, 128:256], n1)
        v = jnp.where(lane < 60, normed * mask, jnp.where(lane == 64, mask, 0.0))
        dnat[0, pl.ds(p, ROWS, stride=POS), :] = v
        return carry

    def early_products():
        lax.fori_loop(0, POS, normed_nat, 0, unroll=7)
        for at_, v in products(128):
            gw1_ref[1, at_, :] = v
        psend[...] = jnp.zeros_like(psend)
        put_late(psend.at[0])
        for k in range(NC):
            at_ = slice(k * CB, (k + 1) * CB)
            gw1_ref[1, at_, :] = jnp.broadcast_to(gw1_ref[1, at_, 64:65], (CB, 128))
        put_late(psend.at[1])

    def early_copy(d):
        to = lax.rem(me_b + d, NB)
        return send_to(psend.at[:, late_at(to)], pgot.at[me_b], ps, pr, batch_peer(me_b, d))

    def early_start():
        def one(d, carry):
            early_copy(d).start()
            return carry

        lax.fori_loop(1, NB, one, 0)
        pgot[me_b] = psend[:, late_at(me_b), :]

    early_products()
    for i, (who, low, to) in enumerate([(left_i, True, right), (right_i, False, left)]):
        ms_c[i].wait_recv()
        c = send_to(half(who, low), half(who, low), ms.at[4 + i], mr.at[4 + i], to)
        c.start()
        ms_c.append(c)
    for c in ms_c[2:]:
        c.wait_recv()

    def unpack(p, carry):
        g = [got[j, p].astype(F32) for j in range(NC)]
        rl = [pltpu.roll(v, 64, 1) for v in g]
        low = jnp.concatenate(
            [jnp.where(low_half, g[0], rl[1]), jnp.where(low_half, g[2], rl[3])], axis=1
        ).astype(BF16)
        apad[padded(p)] = low
        acol[p] = low
        high = jnp.concatenate(
            [jnp.where(low_half, rl[0], g[1]), jnp.where(low_half, rl[2], g[3])], axis=1
        ).astype(BF16)

        @pl.when(p < POS - HALF)
        def _():
            apad[padded(p + HALF)] = high
            acol[p + HALF] = high

        return carry

    lax.fori_loop(0, HALF, unpack, 0, unroll=5)

    early_start()

    def conv(h, carry):
        s1, s2 = carry
        acc = jnp.zeros((SIDE * ROWS, 384), F32)
        for q in range(9):
            dh, dw = divmod(q, 3)
            lhs = apad[pl.ds((h + dh) * 9 + dw, SIDE)].reshape(SIDE * ROWS, 256)
            acc = acc + dot(lhs, wc_ref[q])
        for w in range(SIDE):
            t = acc[w * ROWS : (w + 1) * ROWS]
            y = t[:, 128:256] + prev_t(t[:, 0:128]) + next_t(t[:, 256:384])
            y2[h * SIDE + w] = y
            m = y * mask
            s1 = s1 + m
            s2 = s2 + m * y
        return s1, s2

    s1, s2 = lax.fori_loop(0, SIDE, conv, (zero128, zero128))
    sbuf_b[me_b] = pack_rows([col(s1), col(s2)], 2)
    share_start(sbuf_b, me_b, bs, br)
    at[...] = jnp.transpose(acol[...].reshape(VOX, 256))
    share_wait(sbuf_b, me_b, bs, br)
    totb = total_of(sbuf_b, NB)
    n2 = norm_of(totb[0:1], totb[1:2], 2)

    def act2(p, carry):
        _, pre, sig = forward(y2[p], n2)
        return carry + mask * (pre * sig)

    feat2 = lax.fori_loop(0, POS, act2, zero128, unroll=7)
    feature = (jnp.concatenate([feat0, feat2], axis=1) / float(POS)).astype(BF16)
    lbuf[me] = dot(feature, r_ref[...])
    ls_c = []
    for d in range(1, NC):
        c = send_to(lbuf.at[me], lbuf.at[me], ls.at[d], lr.at[d], chan_peer(me, d))
        c.start()
        ls_c.append(c)
    for c in ls_c:
        c.wait_recv()
    logits = total_of(lbuf, NC)
    cls = lax.broadcasted_iota(jnp.int32, (ROWS, 512), 1)
    row512 = lax.broadcasted_iota(jnp.int32, (ROWS, 512), 0)
    labs = jnp.zeros((ROWS, 512), jnp.int32)
    for i in range(ROWS):
        labs = jnp.where(row512 == i, lab_ref[i % 4, i // 4], labs)
    real = cls < CLASSES
    logits = jnp.where(real, logits, -1e30)
    peak = jnp.max(logits, axis=1, keepdims=True)
    ex = jnp.exp(logits - peak)
    se = jnp.sum(ex, axis=1, keepdims=True)
    logprob = logits - peak - jnp.log(se)
    mask1 = mask[:, 0:1]
    hit = cls == labs
    loss_rows = -jnp.sum(jnp.where(hit, logprob, 0.0), axis=1, keepdims=True) * mask1
    soft = jnp.where(real, jnp.exp(logprob), 0.0)
    dlog = ((soft - hit.astype(F32)) * mask1 / counted[:, 0:1]).astype(BF16)
    dfeat = dot_t(dlog, r_ref[...], 1, 1) / float(POS)
    df0, df2 = dfeat[:, 0:128], dfeat[:, 128:256]

    def back(y, n, dout):
        normed, pre, sig = forward(y, n)
        return dout * mask * sig * (1.0 + pre * (1.0 - sig)), normed

    def back02(p, carry):
        g0, b0, g2, b2 = carry
        d0, m0 = back(ypos[p][:, 0:128], n0, df0)
        d2, m2 = back(y2[p], n2, df2)
        dpre[p] = jnp.concatenate([d0, d2], axis=1)
        return g0 + d0 * m0, b0 + d0, g2 + d2 * m2, b2 + d2

    g0, b0, g2, b2 = lax.fori_loop(0, POS, back02, (zero128,) * 4, unroll=7)
    loss_row = jnp.broadcast_to(jnp.sum(loss_rows, axis=0, keepdims=True), (1, 128))
    sbuf_c[me_b] = pack_rows([col(g0), col(b0), col(g2), col(b2), loss_row])
    share_start(sbuf_c, me_b, cs, cr)
    grr = dot_t(feature, dlog, 0, 0)
    for t in range(4):
        for dst, src, count in ((0, 0, 96), (96, 224, 32), (128, 96, 96), (224, 192, 32)):
            gr[t, src : src + count, :] = grr[dst : dst + count, 128 * t : 128 * t + 128]
    lane32 = lanes_of((32, 128))
    parts = []
    for j in range(8):
        for t in range(4):
            parts.append(
                (gr[t, pl.ds(j, 32, stride=8), :], 0, CLASSES * j + 128 * t,
                 min(128, CLASSES - 128 * t))
            )
    for i, v in enumerate(joined(parts, lane32, 25)):
        g[pl.ds(BULK["readout"] + i, 32, stride=25), :] = v
    for c in ls_c:
        c.wait_send()
    for c in ms_c:
        c.wait_send()
    share_wait(sbuf_c, me_b, cs, cr)
    totc = total_of(sbuf_c, NB)

    def finish(y, n, d, gg, gb):
        normed = (y - n[0]) * n[2]
        return mask * n[3] * n[2] * (d - gb / voxels - normed * gg / voxels)

    def dy2_at(p, carry):
        d = dpre[p]
        v = finish(y2[p], n2, d[:, 128:256], totc[2:3], totc[3:4])
        dypad[padded(p)] = jnp.concatenate([next_t(v), v, prev_t(v)], axis=1).astype(BF16)
        return carry

    lax.fori_loop(0, POS, dy2_at, 0, unroll=7)

    core_i = lax.rem(me_b, 2)
    mate = digit_peer(me_b, 1, 2, 1)
    along = ((2, 8), (8, 2))
    digits = [[digit_of(me_b, along[i][s], 4) for i in range(2)] for s in range(2)]

    class Chunk:
        def __init__(self, index):
            self.base, self.last = CHUNKS[index]
            self.k = index
            self.first = 4 * self.last
            self.group = 4 * self.first
            self.half = 2 * self.group
            self.own = pl.multiple_of(self.base + core_i * self.half, self.last)
            self.r1 = (r1a, r1b)[index]
            self.r2 = (r2a, r2b)[index]
            self.gc = (gca, gcb)[index]
            self.s1 = ((g1sa, g1ra), (g1sb, g1rb))[index]

        def rows(self, at, count):
            return pl.ds(pl.multiple_of(at, self.last), count)

        def core_start(self):
            theirs = self.rows(self.base + (1 - core_i) * self.half, self.half)
            self.c0 = send_to(g.at[theirs], self.gc, co_s.at[self.k], co_r.at[self.k], mate)
            self.c0.start()

        def one_start(self):
            self.c0.wait()
            n = self.first

            def add(i, carry):
                at_ = self.rows(i * n, n)
                self.gc[at_, :] = self.gc[at_, :] + g[self.rows(self.own + i * n, n), :]
                return carry

            lax.fori_loop(0, self.half // n, add, 0)
            self.c1 = []
            for i in range(2):
                mine = digits[0][i]
                for d in range(1, 4):
                    to = lax.rem(mine + d, 4)
                    c = send_to(
                        self.gc.at[self.rows(i * self.group + to * self.first, self.first)],
                        self.r1.at[i, mine], s1s.at[self.k, i, d], s1r.at[self.k, i, d],
                        digit_peer(me_b, along[i][0], 4, d),
                    )
                    c.start()
                    self.c1.append(c)
                self.r1[i, mine] = self.gc[
                    self.rows(i * self.group + mine * self.first, self.first), :
                ]

        def two_start(self):
            for c in self.c1:
                c.wait()
            self.c2 = []
            for i in range(2):
                mine = digits[1][i]
                self.r1[i, 0] = total_of(self.r1.at[i], 4)
                for d in range(1, 4):
                    to = lax.rem(mine + d, 4)
                    c = send_to(
                        self.r1.at[i, 0, self.rows(to * self.last, self.last)],
                        self.r2.at[i, mine], s2s.at[self.k, i, d], s2r.at[self.k, i, d],
                        digit_peer(me_b, along[i][1], 4, d),
                    )
                    c.start()
                    self.c2.append(c)
                self.r2[i, mine] = self.r1[i, 0, self.rows(mine * self.last, self.last), :]

        def gather_start(self):
            for c in self.c2:
                c.wait()
            for i in range(2):
                mine = self.piece_at(i)
                gb_ref[mine, :] = total_of(self.r2.at[i], 4)

                def one(d, carry, mine=mine):
                    send_to(gb_ref.at[mine], gb_ref.at[mine], *self.s1, chip_peer(d)).start()
                    return carry

                lax.fori_loop(1, 16, one, 0)

        def piece_at(self, i):
            return self.rows(
                self.own + i * self.group + digits[0][i] * self.first + digits[1][i] * self.last,
                self.last,
            )

        def all_others(self):
            some = gb_ref.at[pl.ds(self.base, 30 * self.last)]
            return send_to(some, some, *self.s1, mate)

        def mate_rest(self):
            self.all_others().wait_recv()
            rows_ = self.rows(self.own, self.half)
            self.c5 = send_to(
                gb_ref.at[rows_], gb_ref.at[rows_], g3s.at[self.k], g3r.at[self.k], mate
            )
            self.c5.start()

        def finish(self):
            self.all_others().wait_send()
            self.c5.wait()

    chip = me_b // 2

    def chip_peer(d):
        return {"batch": lax.rem(chip + d, 16) * 2 + core_i}

    class Direct:
        half = 16 * DIRECT_ROWS

        def rows(self, at_, count=DIRECT_ROWS):
            return pl.ds(pl.multiple_of(at_, DIRECT_ROWS), count)

        def core_start(self):
            theirs = self.rows(DIRECT_AT + (1 - core_i) * self.half, self.half)
            self.c0 = send_to(g.at[theirs], gcc, co_s.at[2], co_r.at[2], mate)
            self.c0.start()

        def one_start(self):
            self.c0.wait()
            own = DIRECT_AT + core_i * self.half
            gcc[...] = gcc[...] + g[self.rows(own, self.half), :]

            def one(d, carry):
                to = lax.rem(chip + d, 16)
                send_to(
                    gcc.at[self.rows(to * DIRECT_ROWS)], rc.at[chip], d1s, d1r, chip_peer(d)
                ).start()
                return carry

            lax.fori_loop(1, 16, one, 0)
            rc[chip] = gcc[self.rows(chip * DIRECT_ROWS), :]

        def all_of(self, send, recv):
            some = rc.at[pl.ds(0, 15)]
            return send_to(some, some, send, recv, chip_peer(1))

        def two_start(self):
            self.all_of(d1s, d1r).wait_recv()
            mine = self.rows(DIRECT_AT + core_i * self.half + chip * DIRECT_ROWS)
            gb_ref[mine, :] = total_of(rc, 16)

            def one(d, carry):
                send_to(gb_ref.at[mine], gb_ref.at[mine], d2s, d2r, chip_peer(d)).start()
                return carry

            lax.fori_loop(1, 16, one, 0)

        def mate_rest(self):
            self.all_of(d2s, d2r).wait_recv()
            mine = self.rows(DIRECT_AT + core_i * self.half, self.half)
            self.c3 = send_to(gb_ref.at[mine], gb_ref.at[mine], d3s, d3r, mate)
            self.c3.start()

        def finish(self):
            self.all_of(d1s, d1r).wait_send()
            self.all_of(d2s, d2r).wait_send()
            self.c3.wait()

    a_, b_, c_ = Chunk(0), Chunk(1), Direct()

    def grad_conv(q, carry):
        dh = q // 3
        dw = q - dh * 3
        rhs = jnp.concatenate(
            [
                dypad[pl.ds((h + 2 - dh) * 9 + 2 - dw, SIDE)].reshape(SIDE * ROWS, 384)
                for h in range(SIDE)
            ],
            axis=0,
        )
        res = dot(at[...], rhs)
        for dt in range(3):
            tap = dt * 9 + q
            for j in range(NC):
                gq[48 * j : 48 * j + 48, :] = res[64 * j : 64 * j + 48, 128 * dt : 128 * dt + 128]
                vn[pl.ds(tap * 48 + 12 * j, 12), :] = res[
                    64 * j + 48 : 64 * j + 60, 128 * dt : 128 * dt + 128
                ]

            def put(i, v, base=tap_rows(dt, q)):
                g[pl.ds(base + i, 48, stride=3), :] = v

            flatten_96(lambda j: gq[pl.ds(j, 48, stride=4), :], 48, put)
        return carry

    lax.fori_loop(0, EARLY_TAPS, grad_conv, 0)
    a_.core_start()
    lax.fori_loop(EARLY_TAPS, 9, grad_conv, 0)
    g[BULK["volume"] : BULK["volume"] + 324, :] = flatten_32(
        lambda j: vn[pl.ds(j, 324, stride=4), :], 324
    )

    b_.core_start()
    a_.one_start()

    def conv_back(h, carry):
        acc = jnp.zeros((SIDE * ROWS, 256), F32)
        for q in range(9):
            dh, dw = divmod(q, 3)
            lhs = dypad[pl.ds((h + 2 - dh) * 9 + 2 - dw, SIDE)].reshape(SIDE * ROWS, 384)
            acc = acc + dot(lhs, wct_ref[q])
        for t in range(2):
            ynat[t, pl.ds(pl.multiple_of(h * SIDE * ROWS, SIDE * ROWS), SIDE * ROWS), :] = acc[
                :, 128 * t : 128 * t + 128
            ]
        return carry

    lax.fori_loop(0, 5, conv_back, 0)
    b_.one_start()
    lax.fori_loop(5, SIDE, conv_back, 0)

    def to_dm(p, carry):
        for j in range(NC):
            a = ynat[j // 2, pl.ds(pl.multiple_of(p * ROWS, ROWS), ROWS), :]
            b = ynat[j // 2, pl.ds(pl.multiple_of((p + HALF) * ROWS, ROWS), ROWS), :]
            if j % 2 == 0:
                dm[j, p] = jnp.where(low_half, a, pltpu.roll(b, 64, 1)).astype(BF16)
            else:
                dm[j, p] = jnp.where(low_half, pltpu.roll(a, 64, 1), b).astype(BF16)
        return carry

    for t in range(2):
        ynat[t, pl.ds(VOX, ROWS), :] = zero128
    lax.fori_loop(0, HALF, to_dm, 0, unroll=5)
    lo_, hi_ = pl.ds(0, near), pl.ds(near, HALF - near)

    def far_copy(i):
        rows_, to = ((lo_, right), (hi_, left))[i]
        return send_to(dm.at[far_i, rows_], dgot.at[2, rows_], ds_.at[i], dr.at[i], to)

    def near_copy(i):
        who, rows_, to, slot = (
            (right_i, hi_, right, 0), (left_i, lo_, left, 1), (right_i, lo_, right, 0),
            (left_i, hi_, left, 1),
        )[i]
        return send_to(
            dm.at[who, rows_], dgot.at[slot, rows_], ds_.at[2 + i], dr.at[2 + i], to
        )

    far_c = [far_copy(i) for i in range(2)]
    near_c = [near_copy(i) for i in range(4)]
    for c in far_c + near_c[0:2]:
        c.start()

    a_.two_start()

    def dy0_at(p, carry):
        v = finish(ypos[p][:, 0:128], n0, dpre[p][:, 0:128], totc[0:1], totc[1:2])
        v = v.astype(BF16).astype(F32)
        h, w = p // SIDE, lax.rem(p, SIDE)
        n_h = 3 - (h == 0).astype(jnp.int32) - (h == SIDE - 1).astype(jnp.int32)
        n_w = 3 - (w == 0).astype(jnp.int32) - (w == SIDE - 1).astype(jnp.int32)
        share = v / jnp.maximum(n_t * (n_h * n_w).astype(F32), 1.0)
        box[padded(p)] = share + prev_t(share) + next_t(share)
        ypos[p, :, 0:128] = v
        return carry

    lax.fori_loop(0, POS, dy0_at, 0, unroll=7)

    def dy0_nat(p, carry):
        acc, _ = spread(p)
        v = jnp.where(is_pool, acc * mask, ypos[p][:, 0:128])
        lowv = v - v.astype(BF16).astype(F32)
        dnat[0, pl.ds(p, ROWS, stride=POS), :] = v
        dnat[1, pl.ds(p, ROWS, stride=POS), :] = lowv
        return carry

    lax.fori_loop(0, POS, dy0_nat, 0, unroll=7)

    for c in far_c:
        c.wait_recv()

    def add_far(p, carry):
        who = jnp.where(p < near, right_i, left_i)
        dm[who, p] = (dm[who, p].astype(F32) + dgot[2, p].astype(F32)).astype(dm.dtype)
        return carry

    lax.fori_loop(0, HALF, add_far, 0, unroll=5)
    for c in near_c[2:4]:
        c.start()
    for at_, v in products(256):
        gw1_ref[0, at_, :] = v[:, 0:128] + v[:, 128:256]

    def put_direct(i, v):
        g[pl.ds(BULK["direct"] + i, 208, stride=3), :] = v

    flatten_96(lambda j: gw1_ref[0, pl.ds(j, 208, stride=4), :], 208, put_direct)
    g[BULK["pooled"] : BULK["pooled"] + 208, :] = flatten_32(
        lambda j: gw1_ref[0, pl.ds(j, 208, stride=4), :], 208
    )

    c_.core_start()
    a_.gather_start()
    b_.two_start()

    for c in near_c:
        c.wait_recv()


    def back1(p, carry):
        g1, b1 = carry
        s = dm[me, p].astype(F32) + dgot[0, p].astype(F32) + dgot[1, p].astype(F32)
        d, m = back(ypos[p][:, 128:256], n1, jnp.where(low_half, s, 0.0))
        ob[p] = d
        g1, b1 = g1 + d * m, b1 + d
        q = jnp.minimum(p + HALF, POS - 1)
        live = (p < POS - HALF).astype(F32)
        d, m = back(ypos[q][:, 128:256], n1, jnp.where(low_half, pltpu.roll(s, 64, 1), 0.0) * live)

        @pl.when(p < POS - HALF)
        def _():
            ob[p + HALF] = d

        return g1 + d * m, b1 + d

    g1, b1 = lax.fori_loop(0, HALF, back1, (zero128, zero128), unroll=5)
    sbuf_d[me_b] = pack_rows([col(g1), col(b1)], 2)
    share_start(sbuf_d, me_b, es, er)
    c_.one_start()

    def dy1_nat(p, carry):
        d = ob[p]
        top = d.astype(BF16).astype(F32)
        dnat[0, pl.ds(p, ROWS, stride=POS), :] = top + pltpu.roll(d - top, 64, 1)
        return carry

    lax.fori_loop(0, POS, dy1_nat, 0, unroll=7)
    for at_, v in products(128):
        gw1_ref[1, at_, :] = v + pltpu.roll(v, 64, 1)
    lsend[pl.ds(384, 128), :] = jnp.zeros((128, 128), F32)
    put_late(lsend)

    def late_copy(d):
        to = lax.rem(me_b + d, NB)
        return send_to(lsend.at[late_at(to)], lgot.at[me_b], fs, fr, batch_peer(me_b, d))

    def late_start(d, carry):
        late_copy(d).start()
        return carry

    lax.fori_loop(1, NB, late_start, 0)
    lgot[me_b] = lsend[late_at(me_b), :]
    for c in far_c + near_c:
        c.wait_send()
    b_.gather_start()
    share_wait(sbuf_d, me_b, es, er)
    totd = total_of(sbuf_d, NB)

    rowl = lax.broadcasted_iota(jnp.int32, (LATE_ROWS, 128), 0) + me_b * LATE_ROWS
    third = lax.rem(rowl, 3)

    def late_lanes(v):
        lane1 = lanes_of((1, 128))
        sq = joined([(v, 0, 48 * j, 48) for j in range(8)], lane1, 3)
        sh = joined([(v, 48, 12 * j, 12) for j in range(32)], lane1, 3)
        pick = [jnp.where(rowl < LATE["shrink"], a, b) for a, b in zip(sq, sh)]
        return jnp.where(third == 0, pick[0], jnp.where(third == 1, pick[1], pick[2]))

    scale_l = late_lanes(n1[3] * n1[2])
    bias_l = late_lanes(totd[1:2] / voxels)
    gain_l = late_lanes(totd[0:1] / voxels)
    share_wait(pgot, me_b, ps, pr)
    c_.two_start()
    share_wait(lgot, me_b, fs, fr)
    both = total_of(pgot, NB)
    late_ref[me_b] = scale_l * (total_of(lgot, NB) - bias_l * both[1] - gain_l * both[0])
    share_start(late_ref, me_b, hs, hr)
    a_.mate_rest()
    b_.mate_rest()

    fix = voxels / (voxels - 1.0)
    for tile, n, gg, gb in (
        (0, n0, totc[0:1], totc[1:2]),
        (1, n1, totd[0:1], totd[1:2]),
        (2, n2, totc[2:3], totc[3:4]),
    ):
        st_ref[:, 128 * tile : 128 * tile + 128] = pack_rows([gg, gb, n[0], n[1] * fix])
    sc_ref[...] = pack_rows([totc[4:5], counted])

    for buf, send, recv in (
        (sbuf_a, as_, ar), (sbuf_b, bs, br), (sbuf_c, cs, cr), (sbuf_d, es, er), (lgot, fs, fr),
        (pgot, ps, pr),
    ):
        share_sent(buf, me_b, send, recv)
    c_.mate_rest()
    share_wait(late_ref, me_b, hs, hr)
    share_sent(late_ref, me_b, hs, hr)
    for chunk in (a_, b_, c_):
        chunk.finish()


def core(x, lengths, labels, weights, affine):
    vm = pl.BlockSpec(memory_space=pltpu.VMEM)
    sm = pl.BlockSpec(memory_space=pltpu.SMEM)
    hbm = pl.BlockSpec(memory_space=pltpu.HBM)
    dma = pltpu.SemaphoreType.DMA
    vmem = pltpu.VMEM
    return pl.pallas_call(
        core_kernel,
        out_shape=(
            pltpu.VMEM((BULK_ROWS, 128), F32),
            jax.ShapeDtypeStruct((NB, LATE_ROWS, 128), F32),
            jax.ShapeDtypeStruct((8, 384), F32),
            jax.ShapeDtypeStruct((8, 128), F32),
        ),
        in_specs=[hbm, sm, sm] + [hbm] * 7 + [vm],
        out_specs=(vm,) * 4,
        scratch_shapes=[
            vmem((1, 326144), BF16),
            *[vmem((1, FLAT[n] * 128), F32) for n in NARROW],
            vmem((2, CIN, 128), F32),
            vmem((CIN, 128), F32),
            vmem((R1, 128), F32),
            vmem((1304, 128), F32),
            vmem((4, 256, 128), F32),
            vmem((9, 256, 384), BF16),
            vmem((9, 384, 256), BF16),
            vmem((256, 512), BF16),
            vmem((8, 384), F32),
            vmem((13 * GPAD, 128), F32),
            vmem((NC, GPAD, GW), BF16),
            vmem((NC, GW, 256), BF16),
            vmem((8, 256, 256), BF16),
            vmem((NC, W1_ROWS, 256), BF16),
            vmem((2, 8 * GPAD, 128), F32),
            vmem((POS, ROWS, 256), F32),
            vmem((81, ROWS, 128), F32),
            vmem((POS + 1, ROWS, 128), F32),
            vmem((NC, HALF, ROWS, 128), BF16),
            vmem((81, ROWS, 256), BF16),
            vmem((POS, ROWS, 256), BF16),
            vmem((256, VOX), BF16),
            vmem((POS, ROWS, 128), F32),
            vmem((POS, ROWS, 256), F32),
            vmem((81, ROWS, 384), BF16),
            vmem((NC, HALF, ROWS, 128), BF16),
            vmem((3, HALF, ROWS, 128), BF16),
            vmem((2, 8 * GPAD, 128), F32),
            vmem((2, CIN, 128), F32),
            vmem((R1, 128), F32),
            vmem((4, 256, 128), F32),
            vmem((BULK_ROWS, 128), F32),
            *[vmem((32 * n, 128), F32) for _, n in CHUNKS],
            vmem((16 * DIRECT_ROWS, 128), F32),
            *[vmem((2, 4, 4 * n, 128), F32) for _, n in CHUNKS],
            *[vmem((2, 4, n, 128), F32) for _, n in CHUNKS],
            vmem((16, DIRECT_ROWS, 128), F32),
            vmem((NB * LATE_ROWS, 128), F32),
            vmem((NB, LATE_ROWS, 128), F32),
            vmem((2, NB * LATE_ROWS, 128), F32),
            vmem((NB, 2, LATE_ROWS, 128), F32),
            vmem((NC, ROWS, 512), F32),
            *[vmem((NB, n, 128), F32) for n in (8, 2, 8, 2)],
            dma((4,)), dma((7,)), dma((12,)), dma((12,)),
            dma((6,)), dma((6,)), dma((NC,)), dma((NC,)), dma((6,)), dma((6,)),
            *[dma] * 12,
            dma((3,)), dma((3,)),
            *[dma((2, 2, 4))] * 4,
            *[dma] * 4,
            dma((2,)), dma((2,)),
            *[dma] * 8,
        ],
        compiler_params=pltpu.CompilerParams(
            collective_id=0, has_side_effects=True, vmem_limit_bytes=47 << 20
        ),
        name="block",
    )(x, lengths, labels, *weights, affine)


def unlanes(tiles):
    t0, t1, t2 = tiles
    lane = lanes_of(t0.shape)
    parts = [(t0, 0, 0, 96), (t1, 0, 96, 60), (t0, 96, 156, 32), (t2, 0, 188, 128)]
    return joined(parts, lane, 3)


def adam_kernel(*refs):
    gb, late, st, sc, running = refs[0:5]
    w_in, m_in, v_in = refs[5:13], refs[13:21], refs[21:29]
    m_out, v_out, w_out = refs[29:37], refs[37:45], refs[45:53]
    run_out, loss_out, count_out, copies_out = refs[53:57]
    wb, mb, vb = refs[57:64], refs[64:71], refs[71:78]
    cb, insem, outsem, csem = refs[78:82]
    rates = step_rates()
    parts = []
    for i in ADAM_ORDER:
        parts.append((i, 0, FLAT[NAMES[i]]))
    for first in range(0, FLAT["spatial"], ADAM_ROWS):
        parts.append((2, first, ADAM_ROWS))

    def at_rows(ref, i, first, count):
        if NAMES[i] in NARROW:
            return ref.at[:, pl.ds(first * 128, count * 128)]
        return ref.at[pl.ds(first, count)]

    ins = []
    for n, (i, first, count) in enumerate(parts):
        mine = []
        for kind, (src, dst) in enumerate(((w_in[i], wb[i]), (m_in[i], mb[i]), (v_in[i], vb[i]))):
            if NAMES[i] == "spatial" and kind < 2:
                continue
            c = pltpu.make_async_copy(
                at_rows(src, i, first, count), at_rows(dst, i, first, count), insem.at[n, kind]
            )
            c.start()
            mine.append(c)
        ins.append(mine)

    starts = []
    total = 0
    for name in NAMES:
        starts.append(total * 128)
        total += FLAT[name]
    outs = []
    for n, (i, first, rows) in enumerate(parts):
        name = NAMES[i]
        for c in ins[n]:
            c.wait()

        def step(at, count, i=i, name=name, first=first):
            if name == "spatial":
                tap = at // 144
                row = tap_rows(tap // 9, lax.rem(tap, 9)) + lax.rem(at, 144)
                grad = gb[pl.ds(pl.multiple_of(row, 8), count), :]
            elif name in BULK:
                grad = gb[pl.ds(BULK[name] + at, count), :]
            else:
                grad = late[pl.ds(LATE[name] + at, count), :]
            wide = pl.ds(pl.multiple_of(at * 128, 128), count * 128)
            narrow = name in NARROW

            def load(ref):
                if narrow:
                    return ref[:, wide].reshape(count, 128)
                return ref[pl.ds(at, count), :]

            def store(ref, v):
                if narrow:
                    ref[:, wide] = v.reshape(1, count * 128)
                else:
                    ref[pl.ds(at, count), :] = v

            old = (w_in, m_in, vb) if name == "spatial" else (wb, mb, vb)
            m, v, w = adamw(*(load(group[i]) for group in old), grad, rates[i])
            store(mb[i], m)
            store(vb[i], v)
            store(wb[i], w)
            cb[:, pl.ds(pl.multiple_of(starts[i] + at * 128, 128), count * 128)] = w.astype(
                BF16
            ).reshape(1, count * 128)

        block = {"spatial": 72, "readout": 80, "direct": 48, "pooled": 104, "squeeze": 104}.get(
            name, 24
        )
        loops = rows // block

        def body(j, carry, step=step, block=block, first=first):
            step(pl.multiple_of(first + j * block, 8), block)
            return carry

        lax.fori_loop(0, loops, body, 0, unroll=3)
        at, rest = first + loops * block, rows - loops * block
        if rest // 8:
            step(at, rest // 8 * 8)
        if rest % 8:
            step(at + rest // 8 * 8, rest % 8)
        for kind, (src, dst) in enumerate(((wb[i], w_out[i]), (mb[i], m_out[i]), (vb[i], v_out[i]))):
            c = pltpu.make_async_copy(
                at_rows(src, i, first, rows), at_rows(dst, i, first, rows), outsem.at[n, kind]
            )
            c.start()
            outs.append(c)
        at = pl.ds(starts[i] + first * 128, rows * 128)
        c = pltpu.make_async_copy(cb.at[:, at], copies_out.at[:, at], csem.at[n])
        c.start()
        outs.append(c)

    tiles = [st[:, 128 * t : 128 * t + 128] for t in range(3)]
    for t, v in enumerate(unlanes(tiles)):
        width = min(128, 316 - 128 * t)
        at = slice(128 * t, 128 * t + width)
        v = v[:, 0:width]
        m, s, w = adamw(w_in[7][:, at], m_in[7][:, at], v_in[7][:, at], v[0:2], rates[7])
        m_out[7][:, at] = m
        v_out[7][:, at] = s
        w_out[7][:, at] = w
        run_out[:, at] = MOMENTUM * running[:, at] + (1.0 - MOMENTUM) * v[2:4]
    loss_out[...] = sc[0:1, 0:1]
    count_out[...] = sc[1:2, 0:1]
    for c in outs:
        c.wait()


def adam(gb, late, st, sc, running, masters, firsts, seconds):
    vm = pl.BlockSpec(memory_space=pltpu.VMEM)
    hbm = pl.BlockSpec(memory_space=pltpu.HBM)
    dma = pltpu.SemaphoreType.DMA
    shapes = [(1, FLAT[n] * 128) if n in NARROW else (FLAT[n], 128) for n in NAMES]
    flats = [jax.ShapeDtypeStruct(shape, F32) for shape in shapes]
    small = jax.ShapeDtypeStruct((2, 316), F32)
    total = sum(FLAT[n] for n in NAMES) * 128
    one = jax.ShapeDtypeStruct((1, 1), F32)
    specs = [hbm] * 7 + [vm]
    buffers = [pltpu.VMEM(shape, F32) for shape in shapes]
    count = 6 + FLAT["spatial"] // ADAM_ROWS
    return pl.pallas_call(
        adam_kernel,
        out_shape=[*(flats + [small]) * 3, small, one, one, jax.ShapeDtypeStruct((1, total), BF16)],
        in_specs=[vm] * 5 + ([hbm] * 2 + [vm] + [hbm] * 4 + [vm]) * 2 + specs,
        out_specs=[*specs * 3, vm, vm, vm, hbm],
        scratch_shapes=[
            *buffers * 3, pltpu.VMEM((1, total), BF16), dma((count, 3)), dma((count, 3)), dma((count,)),
        ],
        compiler_params=pltpu.CompilerParams(vmem_limit_bytes=20 << 20),
        name="adamw",
    )(gb, late, st, sc, running, *masters, *firsts, *seconds)


def per_device(
    features, lengths, labels, direct, squeeze, spatial, shrink, volume, pooled, readout, affine,
    first_direct, first_squeeze, first_spatial, first_shrink, first_volume, first_pooled,
    first_readout, first_affine, second_direct, second_squeeze, second_spatial, second_shrink,
    second_volume, second_pooled, second_readout, second_affine, running,
):
    masters = [direct, squeeze, spatial, shrink, volume, pooled, readout, affine]
    firsts = [
        first_direct, first_squeeze, first_spatial, first_shrink, first_volume, first_pooled,
        first_readout, first_affine,
    ]
    seconds = [
        second_direct, second_squeeze, second_spatial, second_shrink, second_volume,
        second_pooled, second_readout, second_affine,
    ]
    def rows(flat, name):
        return flat if name in NARROW else flat.reshape(-1, 128)

    masters, firsts, seconds = (
        [rows(a, n) for a, n in zip(group, NAMES)] + [group[7]]
        for group in (masters, firsts, seconds)
    )
    def put(arrays, space):
        return [pltpu.with_memory_space_constraint(a, space) for a in arrays]

    x, lens, labs, aff = put([features, lengths, labels.T, affine], pltpu.HBM)
    gb, late, st, sc = core(x, lens, labs, put(masters[:7], pltpu.HBM), aff)
    (gb,) = put([gb], pltpu.VMEM)
    masters, firsts, seconds = (
        put(group[:2], pltpu.HBM) + put(group[2:3], space) + put(group[3:7], pltpu.HBM)
        + [group[7]]
        for group, space in ((masters, pltpu.VMEM), (firsts, pltpu.VMEM), (seconds, pltpu.HBM))
    )
    out = adam(gb, late.reshape(NB * LATE_ROWS, 128), st, sc, running, masters, firsts, seconds)
    flat_out = [a if i % 8 == 7 else a.reshape(1, -1) for i, a in enumerate(out[:24])]
    return (*flat_out, out[24], out[25].reshape(()), out[26].reshape(()), out[27])


def solution(mesh):
    flat = P("chan", None)
    wide = P(None, "chan")
    weights = (flat,) * 7 + (wide,)
    return jax.shard_map(
        per_device,
        mesh=mesh,
        in_specs=(P("chan", "batch"), P("batch"), P("batch", None)) + weights * 3 + (wide,),
        out_specs=weights * 3 + (wide, P(), P(), flat),
        check_vma=False,
    )
```

```python
import math
from functools import partial

import jax
import jax.numpy as jnp
from jax import lax
from jax.experimental import pallas as pl
from jax.experimental.pallas import tpu as pltpu
from jax.sharding import PartitionSpec as P

CIN = 832
B0 = 384
R1 = 192
O1 = 384
R2 = 48
O2 = 128
B3 = 128
CLASSES = 400
SIDE = 7
STEP = 5
NC = 4
NB = 32
POS = SIDE * SIDE
ROWS = 32
VOX = POS * ROWS
GROUPS = VOX // 8
GPAD = 208
CB = CIN // NC
GW = 8 * CB
HALF = 25
SHIFT = 112
W1_ROWS = 448
TAPS = 27
FLAT = {"direct": 624, "squeeze": 312, "spatial": 3888, "shrink": 78, "volume": 324, "pooled": 208,
        "readout": 800}
NAMES = ("direct", "squeeze", "spatial", "shrink", "volume", "pooled", "readout")
HELD = {"spatial": 0, "volume": 3888, "direct": 4216, "pooled": 4840, "readout": 5048}
BULK = {"volume": 4720, "direct": 5120, "pooled": 5744, "readout": 1728}
EARLY_TAPS = 4
NARROW = ("shrink", "volume")
LATE = {"squeeze": 0, "shrink": 312}
CHUNKS = ((0, 40), (2560, 40))
DIRECT_AT = 5120
DIRECT_ROWS = 32
BULK_ROWS = 6144
LATE_ROWS = 16
ADAM_ROWS = 648
ADAM_ORDER = (3, 1, 5, 0, 6, 4)

EPS = 1e-05
BETA_ONE = 0.5
BETA_TWO = 0.5
DECAY = 0.01
MOMENTUM = 0.99

MESH = pl.DeviceIdType.MESH
F32 = jnp.float32
BF16 = jnp.bfloat16


def step_rates():
    return [
        1.5 / math.sqrt(CIN),
        1.5 / math.sqrt(CIN),
        1.5 / math.sqrt(27 * R1),
        1.5 / math.sqrt(CIN),
        1.5 / math.sqrt(27 * R2),
        1.5 / math.sqrt(CIN),
        0.2,
        0.3,
    ]


def adamw(weight, moment_one, moment_two, gradient, step_rate):
    first_new = BETA_ONE * moment_one + (1.0 - BETA_ONE) * gradient
    second_new = BETA_TWO * moment_two + (1.0 - BETA_TWO) * (gradient * gradient)
    scale_one = step_rate / (1.0 - BETA_ONE**STEP)
    scale_two = 1.0 / (1.0 - BETA_TWO**STEP)
    weight_new = weight * (1.0 - step_rate * DECAY) - scale_one * first_new / (
        jnp.sqrt(second_new * scale_two) + 1e-08
    )
    return (first_new, second_new, weight_new)


def window_of(r):
    start = CB * r
    tile, offset = divmod(start, 128)
    lanes = 256 if offset + CB <= 256 else 384
    return tile * 128, offset, lanes


def dot(a, b):
    return jnp.dot(a, b, preferred_element_type=F32)


def dot_t(a, b, ca, cb):
    return lax.dot_general(a, b, (((ca,), (cb,)), ((), ())), preferred_element_type=F32)


def send_to(src, dst, send, recv, target):
    return pltpu.make_async_remote_copy(
        src_ref=src, dst_ref=dst, send_sem=send, recv_sem=recv, device_id=target,
        device_id_type=MESH,
    )


def batch_peer(me, d):
    return {"batch": lax.rem(me + d, NB)}


def chan_peer(me, d):
    return {"chan": lax.rem(me + d, NC)}


def share_start(buf, me, send, recv):
    def one(d, carry):
        send_to(buf.at[me], buf.at[me], send, recv, batch_peer(me, d)).start()
        return carry

    lax.fori_loop(1, NB, one, 0)


def share_copy(buf, me, send, recv):
    others = buf.at[pl.ds(0, NB - 1)]
    return send_to(others, others, send, recv, batch_peer(me, 1))


def share_wait(buf, me, send, recv):
    share_copy(buf, me, send, recv).wait_recv()


def share_sent(buf, me, send, recv):
    share_copy(buf, me, send, recv).wait_send()


def digit_of(me, stride, size):
    return lax.rem(me // stride, size)


def digit_peer(me, stride, size, d):
    digit = digit_of(me, stride, size)
    return {"batch": me + stride * (lax.rem(digit + d, size) - digit)}


def piece(tiles, start, width, dest, lane):
    tile, off = divmod(start, 128)
    v = tiles[tile]
    if off + width > 128:
        v = jnp.where(lane >= off, v, tiles[tile + 1])
    shift = (dest - off) % 128
    return pltpu.roll(v, shift, 1) if shift else v


def joined(parts, lane, count):
    out = []
    moved = []
    for value, src, start, width in parts:
        shift = (start - src) % 128
        moved.append((pltpu.roll(value, shift, 1) if shift else value, start, width))
    for i in range(count):
        acc = None
        for value, start, width in moved:
            lo, hi = max(0, start - 128 * i), min(128, start + width - 128 * i)
            if lo < hi:
                acc = value if acc is None else jnp.where(lane >= lo, value, acc)
        out.append(acc)
    return out


def lanes_of(v):
    return lax.broadcasted_iota(jnp.int32, v, 1)


def tap_rows(dt, q):
    return q * 432 + jnp.where(q >= EARLY_TAPS, 832, 0) + dt * 144


def prepare_w1(flat, wn, wk, w1p):
    lane = lanes_of((208, 128))
    tiles = [flat["direct"][pl.ds(i, 208, stride=3), :] for i in range(3)]
    pool = flat["pooled"][...]
    for j in range(4):
        v = jnp.where(
            lane < 96, piece(tiles, 96 * j, 96, 0, lane), piece([pool], 32 * j, 32, 96, lane)
        )
        wn[0, pl.ds(j, 208, stride=4), :] = v
    lane = lanes_of((104, 128))
    tiles = [flat["squeeze"][pl.ds(i, 104, stride=3), :] for i in range(3)]
    for j in range(8):
        wn[1, pl.ds(j, 104, stride=8), :] = piece(tiles, 48 * j, 48, 0, lane)
    lane = lanes_of((26, 128))
    tiles = [flat["shrink"][pl.ds(i, 26, stride=3), :] for i in range(3)]
    for j in range(32):
        wk[pl.ds(j, 26, stride=32), :] = piece(tiles, 12 * j, 12, 48, lane)
    lane = lanes_of((CB, 128))
    for k in range(NC):
        rows = slice(k * CB, (k + 1) * CB)
        second = jnp.where(lane < 48, wn[1, rows, :], jnp.where(lane < 60, wk[rows, :], 0.0))
        both = jnp.concatenate([wn[0, rows, :], second], axis=1).astype(BF16)
        w1p[k, 0:SHIFT, :] = jnp.zeros((SHIFT, 256), BF16)
        w1p[k, SHIFT : SHIFT + CB, :] = both
        w1p[k, SHIFT + CB : W1_ROWS, :] = jnp.zeros((W1_ROWS - SHIFT - CB, 256), BF16)


def prepare_conv(flat, tb, vn, wc, wct):
    lane = lanes_of((324, 128))
    for j in range(4):
        v = piece([flat["volume"][...]], 32 * j, 32, 96, lane)
        vn[pl.ds(j, 324, stride=4), :] = jnp.where(lane >= 96, v, 0.0)
    vn[pl.ds(1296, 8), :] = jnp.zeros((8, 128), F32)
    lane48 = lanes_of((48, 128))
    row16 = lax.broadcasted_iota(jnp.int32, (16, 128), 0)

    def one(q, carry):
        for dt in range(3):
            tap = dt * 9 + q
            tiles = [
                flat["spatial"][pl.ds(tap * 144 + i, 48, stride=3), :] for i in range(3)
            ]
            for j in range(4):
                v = piece(tiles, 96 * j, 96, 0, lane48)
                tb[pl.ds(j, 48, stride=4), :] = jnp.where(lane48 < 96, v, 0.0)
            for j in range(NC):
                at = slice(128 * dt, 128 * dt + 128)
                wc[q, 64 * j : 64 * j + 48, at] = tb[48 * j : 48 * j + 48, :].astype(BF16)
                v = vn[pl.ds(tap * 48 + 12 * j, 16), :]
                wc[q, 64 * j + 48 : 64 * j + 64, at] = jnp.where(row16 < 12, v, 0.0).astype(BF16)
        wct[q] = jnp.transpose(wc[q])
        return carry

    lax.fori_loop(0, 9, one, 0)


def prepare_readout(flat, rn, rp):
    lane = lanes_of((32, 128))
    tiles = [flat["readout"][pl.ds(i, 32, stride=25), :] for i in range(25)]
    for t in range(4):
        width = min(128, CLASSES - 128 * t)
        for j in range(8):
            v = piece(tiles, CLASSES * j + 128 * t, width, 0, lane)
            rn[t, pl.ds(j, 32, stride=8), :] = v if width == 128 else jnp.where(lane < width, v, 0.0)
        at = slice(128 * t, 128 * t + 128)
        for dst, src, count in ((0, 0, 96), (96, 224, 32), (128, 96, 96), (224, 192, 32)):
            rp[dst : dst + count, at] = rn[t, src : src + count, :].astype(BF16)


def prepare_affine(aff, out):
    a = [aff[:, 0:128], aff[:, 128:256]]
    a.append(jnp.concatenate([aff[:, 256:316], jnp.zeros((2, 68), F32)], axis=1))
    lane = lanes_of((2, 128))
    t0 = jnp.where(lane < 96, a[0], piece(a, 156, 32, 96, lane))
    t1 = jnp.where(lane < 60, piece(a, 96, 60, 0, lane), 0.0)
    t2 = piece(a, 188, 128, 0, lane)
    for i, t in enumerate((t0, t1, t2)):
        out[0:2, 128 * i : 128 * i + 128] = t


def flatten_96(src, rows, put):
    lane = lanes_of((rows, 128))
    for i, v in enumerate(joined([(src(j), 0, 96 * j, 96) for j in range(4)], lane, 3)):
        put(i, v)


def flatten_32(src, rows):
    lane = lanes_of((rows, 128))
    return joined([(src(j), 96, 32 * j, 32) for j in range(4)], lane, 1)[0]


def total_of(buf, count):
    acc = buf[0]
    for slot in range(1, count):
        acc = acc + buf[slot]
    return acc


def core_kernel(
    x_hbm, len_ref, lab_ref, direct_hbm, squeeze_hbm, spatial_hbm, shrink_hbm, volume_hbm,
    pooled_hbm, readout_hbm, affine_ref,
    gb_ref, late_ref, st_ref, sc_ref,
    x_ref, n_shrink, n_volume,
    wn, wk, tb, vn, rn, wc_ref, wct_ref, r_ref, aff_ref,
    xf, xg, xt, cols, w1p, ynat, ypos, box, ob, got, apad, acol, at, y2, dpre, dypad, dm, dgot, dnat,
    gw1_ref, gq, gr, g, gca, gcb, gcc, r1a, r1b, r2a, r2b, rc, lsend, lgot, psend, pgot,
    lbuf, sbuf_a, sbuf_b, sbuf_c, sbuf_d,
    xin, win, xs, xr, ms, mr, ls, lr, ds_, dr,
    as_, ar, bs, br, cs, cr, es, er, fs, fr, hs, hr,
    co_s, co_r, s1s, s1r, s2s, s2r, g1sa, g1sb, g1ra, g1rb, g3s, g3r, ps, pr, d1s, d1r, d2s, d2r, d3s, d3r,
):
    me_b = lax.axis_index("batch")
    me = lax.axis_index("chan")

    barrier = pltpu.get_barrier_semaphore()

    loops = (0, 104, 182, 260, 318)
    cuts = [1024 * n for n in loops[:4]] + [326144]
    x_in = []
    for i in range(4):
        at_ = pl.ds(cuts[i], cuts[i + 1] - cuts[i])
        c = pltpu.make_async_copy(x_hbm.at[:, at_], x_ref.at[:, at_], xin.at[i])
        c.start()
        x_in.append(c)
    flat = {n: g.at[at_ : at_ + FLAT[n]] for n, at_ in HELD.items()}
    flat.update({n: lsend.at[at_ : at_ + FLAT[n]] for n, at_ in LATE.items()})
    w_in = []
    for i, (src, name) in enumerate(
        zip(
            (direct_hbm, squeeze_hbm, spatial_hbm, shrink_hbm, volume_hbm, pooled_hbm, readout_hbm),
            NAMES,
        )
    ):
        dst = {"shrink": n_shrink, "volume": n_volume}.get(name, flat[name])
        c = pltpu.make_async_copy(src, dst, win.at[i])
        c.start()
        w_in.append(c)

    def greet(d, carry):
        pl.semaphore_signal(barrier, inc=1, device_id=batch_peer(me_b, d), device_id_type=MESH)
        return carry

    lax.fori_loop(1, NB, greet, 0)
    for d in range(1, NC):
        pl.semaphore_signal(barrier, inc=1, device_id=chan_peer(me, d), device_id_type=MESH)

    def flat_rows(i, carry):
        v = x_ref[:, pl.ds(pl.multiple_of(i * 1024, 1024), 1024)].astype(F32)
        xf[pl.ds(pl.multiple_of(i * 8, 8), 8), :] = v.reshape(8, 128)
        return carry

    right, left = chan_peer(me, 1), chan_peer(me, NC - 1)
    left_i, right_i = lax.rem(me + NC - 1, NC), lax.rem(me + 1, NC)
    bounds = (0, 64, 112, 160, GPAD)

    def part(who, i):
        return xg.at[who, bounds[i] : bounds[i + 1]]

    def hop(i, side):
        return send_to(
            part(me, i), part(me, i), xs.at[4 * side + i], xr.at[4 * side + i], (right, left)[side]
        )

    def pass_on(i):
        who, to = ((left_i, right), (right_i, left))[i // 2]
        return send_to(part(who, i), part(who, i), xs.at[8 + i], xr.at[8 + i], to)

    xf[pl.ds(2548, 2704 - 2548), :] = jnp.zeros((2704 - 2548, 128), F32)
    for i in range(4):
        x_in[i].wait()
        lax.fori_loop(loops[i], loops[i + 1], flat_rows, 0, unroll=(8, 6, 6, 2)[i])
        if i == 3:
            xf[pl.ds(2544, 4), :] = x_ref[:, 318 * 1024 : 318 * 1024 + 512].astype(F32).reshape(
                4, 128
            )
        low, count = bounds[i], bounds[i + 1] - bounds[i]
        for t in range(13):
            xg[me, low : low + count, 128 * t : 128 * t + 128] = xf[
                pl.ds(13 * low + t, count, stride=13), :
            ].astype(BF16)
        if i == 0:
            pl.semaphore_wait(barrier, NB - 1 + NC - 1)
        for side in range(2):
            hop(i, side).start()

    rowi = lax.broadcasted_iota(jnp.int32, (ROWS, 128), 0)
    lane = lax.broadcasted_iota(jnp.int32, (ROWS, 128), 1)
    clip = rowi // 4
    step = rowi - clip * 4
    lens = jnp.zeros((ROWS, 128), jnp.int32)
    for c in range(8):
        lens = jnp.where(clip == c, len_ref[c], lens)
    mask = (step < lens).astype(F32)
    has_prev = (step > 0).astype(F32)
    has_next = (step < 3).astype(F32)

    def prev_t(v):
        return pltpu.roll(v, 1, 0) * has_prev

    def next_t(v):
        return pltpu.roll(v, ROWS - 1, 0) * has_next

    n_t = mask + prev_t(mask) + next_t(mask)
    is_pool = lane >= 96
    low_half = lane < 64

    for c in w_in:
        c.wait()
    for src, dst in ((n_shrink, flat["shrink"]), (n_volume, flat["volume"])):
        count = dst.shape[0]
        whole = count // 8 * 8
        dst[0:whole, :] = src[:, 0 : whole * 128].reshape(whole, 128)
        dst[whole:count, :] = src[:, whole * 128 : count * 128].reshape(count - whole, 128)
    prepare_w1(flat, wn, wk, w1p)
    prepare_affine(affine_ref, aff_ref)
    prepare_readout(flat, rn, r_ref)

    def zero_pad(i, carry):
        apad[i] = jnp.zeros((ROWS, 256), BF16)
        dypad[i] = jnp.zeros((ROWS, 384), BF16)
        box[i] = jnp.zeros((ROWS, 128), F32)
        return carry

    lax.fori_loop(0, 81, zero_pad, 0, unroll=9)
    dnat[...] = jnp.zeros_like(dnat)
    prepare_conv(flat, tb, vn, wc_ref, wct_ref)

    for i in range(4):
        hop(i, i // 2).wait_recv()
        pass_on(i).start()
    for i in range(4):
        hop(i, 1 - i // 2).wait_recv()

    far_i = lax.rem(me + 2, NC)

    def one_by_one(r, blocks):
        first, off, lanes = window_of(r)
        acc = None
        for k in blocks:
            v = dot(
                xg[k, :, first : first + lanes], w1p[k, SHIFT - off : SHIFT - off + lanes, :]
            )
            acc = v if acc is None else acc + v
        return acc

    for r in range(8):
        acc = one_by_one(r, (me, left_i, right_i))
        for t in range(2):
            ynat[t, pl.ds(r, GPAD, stride=8), :] = acc[:, 128 * t : 128 * t + 128]
    for i in range(4):
        pass_on(i).wait_recv()
    for r in range(8):
        acc = one_by_one(r, (far_i,))
        for t in range(2):
            at_ = pl.ds(r, GPAD, stride=8)
            ynat[t, at_, :] = ynat[t, at_, :] + acc[:, 128 * t : 128 * t + 128]
    for i in range(4):
        pass_on(i).wait_send()
        for side in range(2):
            hop(i, side).wait_send()

    def padded(p):
        return (p // SIDE + 1) * 9 + lax.rem(p, SIDE) + 1

    def to_pos(p, carry):
        v = ynat[0, pl.ds(p, ROWS, stride=POS), :]
        ypos[p, :, 0:128] = v
        ypos[p, :, 128:256] = ynat[1, pl.ds(p, ROWS, stride=POS), :]
        mz = v * mask
        box[padded(p)] = mz + prev_t(mz) + next_t(mz)
        return carry

    lax.fori_loop(0, POS, to_pos, 0, unroll=7)

    def spread(p):
        h, w = p // SIDE, lax.rem(p, SIDE)
        acc = jnp.zeros((ROWS, 128), F32)
        for dh in range(3):
            for dw in range(3):
                acc = acc + box[(h + dh) * 9 + w + dw]
        n_h = 3 - (h == 0).astype(jnp.int32) - (h == SIDE - 1).astype(jnp.int32)
        n_w = 3 - (w == 0).astype(jnp.int32) - (w == SIDE - 1).astype(jnp.int32)
        return acc, (n_h * n_w).astype(F32)

    def pool(p, carry):
        s1, s2 = carry
        acc, n = spread(p)
        v = ypos[p]
        v0 = jnp.where(is_pool, acc / jnp.maximum(n_t * n, 1.0), v[:, 0:128])
        v1 = v[:, 128:256]
        ypos[p] = jnp.concatenate([v0, v1], axis=1)
        m0, m1 = v0 * mask, v1 * mask
        return (
            s1 + jnp.concatenate([m0, m1], axis=1),
            s2 + jnp.concatenate([m0 * v0, m1 * v1], axis=1),
        )

    zero256 = jnp.zeros((ROWS, 256), F32)
    zero128 = jnp.zeros((ROWS, 128), F32)
    s1, s2 = lax.fori_loop(0, POS, pool, (zero256, zero256), unroll=7)

    def col(v):
        return jnp.sum(v, axis=0, keepdims=True)

    def pack_rows(rows, count=8):
        fill = [jnp.zeros((1, 128), F32)] * (count - len(rows))
        return jnp.concatenate(list(rows) + fill, axis=0)

    sbuf_a[me_b] = pack_rows(
        [col(s1[:, 0:128]), col(s1[:, 128:256]), col(s2[:, 0:128]), col(s2[:, 128:256]), col(mask)]
    )
    share_start(sbuf_a, me_b, as_, ar)
    cols[...] = jnp.zeros_like(cols)
    for k in range(NC):
        xt[k, :, GPAD:256] = jnp.zeros((GW, 256 - GPAD), BF16)
        xt[k, :, 0:GPAD] = jnp.transpose(xg[k])
    share_wait(sbuf_a, me_b, as_, ar)
    tot = total_of(sbuf_a, NB)
    counted = tot[4:5, :]
    voxels = counted * float(POS)

    def norm_of(sum1, sum2, tile):
        avg = sum1 / voxels
        var = sum2 / voxels - avg * avg
        inv = lax.rsqrt(var + EPS)
        gain = aff_ref[0:1, 128 * tile : 128 * tile + 128]
        bias = aff_ref[1:2, 128 * tile : 128 * tile + 128]
        return avg, var, inv, gain, bias

    n0 = norm_of(tot[0:1], tot[2:3], 0)
    n1 = norm_of(tot[1:2], tot[3:4], 1)

    def forward(y, n):
        normed = (y - n[0]) * n[2]
        pre = n[3] * normed + n[4]
        sig = jax.nn.sigmoid(pre)
        return normed, pre, sig

    def act1(p, carry):
        _, pre, sig = forward(ypos[p][:, 128:256], n1)
        ob[p] = (mask * (pre * sig))
        return carry

    lax.fori_loop(0, POS, act1, 0, unroll=7)
    ob[POS] = zero128

    def to_msg(p, carry):
        got[me, p] = jnp.where(low_half, ob[p], pltpu.roll(ob[p + HALF], 64, 1)).astype(BF16)
        return carry

    lax.fori_loop(0, HALF, to_msg, 0, unroll=5)
    near = 12

    def half(who, low):
        return got.at[who, 0:near] if low else got.at[who, near:HALF]

    ms_c = []
    for i, (low, to) in enumerate([(True, right), (False, left), (False, right), (True, left)]):
        c = send_to(half(me, low), half(me, low), ms.at[i], mr.at[i], to)
        c.start()
        ms_c.append(c)

    def act0(p, carry):
        _, pre, sig = forward(ypos[p][:, 0:128], n0)
        return carry + mask * (pre * sig)

    feat0 = lax.fori_loop(0, POS, act0, zero128, unroll=7)

    def products(width):
        for r in range(8):
            for t in range(width // 128):
                cols[r, 0:GPAD, 128 * t : 128 * t + 128] = dnat[
                    t, pl.ds(r, GPAD, stride=8), :
                ].astype(BF16)
        rhs = cols[:, :, 0:width].reshape(8 * 256, width)
        for k in range(NC):
            lhs = jnp.concatenate([xt[k, CB * r : CB * r + CB, :] for r in range(8)], axis=1)
            yield slice(k * CB, (k + 1) * CB), dot(lhs, rhs)

    def put_late(dst):
        lane104, lane26 = lanes_of((104, 128)), lanes_of((26, 128))
        parts = [(gw1_ref[1, pl.ds(j, 104, stride=8), :], 0, 48 * j, 48) for j in range(8)]
        for i, v in enumerate(joined(parts, lane104, 3)):
            dst[pl.ds(LATE["squeeze"] + i, 104, stride=3), :] = v
        parts = [(gw1_ref[1, pl.ds(j, 26, stride=32), :], 48, 12 * j, 12) for j in range(32)]
        for i, v in enumerate(joined(parts, lane26, 3)):
            dst[pl.ds(LATE["shrink"] + i, 26, stride=3), :] = v

    def late_at(i):
        return pl.ds(pl.multiple_of(i * LATE_ROWS, LATE_ROWS), LATE_ROWS)

    def normed_nat(p, carry):
        normed, _, _ = forward(ypos[p][:, 128:256], n1)
        v = jnp.where(lane < 60, normed * mask, jnp.where(lane == 64, mask, 0.0))
        dnat[0, pl.ds(p, ROWS, stride=POS), :] = v
        return carry

    def early_products():
        lax.fori_loop(0, POS, normed_nat, 0, unroll=7)
        for at_, v in products(128):
            gw1_ref[1, at_, :] = v
        psend[...] = jnp.zeros_like(psend)
        put_late(psend.at[0])
        for k in range(NC):
            at_ = slice(k * CB, (k + 1) * CB)
            gw1_ref[1, at_, :] = jnp.broadcast_to(gw1_ref[1, at_, 64:65], (CB, 128))
        put_late(psend.at[1])

    def early_copy(d):
        to = lax.rem(me_b + d, NB)
        return send_to(psend.at[:, late_at(to)], pgot.at[me_b], ps, pr, batch_peer(me_b, d))

    def early_start():
        def one(d, carry):
            early_copy(d).start()
            return carry

        lax.fori_loop(1, NB, one, 0)
        pgot[me_b] = psend[:, late_at(me_b), :]

    early_products()
    for i, (who, low, to) in enumerate([(left_i, True, right), (right_i, False, left)]):
        ms_c[i].wait_recv()
        c = send_to(half(who, low), half(who, low), ms.at[4 + i], mr.at[4 + i], to)
        c.start()
        ms_c.append(c)
    for c in ms_c[2:]:
        c.wait_recv()

    def unpack(p, carry):
        g = [got[j, p].astype(F32) for j in range(NC)]
        rl = [pltpu.roll(v, 64, 1) for v in g]
        low = jnp.concatenate(
            [jnp.where(low_half, g[0], rl[1]), jnp.where(low_half, g[2], rl[3])], axis=1
        ).astype(BF16)
        apad[padded(p)] = low
        acol[p] = low
        high = jnp.concatenate(
            [jnp.where(low_half, rl[0], g[1]), jnp.where(low_half, rl[2], g[3])], axis=1
        ).astype(BF16)

        @pl.when(p < POS - HALF)
        def _():
            apad[padded(p + HALF)] = high
            acol[p + HALF] = high

        return carry

    lax.fori_loop(0, HALF, unpack, 0, unroll=5)

    early_start()

    def conv(h, carry):
        s1, s2 = carry
        acc = jnp.zeros((SIDE * ROWS, 384), F32)
        for q in range(9):
            dh, dw = divmod(q, 3)
            lhs = apad[pl.ds((h + dh) * 9 + dw, SIDE)].reshape(SIDE * ROWS, 256)
            acc = acc + dot(lhs, wc_ref[q])
        for w in range(SIDE):
            t = acc[w * ROWS : (w + 1) * ROWS]
            y = t[:, 128:256] + prev_t(t[:, 0:128]) + next_t(t[:, 256:384])
            y2[h * SIDE + w] = y
            m = y * mask
            s1 = s1 + m
            s2 = s2 + m * y
        return s1, s2

    s1, s2 = lax.fori_loop(0, SIDE, conv, (zero128, zero128), unroll=7)
    sbuf_b[me_b] = pack_rows([col(s1), col(s2)], 2)
    share_start(sbuf_b, me_b, bs, br)
    at[...] = jnp.transpose(acol[...].reshape(VOX, 256))
    share_wait(sbuf_b, me_b, bs, br)
    totb = total_of(sbuf_b, NB)
    n2 = norm_of(totb[0:1], totb[1:2], 2)

    def act2(p, carry):
        _, pre, sig = forward(y2[p], n2)
        return carry + mask * (pre * sig)

    feat2 = lax.fori_loop(0, POS, act2, zero128, unroll=7)
    feature = (jnp.concatenate([feat0, feat2], axis=1) / float(POS)).astype(BF16)
    lbuf[me] = dot(feature, r_ref[...])
    ls_c = []
    for d in range(1, NC):
        c = send_to(lbuf.at[me], lbuf.at[me], ls.at[d], lr.at[d], chan_peer(me, d))
        c.start()
        ls_c.append(c)
    for c in ls_c:
        c.wait_recv()
    logits = total_of(lbuf, NC)
    cls = lax.broadcasted_iota(jnp.int32, (ROWS, 512), 1)
    row512 = lax.broadcasted_iota(jnp.int32, (ROWS, 512), 0)
    labs = jnp.zeros((ROWS, 512), jnp.int32)
    for i in range(ROWS):
        labs = jnp.where(row512 == i, lab_ref[i % 4, i // 4], labs)
    real = cls < CLASSES
    logits = jnp.where(real, logits, -1e30)
    peak = jnp.max(logits, axis=1, keepdims=True)
    ex = jnp.exp(logits - peak)
    se = jnp.sum(ex, axis=1, keepdims=True)
    logprob = logits - peak - jnp.log(se)
    mask1 = mask[:, 0:1]
    hit = cls == labs
    loss_rows = -jnp.sum(jnp.where(hit, logprob, 0.0), axis=1, keepdims=True) * mask1
    soft = jnp.where(real, jnp.exp(logprob), 0.0)
    dlog = ((soft - hit.astype(F32)) * mask1 / counted[:, 0:1]).astype(BF16)
    dfeat = dot_t(dlog, r_ref[...], 1, 1) / float(POS)
    df0, df2 = dfeat[:, 0:128], dfeat[:, 128:256]

    def back(y, n, dout):
        normed, pre, sig = forward(y, n)
        return dout * mask * sig * (1.0 + pre * (1.0 - sig)), normed

    def back02(p, carry):
        g0, b0, g2, b2 = carry
        d0, m0 = back(ypos[p][:, 0:128], n0, df0)
        d2, m2 = back(y2[p], n2, df2)
        dpre[p] = jnp.concatenate([d0, d2], axis=1)
        return g0 + d0 * m0, b0 + d0, g2 + d2 * m2, b2 + d2

    g0, b0, g2, b2 = lax.fori_loop(0, POS, back02, (zero128,) * 4, unroll=7)
    loss_row = jnp.broadcast_to(jnp.sum(loss_rows, axis=0, keepdims=True), (1, 128))
    sbuf_c[me_b] = pack_rows([col(g0), col(b0), col(g2), col(b2), loss_row])
    share_start(sbuf_c, me_b, cs, cr)
    grr = dot_t(feature, dlog, 0, 0)
    for t in range(4):
        for dst, src, count in ((0, 0, 96), (96, 224, 32), (128, 96, 96), (224, 192, 32)):
            gr[t, src : src + count, :] = grr[dst : dst + count, 128 * t : 128 * t + 128]
    lane32 = lanes_of((32, 128))
    parts = []
    for j in range(8):
        for t in range(4):
            parts.append(
                (gr[t, pl.ds(j, 32, stride=8), :], 0, CLASSES * j + 128 * t,
                 min(128, CLASSES - 128 * t))
            )
    for i, v in enumerate(joined(parts, lane32, 25)):
        g[pl.ds(BULK["readout"] + i, 32, stride=25), :] = v
    for c in ls_c:
        c.wait_send()
    for c in ms_c:
        c.wait_send()
    share_wait(sbuf_c, me_b, cs, cr)
    totc = total_of(sbuf_c, NB)

    def finish(y, n, d, gg, gb):
        normed = (y - n[0]) * n[2]
        return mask * n[3] * n[2] * (d - gb / voxels - normed * gg / voxels)

    def dy2_at(p, carry):
        d = dpre[p]
        v = finish(y2[p], n2, d[:, 128:256], totc[2:3], totc[3:4])
        dypad[padded(p)] = jnp.concatenate([next_t(v), v, prev_t(v)], axis=1).astype(BF16)
        return carry

    lax.fori_loop(0, POS, dy2_at, 0, unroll=7)

    core_i = lax.rem(me_b, 2)
    mate = digit_peer(me_b, 1, 2, 1)
    along = ((2, 8), (8, 2))
    digits = [[digit_of(me_b, along[i][s], 4) for i in range(2)] for s in range(2)]

    class Chunk:
        def __init__(self, index):
            self.base, self.last = CHUNKS[index]
            self.k = index
            self.first = 4 * self.last
            self.group = 4 * self.first
            self.half = 2 * self.group
            self.own = pl.multiple_of(self.base + core_i * self.half, self.last)
            self.r1 = (r1a, r1b)[index]
            self.r2 = (r2a, r2b)[index]
            self.gc = (gca, gcb)[index]
            self.s1 = ((g1sa, g1ra), (g1sb, g1rb))[index]

        def rows(self, at, count):
            return pl.ds(pl.multiple_of(at, self.last), count)

        def core_start(self):
            theirs = self.rows(self.base + (1 - core_i) * self.half, self.half)
            self.c0 = send_to(g.at[theirs], self.gc, co_s.at[self.k], co_r.at[self.k], mate)
            self.c0.start()

        def one_start(self):
            self.c0.wait()
            n = self.first

            def add(i, carry):
                at_ = self.rows(i * n, n)
                self.gc[at_, :] = self.gc[at_, :] + g[self.rows(self.own + i * n, n), :]
                return carry

            lax.fori_loop(0, self.half // n, add, 0)
            self.c1 = []
            for i in range(2):
                mine = digits[0][i]
                for d in range(1, 4):
                    to = lax.rem(mine + d, 4)
                    c = send_to(
                        self.gc.at[self.rows(i * self.group + to * self.first, self.first)],
                        self.r1.at[i, mine], s1s.at[self.k, i, d], s1r.at[self.k, i, d],
                        digit_peer(me_b, along[i][0], 4, d),
                    )
                    c.start()
                    self.c1.append(c)
                self.r1[i, mine] = self.gc[
                    self.rows(i * self.group + mine * self.first, self.first), :
                ]

        def two_start(self):
            for c in self.c1:
                c.wait()
            self.c2 = []
            for i in range(2):
                mine = digits[1][i]
                self.r1[i, 0] = total_of(self.r1.at[i], 4)
                for d in range(1, 4):
                    to = lax.rem(mine + d, 4)
                    c = send_to(
                        self.r1.at[i, 0, self.rows(to * self.last, self.last)],
                        self.r2.at[i, mine], s2s.at[self.k, i, d], s2r.at[self.k, i, d],
                        digit_peer(me_b, along[i][1], 4, d),
                    )
                    c.start()
                    self.c2.append(c)
                self.r2[i, mine] = self.r1[i, 0, self.rows(mine * self.last, self.last), :]

        def gather_start(self):
            for c in self.c2:
                c.wait()
            for i in range(2):
                mine = self.piece_at(i)
                gb_ref[mine, :] = total_of(self.r2.at[i], 4)

                def one(d, carry, mine=mine):
                    send_to(gb_ref.at[mine], gb_ref.at[mine], *self.s1, chip_peer(d)).start()
                    return carry

                lax.fori_loop(1, 16, one, 0)

        def piece_at(self, i):
            return self.rows(
                self.own + i * self.group + digits[0][i] * self.first + digits[1][i] * self.last,
                self.last,
            )

        def all_others(self):
            some = gb_ref.at[pl.ds(self.base, 30 * self.last)]
            return send_to(some, some, *self.s1, mate)

        def mate_rest(self):
            self.all_others().wait_recv()
            rows_ = self.rows(self.own, self.half)
            self.c5 = send_to(
                gb_ref.at[rows_], gb_ref.at[rows_], g3s.at[self.k], g3r.at[self.k], mate
            )
            self.c5.start()

        def finish(self):
            self.all_others().wait_send()
            self.c5.wait()

    chip = me_b // 2

    def chip_peer(d):
        return {"batch": lax.rem(chip + d, 16) * 2 + core_i}

    class Direct:
        half = 16 * DIRECT_ROWS

        def rows(self, at_, count=DIRECT_ROWS):
            return pl.ds(pl.multiple_of(at_, DIRECT_ROWS), count)

        def core_start(self):
            theirs = self.rows(DIRECT_AT + (1 - core_i) * self.half, self.half)
            self.c0 = send_to(g.at[theirs], gcc, co_s.at[2], co_r.at[2], mate)
            self.c0.start()

        def one_start(self):
            self.c0.wait()
            own = DIRECT_AT + core_i * self.half
            gcc[...] = gcc[...] + g[self.rows(own, self.half), :]

            def one(d, carry):
                to = lax.rem(chip + d, 16)
                send_to(
                    gcc.at[self.rows(to * DIRECT_ROWS)], rc.at[chip], d1s, d1r, chip_peer(d)
                ).start()
                return carry

            lax.fori_loop(1, 16, one, 0)
            rc[chip] = gcc[self.rows(chip * DIRECT_ROWS), :]

        def all_of(self, send, recv):
            some = rc.at[pl.ds(0, 15)]
            return send_to(some, some, send, recv, chip_peer(1))

        def two_start(self):
            self.all_of(d1s, d1r).wait_recv()
            mine = self.rows(DIRECT_AT + core_i * self.half + chip * DIRECT_ROWS)
            gb_ref[mine, :] = total_of(rc, 16)

            def one(d, carry):
                send_to(gb_ref.at[mine], gb_ref.at[mine], d2s, d2r, chip_peer(d)).start()
                return carry

            lax.fori_loop(1, 16, one, 0)

        def mate_rest(self):
            self.all_of(d2s, d2r).wait_recv()
            mine = self.rows(DIRECT_AT + core_i * self.half, self.half)
            self.c3 = send_to(gb_ref.at[mine], gb_ref.at[mine], d3s, d3r, mate)
            self.c3.start()

        def finish(self):
            self.all_of(d1s, d1r).wait_send()
            self.all_of(d2s, d2r).wait_send()
            self.c3.wait()

    a_, b_, c_ = Chunk(0), Chunk(1), Direct()

    def grad_conv(q, carry):
        dh = q // 3
        dw = q - dh * 3
        rhs = jnp.concatenate(
            [
                dypad[pl.ds((h + 2 - dh) * 9 + 2 - dw, SIDE)].reshape(SIDE * ROWS, 384)
                for h in range(SIDE)
            ],
            axis=0,
        )
        res = dot(at[...], rhs)
        for dt in range(3):
            tap = dt * 9 + q
            for j in range(NC):
                gq[48 * j : 48 * j + 48, :] = res[64 * j : 64 * j + 48, 128 * dt : 128 * dt + 128]
                vn[pl.ds(tap * 48 + 12 * j, 12), :] = res[
                    64 * j + 48 : 64 * j + 60, 128 * dt : 128 * dt + 128
                ]

            def put(i, v, base=tap_rows(dt, q)):
                g[pl.ds(base + i, 48, stride=3), :] = v

            flatten_96(lambda j: gq[pl.ds(j, 48, stride=4), :], 48, put)
        return carry

    lax.fori_loop(0, EARLY_TAPS, grad_conv, 0, unroll=2)
    a_.core_start()
    lax.fori_loop(EARLY_TAPS, 9, grad_conv, 0, unroll=5)
    g[BULK["volume"] : BULK["volume"] + 324, :] = flatten_32(
        lambda j: vn[pl.ds(j, 324, stride=4), :], 324
    )

    b_.core_start()
    a_.one_start()

    def conv_back(h, carry):
        acc = jnp.zeros((SIDE * ROWS, 256), F32)
        for q in range(9):
            dh, dw = divmod(q, 3)
            lhs = dypad[pl.ds((h + 2 - dh) * 9 + 2 - dw, SIDE)].reshape(SIDE * ROWS, 384)
            acc = acc + dot(lhs, wct_ref[q])
        for t in range(2):
            ynat[t, pl.ds(pl.multiple_of(h * SIDE * ROWS, SIDE * ROWS), SIDE * ROWS), :] = acc[
                :, 128 * t : 128 * t + 128
            ]
        return carry

    lax.fori_loop(0, 5, conv_back, 0)
    b_.one_start()
    lax.fori_loop(5, SIDE, conv_back, 0)

    def to_dm(p, carry):
        for j in range(NC):
            a = ynat[j // 2, pl.ds(pl.multiple_of(p * ROWS, ROWS), ROWS), :]
            b = ynat[j // 2, pl.ds(pl.multiple_of((p + HALF) * ROWS, ROWS), ROWS), :]
            if j % 2 == 0:
                dm[j, p] = jnp.where(low_half, a, pltpu.roll(b, 64, 1)).astype(BF16)
            else:
                dm[j, p] = jnp.where(low_half, pltpu.roll(a, 64, 1), b).astype(BF16)
        return carry

    for t in range(2):
        ynat[t, pl.ds(VOX, ROWS), :] = zero128
    lax.fori_loop(0, HALF, to_dm, 0, unroll=5)
    lo_, hi_ = pl.ds(0, near), pl.ds(near, HALF - near)

    def far_copy(i):
        rows_, to = ((lo_, right), (hi_, left))[i]
        return send_to(dm.at[far_i, rows_], dgot.at[2, rows_], ds_.at[i], dr.at[i], to)

    def near_copy(i):
        who, rows_, to, slot = (
            (right_i, hi_, right, 0), (left_i, lo_, left, 1), (right_i, lo_, right, 0),
            (left_i, hi_, left, 1),
        )[i]
        return send_to(
            dm.at[who, rows_], dgot.at[slot, rows_], ds_.at[2 + i], dr.at[2 + i], to
        )

    far_c = [far_copy(i) for i in range(2)]
    near_c = [near_copy(i) for i in range(4)]
    for c in far_c + near_c[0:2]:
        c.start()

    a_.two_start()

    def dy0_at(p, carry):
        v = finish(ypos[p][:, 0:128], n0, dpre[p][:, 0:128], totc[0:1], totc[1:2])
        v = v.astype(BF16).astype(F32)
        h, w = p // SIDE, lax.rem(p, SIDE)
        n_h = 3 - (h == 0).astype(jnp.int32) - (h == SIDE - 1).astype(jnp.int32)
        n_w = 3 - (w == 0).astype(jnp.int32) - (w == SIDE - 1).astype(jnp.int32)
        share = v / jnp.maximum(n_t * (n_h * n_w).astype(F32), 1.0)
        box[padded(p)] = share + prev_t(share) + next_t(share)
        ypos[p, :, 0:128] = v
        return carry

    lax.fori_loop(0, POS, dy0_at, 0, unroll=7)

    def dy0_nat(p, carry):
        acc, _ = spread(p)
        v = jnp.where(is_pool, acc * mask, ypos[p][:, 0:128])
        lowv = v - v.astype(BF16).astype(F32)
        dnat[0, pl.ds(p, ROWS, stride=POS), :] = v
        dnat[1, pl.ds(p, ROWS, stride=POS), :] = lowv
        return carry

    lax.fori_loop(0, POS, dy0_nat, 0, unroll=7)

    for c in far_c:
        c.wait_recv()

    def add_far(p, carry):
        who = jnp.where(p < near, right_i, left_i)
        dm[who, p] = (dm[who, p].astype(F32) + dgot[2, p].astype(F32)).astype(dm.dtype)
        return carry

    lax.fori_loop(0, HALF, add_far, 0, unroll=5)
    for c in near_c[2:4]:
        c.start()
    for at_, v in products(256):
        gw1_ref[0, at_, :] = v[:, 0:128] + v[:, 128:256]

    def put_direct(i, v):
        g[pl.ds(BULK["direct"] + i, 208, stride=3), :] = v

    flatten_96(lambda j: gw1_ref[0, pl.ds(j, 208, stride=4), :], 208, put_direct)
    g[BULK["pooled"] : BULK["pooled"] + 208, :] = flatten_32(
        lambda j: gw1_ref[0, pl.ds(j, 208, stride=4), :], 208
    )

    c_.core_start()
    a_.gather_start()
    b_.two_start()

    for c in near_c:
        c.wait_recv()


    def back1(p, carry):
        g1, b1 = carry
        s = dm[me, p].astype(F32) + dgot[0, p].astype(F32) + dgot[1, p].astype(F32)
        d, m = back(ypos[p][:, 128:256], n1, jnp.where(low_half, s, 0.0))
        ob[p] = d
        g1, b1 = g1 + d * m, b1 + d
        q = jnp.minimum(p + HALF, POS - 1)
        live = (p < POS - HALF).astype(F32)
        d, m = back(ypos[q][:, 128:256], n1, jnp.where(low_half, pltpu.roll(s, 64, 1), 0.0) * live)

        @pl.when(p < POS - HALF)
        def _():
            ob[p + HALF] = d

        return g1 + d * m, b1 + d

    g1, b1 = lax.fori_loop(0, HALF, back1, (zero128, zero128), unroll=5)
    sbuf_d[me_b] = pack_rows([col(g1), col(b1)], 2)
    share_start(sbuf_d, me_b, es, er)
    c_.one_start()

    def dy1_nat(p, carry):
        d = ob[p]
        top = d.astype(BF16).astype(F32)
        dnat[0, pl.ds(p, ROWS, stride=POS), :] = top + pltpu.roll(d - top, 64, 1)
        return carry

    lax.fori_loop(0, POS, dy1_nat, 0, unroll=7)
    for at_, v in products(128):
        gw1_ref[1, at_, :] = v + pltpu.roll(v, 64, 1)
    lsend[pl.ds(384, 128), :] = jnp.zeros((128, 128), F32)
    put_late(lsend)

    def late_copy(d):
        to = lax.rem(me_b + d, NB)
        return send_to(lsend.at[late_at(to)], lgot.at[me_b], fs, fr, batch_peer(me_b, d))

    def late_start(d, carry):
        late_copy(d).start()
        return carry

    lax.fori_loop(1, NB, late_start, 0)
    lgot[me_b] = lsend[late_at(me_b), :]
    for c in far_c + near_c:
        c.wait_send()
    b_.gather_start()
    share_wait(sbuf_d, me_b, es, er)
    totd = total_of(sbuf_d, NB)

    rowl = lax.broadcasted_iota(jnp.int32, (LATE_ROWS, 128), 0) + me_b * LATE_ROWS
    third = lax.rem(rowl, 3)

    def late_lanes(v):
        lane1 = lanes_of((1, 128))
        sq = joined([(v, 0, 48 * j, 48) for j in range(8)], lane1, 3)
        sh = joined([(v, 48, 12 * j, 12) for j in range(32)], lane1, 3)
        pick = [jnp.where(rowl < LATE["shrink"], a, b) for a, b in zip(sq, sh)]
        return jnp.where(third == 0, pick[0], jnp.where(third == 1, pick[1], pick[2]))

    scale_l = late_lanes(n1[3] * n1[2])
    bias_l = late_lanes(totd[1:2] / voxels)
    gain_l = late_lanes(totd[0:1] / voxels)
    share_wait(pgot, me_b, ps, pr)
    c_.two_start()
    share_wait(lgot, me_b, fs, fr)
    both = total_of(pgot, NB)
    late_ref[me_b] = scale_l * (total_of(lgot, NB) - bias_l * both[1] - gain_l * both[0])
    share_start(late_ref, me_b, hs, hr)
    a_.mate_rest()
    b_.mate_rest()

    fix = voxels / (voxels - 1.0)
    for tile, n, gg, gb in (
        (0, n0, totc[0:1], totc[1:2]),
        (1, n1, totd[0:1], totd[1:2]),
        (2, n2, totc[2:3], totc[3:4]),
    ):
        st_ref[:, 128 * tile : 128 * tile + 128] = pack_rows([gg, gb, n[0], n[1] * fix])
    sc_ref[...] = pack_rows([totc[4:5], counted])

    for buf, send, recv in (
        (sbuf_a, as_, ar), (sbuf_b, bs, br), (sbuf_c, cs, cr), (sbuf_d, es, er), (lgot, fs, fr),
        (pgot, ps, pr),
    ):
        share_sent(buf, me_b, send, recv)
    c_.mate_rest()
    share_wait(late_ref, me_b, hs, hr)
    share_sent(late_ref, me_b, hs, hr)
    for chunk in (a_, b_, c_):
        chunk.finish()


def core(x, lengths, labels, weights, affine):
    vm = pl.BlockSpec(memory_space=pltpu.VMEM)
    sm = pl.BlockSpec(memory_space=pltpu.SMEM)
    hbm = pl.BlockSpec(memory_space=pltpu.HBM)
    dma = pltpu.SemaphoreType.DMA
    vmem = pltpu.VMEM
    return pl.pallas_call(
        core_kernel,
        out_shape=(
            pltpu.VMEM((BULK_ROWS, 128), F32),
            jax.ShapeDtypeStruct((NB, LATE_ROWS, 128), F32),
            jax.ShapeDtypeStruct((8, 384), F32),
            jax.ShapeDtypeStruct((8, 128), F32),
        ),
        in_specs=[hbm, sm, sm] + [hbm] * 7 + [vm],
        out_specs=(vm,) * 4,
        scratch_shapes=[
            vmem((1, 326144), BF16),
            *[vmem((1, FLAT[n] * 128), F32) for n in NARROW],
            vmem((2, CIN, 128), F32),
            vmem((CIN, 128), F32),
            vmem((R1, 128), F32),
            vmem((1304, 128), F32),
            vmem((4, 256, 128), F32),
            vmem((9, 256, 384), BF16),
            vmem((9, 384, 256), BF16),
            vmem((256, 512), BF16),
            vmem((8, 384), F32),
            vmem((13 * GPAD, 128), F32),
            vmem((NC, GPAD, GW), BF16),
            vmem((NC, GW, 256), BF16),
            vmem((8, 256, 256), BF16),
            vmem((NC, W1_ROWS, 256), BF16),
            vmem((2, 8 * GPAD, 128), F32),
            vmem((POS, ROWS, 256), F32),
            vmem((81, ROWS, 128), F32),
            vmem((POS + 1, ROWS, 128), F32),
            vmem((NC, HALF, ROWS, 128), BF16),
            vmem((81, ROWS, 256), BF16),
            vmem((POS, ROWS, 256), BF16),
            vmem((256, VOX), BF16),
            vmem((POS, ROWS, 128), F32),
            vmem((POS, ROWS, 256), F32),
            vmem((81, ROWS, 384), BF16),
            vmem((NC, HALF, ROWS, 128), BF16),
            vmem((3, HALF, ROWS, 128), BF16),
            vmem((2, 8 * GPAD, 128), F32),
            vmem((2, CIN, 128), F32),
            vmem((R1, 128), F32),
            vmem((4, 256, 128), F32),
            vmem((BULK_ROWS, 128), F32),
            *[vmem((32 * n, 128), F32) for _, n in CHUNKS],
            vmem((16 * DIRECT_ROWS, 128), F32),
            *[vmem((2, 4, 4 * n, 128), F32) for _, n in CHUNKS],
            *[vmem((2, 4, n, 128), F32) for _, n in CHUNKS],
            vmem((16, DIRECT_ROWS, 128), F32),
            vmem((NB * LATE_ROWS, 128), F32),
            vmem((NB, LATE_ROWS, 128), F32),
            vmem((2, NB * LATE_ROWS, 128), F32),
            vmem((NB, 2, LATE_ROWS, 128), F32),
            vmem((NC, ROWS, 512), F32),
            *[vmem((NB, n, 128), F32) for n in (8, 2, 8, 2)],
            dma((4,)), dma((7,)), dma((12,)), dma((12,)),
            dma((6,)), dma((6,)), dma((NC,)), dma((NC,)), dma((6,)), dma((6,)),
            *[dma] * 12,
            dma((3,)), dma((3,)),
            *[dma((2, 2, 4))] * 4,
            *[dma] * 4,
            dma((2,)), dma((2,)),
            *[dma] * 8,
        ],
        compiler_params=pltpu.CompilerParams(
            collective_id=0, has_side_effects=True, vmem_limit_bytes=47 << 20
        ),
        name="block",
    )(x, lengths, labels, *weights, affine)


def unlanes(tiles):
    t0, t1, t2 = tiles
    lane = lanes_of(t0.shape)
    parts = [(t0, 0, 0, 96), (t1, 0, 96, 60), (t0, 96, 156, 32), (t2, 0, 188, 128)]
    return joined(parts, lane, 3)


def adam_kernel(*refs):
    gb, late, st, sc, running = refs[0:5]
    w_in, m_in, v_in = refs[5:13], refs[13:21], refs[21:29]
    m_out, v_out, w_out = refs[29:37], refs[37:45], refs[45:53]
    run_out, loss_out, count_out, copies_out = refs[53:57]
    wb, mb, vb = refs[57:64], refs[64:71], refs[71:78]
    cb, insem, outsem, csem = refs[78:82]
    rates = step_rates()
    parts = []
    for i in ADAM_ORDER:
        parts.append((i, 0, FLAT[NAMES[i]]))
    for first in range(0, FLAT["spatial"], ADAM_ROWS):
        parts.append((2, first, ADAM_ROWS))

    def at_rows(ref, i, first, count):
        if NAMES[i] in NARROW:
            return ref.at[:, pl.ds(first * 128, count * 128)]
        return ref.at[pl.ds(first, count)]

    ins = []
    for n, (i, first, count) in enumerate(parts):
        mine = []
        for kind, (src, dst) in enumerate(((w_in[i], wb[i]), (m_in[i], mb[i]), (v_in[i], vb[i]))):
            if NAMES[i] == "spatial" and kind < 2:
                continue
            c = pltpu.make_async_copy(
                at_rows(src, i, first, count), at_rows(dst, i, first, count), insem.at[n, kind]
            )
            c.start()
            mine.append(c)
        ins.append(mine)

    starts = []
    total = 0
    for name in NAMES:
        starts.append(total * 128)
        total += FLAT[name]
    outs = []
    for n, (i, first, rows) in enumerate(parts):
        name = NAMES[i]
        for c in ins[n]:
            c.wait()

        def step(at, count, i=i, name=name, first=first):
            if name == "spatial":
                tap = at // 144
                row = tap_rows(tap // 9, lax.rem(tap, 9)) + lax.rem(at, 144)
                grad = gb[pl.ds(pl.multiple_of(row, 8), count), :]
            elif name in BULK:
                grad = gb[pl.ds(BULK[name] + at, count), :]
            else:
                grad = late[pl.ds(LATE[name] + at, count), :]
            wide = pl.ds(pl.multiple_of(at * 128, 128), count * 128)
            narrow = name in NARROW

            def load(ref):
                if narrow:
                    return ref[:, wide].reshape(count, 128)
                return ref[pl.ds(at, count), :]

            def store(ref, v):
                if narrow:
                    ref[:, wide] = v.reshape(1, count * 128)
                else:
                    ref[pl.ds(at, count), :] = v

            old = (w_in, m_in, vb) if name == "spatial" else (wb, mb, vb)
            m, v, w = adamw(*(load(group[i]) for group in old), grad, rates[i])
            store(mb[i], m)
            store(vb[i], v)
            store(wb[i], w)
            cb[:, pl.ds(pl.multiple_of(starts[i] + at * 128, 128), count * 128)] = w.astype(
                BF16
            ).reshape(1, count * 128)

        block = {"spatial": 72, "readout": 80, "direct": 48, "pooled": 104, "squeeze": 104}.get(
            name, 24
        )
        loops = rows // block

        def body(j, carry, step=step, block=block, first=first):
            step(pl.multiple_of(first + j * block, 8), block)
            return carry

        lax.fori_loop(0, loops, body, 0, unroll=3)
        at, rest = first + loops * block, rows - loops * block
        if rest // 8:
            step(at, rest // 8 * 8)
        if rest % 8:
            step(at + rest // 8 * 8, rest % 8)
        for kind, (src, dst) in enumerate(((wb[i], w_out[i]), (mb[i], m_out[i]), (vb[i], v_out[i]))):
            c = pltpu.make_async_copy(
                at_rows(src, i, first, rows), at_rows(dst, i, first, rows), outsem.at[n, kind]
            )
            c.start()
            outs.append(c)
        at = pl.ds(starts[i] + first * 128, rows * 128)
        c = pltpu.make_async_copy(cb.at[:, at], copies_out.at[:, at], csem.at[n])
        c.start()
        outs.append(c)

    tiles = [st[:, 128 * t : 128 * t + 128] for t in range(3)]
    for t, v in enumerate(unlanes(tiles)):
        width = min(128, 316 - 128 * t)
        at = slice(128 * t, 128 * t + width)
        v = v[:, 0:width]
        m, s, w = adamw(w_in[7][:, at], m_in[7][:, at], v_in[7][:, at], v[0:2], rates[7])
        m_out[7][:, at] = m
        v_out[7][:, at] = s
        w_out[7][:, at] = w
        run_out[:, at] = MOMENTUM * running[:, at] + (1.0 - MOMENTUM) * v[2:4]
    loss_out[...] = sc[0:1, 0:1]
    count_out[...] = sc[1:2, 0:1]
    for c in outs:
        c.wait()


def adam(gb, late, st, sc, running, masters, firsts, seconds):
    vm = pl.BlockSpec(memory_space=pltpu.VMEM)
    hbm = pl.BlockSpec(memory_space=pltpu.HBM)
    dma = pltpu.SemaphoreType.DMA
    shapes = [(1, FLAT[n] * 128) if n in NARROW else (FLAT[n], 128) for n in NAMES]
    flats = [jax.ShapeDtypeStruct(shape, F32) for shape in shapes]
    small = jax.ShapeDtypeStruct((2, 316), F32)
    total = sum(FLAT[n] for n in NAMES) * 128
    one = jax.ShapeDtypeStruct((1, 1), F32)
    specs = [hbm] * 7 + [vm]
    buffers = [pltpu.VMEM(shape, F32) for shape in shapes]
    count = 6 + FLAT["spatial"] // ADAM_ROWS
    return pl.pallas_call(
        adam_kernel,
        out_shape=[*(flats + [small]) * 3, small, one, one, jax.ShapeDtypeStruct((1, total), BF16)],
        in_specs=[vm] * 5 + ([hbm] * 2 + [vm] + [hbm] * 4 + [vm]) * 2 + specs,
        out_specs=[*specs * 3, vm, vm, vm, hbm],
        scratch_shapes=[
            *buffers * 3, pltpu.VMEM((1, total), BF16), dma((count, 3)), dma((count, 3)), dma((count,)),
        ],
        compiler_params=pltpu.CompilerParams(vmem_limit_bytes=20 << 20),
        name="adamw",
    )(gb, late, st, sc, running, *masters, *firsts, *seconds)


def per_device(
    features, lengths, labels, direct, squeeze, spatial, shrink, volume, pooled, readout, affine,
    first_direct, first_squeeze, first_spatial, first_shrink, first_volume, first_pooled,
    first_readout, first_affine, second_direct, second_squeeze, second_spatial, second_shrink,
    second_volume, second_pooled, second_readout, second_affine, running,
):
    masters = [direct, squeeze, spatial, shrink, volume, pooled, readout, affine]
    firsts = [
        first_direct, first_squeeze, first_spatial, first_shrink, first_volume, first_pooled,
        first_readout, first_affine,
    ]
    seconds = [
        second_direct, second_squeeze, second_spatial, second_shrink, second_volume,
        second_pooled, second_readout, second_affine,
    ]
    def rows(flat, name):
        return flat if name in NARROW else flat.reshape(-1, 128)

    masters, firsts, seconds = (
        [rows(a, n) for a, n in zip(group, NAMES)] + [group[7]]
        for group in (masters, firsts, seconds)
    )
    def put(arrays, space):
        return [pltpu.with_memory_space_constraint(a, space) for a in arrays]

    x, lens, labs, aff = put([features, lengths, labels.T, affine], pltpu.HBM)
    gb, late, st, sc = core(x, lens, labs, put(masters[:7], pltpu.HBM), aff)
    (gb,) = put([gb], pltpu.VMEM)
    masters, firsts, seconds = (
        put(group[:2], pltpu.HBM) + put(group[2:3], space) + put(group[3:7], pltpu.HBM)
        + [group[7]]
        for group, space in ((masters, pltpu.VMEM), (firsts, pltpu.VMEM), (seconds, pltpu.HBM))
    )
    out = adam(gb, late.reshape(NB * LATE_ROWS, 128), st, sc, running, masters, firsts, seconds)
    flat_out = [a if i % 8 == 7 else a.reshape(1, -1) for i, a in enumerate(out[:24])]
    return (*flat_out, out[24], out[25].reshape(()), out[26].reshape(()), out[27])


def solution(mesh):
    flat = P("chan", None)
    wide = P(None, "chan")
    weights = (flat,) * 7 + (wide,)
    return jax.shard_map(
        per_device,
        mesh=mesh,
        in_specs=(P("chan", "batch"), P("batch"), P("batch", None)) + weights * 3 + (wide,),
        out_specs=weights * 3 + (wide, P(), P(), flat),
        check_vma=False,
    )
```
